32 devices in a mesh: ens: 2 (over x), mode: 16 (over z, y, core).
Axes of the slice: x: 2, y: 2, z: 4, core: 2. Of those that a mesh axis runs over, the one named last changes fastest.
Arguments:
- velocity: float32 [6, 512, 2048], P('ens', 'mode'), parts along dimension 0, may hold values from -4 to 4
- log_conf: float32 [12, 512, 2048], P('ens', 'mode'), parts along dimension 0, may hold values from -3 to 3
- orientation: int32 [32], replicated, may hold values from 0 to 7
- wall_speed: float32 [2], P('ens'), parts along dimension 0, may hold values from 0.5 to 2
Outputs:
- vel_next: float32 [6, 512, 2048], P('ens', 'mode'), parts along dimension 0
- logc_next: float32 [12, 512, 2048], P('ens', 'mode'), parts along dimension 0
The draws below stay inside these ranges and needn't reach their ends.
There are 2 independent parts, one for each index of `ens`. The reference program is written for one: setup_inputs(seed, part) draws one part's arguments, and reference() takes and returns one part's arrays. A program takes and returns all parts, laid end to end along the dimension named above; an argument that names none is the same for every part. Nothing has to cross between parts.
Inputs may be any that keep to these rules, and one draw needn't show every extreme that they name: orientation[e] is the storage code of element e as in the reference program; elements take the eight codes independently.
All inputs are finite; a program needn't handle non-finite values.
Results may differ from the reference program's by a relative error of at most 0.0003.
Values sent between devices are 32-bit elements; how exact they have to be, the bound alone decides.
No kernel may reach another device: no remote copies, remote signals or barrier semaphores. Data moves between devices by JAX's collectives and lax.ppermute only.
A program may use at most 512 MiB of HBM per device.

```python
import jax
import jax.numpy as jnp
import numpy as np
from jax import lax

NODE_1D = 8
CYCLES = 2
LAYERS_DEV = 1
MODES = 512
ELEMS = 32
NODES = 2048
N_MODE = 16


def touch_ends(entries, own_key, smallest, high):
    shape = entries.shape
    place = [jax.random.randint(jax.random.fold_in(own_key, axis), (), 0, shape[axis]) for axis in range(len(shape))]
    entries = entries.at[tuple(place)].set(smallest)
    longest = shape.index(max(shape))
    place[longest] = (place[longest] + 1) % shape[longest]
    return entries.at[tuple(place)].set(high)


def shard_levels(own_key, dims, shards, smallest, top_value):
    factor_of = 1.0
    for dim, blocks in shards:
        draws = jax.random.uniform(jax.random.fold_in(jax.random.fold_in(own_key, 6), dim), (blocks,), jnp.float32, smallest / len(shards), top_value / len(shards))
        factor_of = factor_of * jnp.repeat(jnp.exp(draws), dims[dim] // blocks).reshape((-1,) + (1,) * (len(dims) - 1 - dim))
    return factor_of


def scatter_about(own_key, extent, scale, most, shards=(), kind=jnp.bfloat16):
    level = shard_levels(own_key, extent, shards, -0.22, 0.18) if shards else 1.0
    entries = jax.random.normal(own_key, extent, jnp.float32) * scale * level
    return jnp.minimum(jnp.maximum(entries, -most), most).astype(kind)


def setup_inputs(seed: int = 0, part: int = 0) -> dict:
    streams_of = jax.random.split(jax.random.key(seed), 5)
    own_keys = jax.random.split(jax.random.fold_in(streams_of[4], part), 5)
    return {
        "velocity": scatter_about(own_keys[0], (3, MODES, NODES), 0.6, 4.0, ((1, 16),), jnp.float32),
        "log_conf": scatter_about(own_keys[1], (6, MODES, NODES), 0.4, 3.0, ((1, 16),), jnp.float32),
        "orientation": touch_ends(jax.random.randint(streams_of[2], (ELEMS,), 0, 8), jax.random.fold_in(streams_of[2], 1), 0, 7).astype(jnp.int32),
        "wall_speed": jnp.clip(jax.random.uniform(own_keys[3], (1,), jnp.float32, 0.5, 2.0), 0.5, 2.0),
    }


STEP_DT = 0.002
RELAX_TIME = 0.02
MOBILITY = 0.3
LAYER_HEIGHT = 0.25
R_INNER = 1.0
HIGHEST = lax.Precision.HIGHEST
PAIRS = ((0, 0), (0, 1), (0, 2), (1, 1), (1, 2), (2, 2))

def cheb_table(points):
    nodes_xi = -np.cos(np.pi * np.arange(points) / (points - 1))
    weights = np.ones(points)
    weights[0] = 2.0
    weights[-1] = 2.0
    weights = weights * (-1.0) ** np.arange(points)
    identity = np.eye(points)
    spacing = nodes_xi[:, None] - nodes_xi[None, :] + identity
    matrix = weights[:, None] / weights[None, :] / spacing
    matrix = matrix * (1.0 - identity)
    matrix = matrix - identity * matrix.sum(axis=1)[:, None]
    return (nodes_xi, matrix)

def cycle_radius(cycle_count, side_pts):
    nodes_xi, matrix = cheb_table(side_pts)
    radius = R_INNER + (np.arange(cycle_count)[:, None] + (nodes_xi[None, :] + 1.0) / 2.0) / cycle_count
    return (jnp.asarray(radius.reshape(-1, 1), dtype=jnp.float32), matrix)

def fourier_basis(planes):
    plane_ids = jnp.arange(planes, dtype=jnp.int32)
    pair_ids = jnp.arange(planes // 2, dtype=jnp.int32)
    phase_ids = plane_ids[:, None] * pair_ids[None, :] % planes
    angles = phase_ids.astype(jnp.float32) * (2.0 * np.pi / planes)
    norm_scale = np.sqrt(2.0 / planes)
    cosine = jnp.cos(angles) * norm_scale
    sine_part = jnp.sin(angles) * norm_scale
    mean_col = jnp.full((planes,), 1.0 / np.sqrt(planes), jnp.float32)
    nyquist = jnp.where(plane_ids % 2 == 0, 1.0, -1.0).astype(jnp.float32) / np.sqrt(planes)
    cosine = cosine.at[:, 0].set(mean_col)
    sine_part = sine_part.at[:, 0].set(nyquist)
    return jnp.stack([cosine, sine_part], axis=2).reshape(planes, planes)

def theta_deriv(coeffs, coef_axis, pair_start):
    shape_in = coeffs.shape
    blocked = coeffs.reshape(shape_in[:coef_axis] + (shape_in[coef_axis] // 2, 2) + shape_in[coef_axis + 1:])
    cos_part = lax.index_in_dim(blocked, 0, coef_axis + 1, keepdims=False)
    sin_part = lax.index_in_dim(blocked, 1, coef_axis + 1, keepdims=False)
    wavenums = (pair_start + jnp.arange(shape_in[coef_axis] // 2, dtype=jnp.int32)).astype(jnp.float32)
    wavenums = wavenums.reshape((-1,) + (1,) * (len(shape_in) - coef_axis - 1))
    return jnp.stack([wavenums * sin_part, -wavenums * cos_part], axis=coef_axis + 1).reshape(shape_in)

def grid_to_stored(orient_block, layers, cycle_count, side_pts):
    layer_ids = jnp.arange(layers, dtype=jnp.int32)[:, None, None, None]
    row_ids = jnp.arange(side_pts, dtype=jnp.int32)[None, :, None, None]
    cycle_ids = jnp.arange(cycle_count, dtype=jnp.int32)[None, None, :, None]
    col_ids = jnp.arange(side_pts, dtype=jnp.int32)[None, None, None, :]
    element = layer_ids * cycle_count + cycle_ids
    orient = orient_block.reshape(layers, cycle_count)[:, None, :, None]
    swapped = orient // 4 % 2 == 1
    leading = jnp.where(swapped, col_ids, row_ids)
    trailing = jnp.where(swapped, row_ids, col_ids)
    leading = jnp.where(orient % 2 == 1, side_pts - 1 - leading, leading)
    trailing = jnp.where(orient // 2 % 2 == 1, side_pts - 1 - trailing, trailing)
    return (element * side_pts * side_pts + leading * side_pts + trailing).reshape(-1)

def stored_coords(orient_block, layers, cycle_count, side_pts):
    layer_ids = jnp.arange(layers, dtype=jnp.int32)[:, None, None, None]
    cycle_ids = jnp.arange(cycle_count, dtype=jnp.int32)[None, :, None, None]
    lead_ids = jnp.arange(side_pts, dtype=jnp.int32)[None, None, :, None]
    trail_ids = jnp.arange(side_pts, dtype=jnp.int32)[None, None, None, :]
    orient = orient_block.reshape(layers, cycle_count)[:, :, None, None]
    lead_ids = jnp.where(orient % 2 == 1, side_pts - 1 - lead_ids, lead_ids)
    trail_ids = jnp.where(orient // 2 % 2 == 1, side_pts - 1 - trail_ids, trail_ids)
    swapped = orient // 4 % 2 == 1
    row_ids = jnp.where(swapped, trail_ids, lead_ids)
    col_ids = jnp.where(swapped, lead_ids, trail_ids)
    position = (layer_ids * side_pts + row_ids) * (cycle_count * side_pts) + cycle_ids * side_pts + col_ids
    inner_wall = jnp.logical_and(cycle_ids == 0, col_ids == 0)
    outer_wall = jnp.logical_and(cycle_ids == cycle_count - 1, col_ids == side_pts - 1)
    full_shape = position.shape
    return (position.reshape(-1), jnp.broadcast_to(inner_wall, full_shape).reshape(-1), jnp.broadcast_to(outer_wall, full_shape).reshape(-1))

def point_sum(blocked, deriv_mat, axis_at, factor):
    axis_pos = axis_at % blocked.ndim
    count = blocked.shape[axis_pos]
    pieces = [lax.index_in_dim(blocked, point, axis_pos, keepdims=False) for point in range(count)]
    rows_out = []
    for target in range(count):
        total = pieces[0] * float(deriv_mat[target][0] * factor)
        for point in range(1, count):
            total = total + pieces[point] * float(deriv_mat[target][point] * factor)
        rows_out.append(total)
    return jnp.stack(rows_out, axis=axis_pos)

def radial_deriv(values, deriv_mat, cycle_count, side_pts):
    shape_in = values.shape
    blocked = values.reshape(shape_in[:-2] + (cycle_count, side_pts, shape_in[-1]))
    return point_sum(blocked, deriv_mat, -2, 2.0 * cycle_count).reshape(shape_in)

def axial_deriv(values, deriv_mat, side_pts):
    shape_in = values.shape
    blocked = values.reshape(shape_in[:-3] + (shape_in[-3] // side_pts, side_pts) + shape_in[-2:])
    return point_sum(blocked, deriv_mat, -3, 2.0 / LAYER_HEIGHT).reshape(shape_in)

def radial_average(values, cycle_count, side_pts):
    shape_in = values.shape
    blocked = values.reshape(shape_in[:-2] + (cycle_count, side_pts, shape_in[-1]))
    left_face = blocked[..., :, 0, :]
    right_face = blocked[..., :, side_pts - 1, :]
    face_mean = 0.5 * (right_face[..., :-1, :] + left_face[..., 1:, :])
    left_face = jnp.concatenate([left_face[..., :1, :], face_mean], axis=-2)
    right_face = jnp.concatenate([face_mean, right_face[..., -1:, :]], axis=-2)
    joined = jnp.concatenate([left_face[..., None, :], blocked[..., 1:side_pts - 1, :], right_face[..., None, :]], axis=-2)
    return joined.reshape(shape_in)

def axial_average(values, below_row, above_row, side_pts):
    shape_in = values.shape
    blocked = values.reshape(shape_in[:-3] + (shape_in[-3] // side_pts, side_pts) + shape_in[-2:])
    bottom = blocked[..., :, 0, :, :]
    top_face = blocked[..., :, side_pts - 1, :, :]
    next_bottom = jnp.concatenate([bottom[..., 1:, :, :], above_row[..., None, :, :]], axis=-3)
    prev_top = jnp.concatenate([below_row[..., None, :, :], top_face[..., :-1, :, :]], axis=-3)
    bottom = 0.5 * (bottom + prev_top)
    top_face = 0.5 * (top_face + next_bottom)
    joined = jnp.concatenate([bottom[..., :, None, :, :], blocked[..., :, 1:side_pts - 1, :, :], top_face[..., :, None, :, :]], axis=-3)
    return joined.reshape(shape_in)

def sym_full(components):
    return [[components[0], components[1], components[2]], [components[1], components[3], components[4]], [components[2], components[4], components[5]]]

def mat_prod(first_mat, second_mat):
    return [[first_mat[row_at][0] * second_mat[0][col_at] + first_mat[row_at][1] * second_mat[1][col_at] + first_mat[row_at][2] * second_mat[2][col_at] for col_at in range(3)] for row_at in range(3)]

def add_diag(matrix, offset):
    return [[matrix[row_at][col_at] + offset if row_at == col_at else matrix[row_at][col_at] for col_at in range(3)] for row_at in range(3)]

def mat_scale(matrix, factor):
    return [[matrix[row_at][col_at] * factor for col_at in range(3)] for row_at in range(3)]

def mat_exp(components):
    scaled = sym_full([member * 0.125 for member in components])
    series = add_diag(mat_scale(scaled, 0.25), 1.0)
    for degree in (3.0, 2.0):
        series = add_diag(mat_scale(mat_prod(scaled, series), 1.0 / degree), 1.0)
    series = add_diag(mat_prod(scaled, series), 1.0)
    for repeat in range(3):
        series = mat_prod(series, series)
    return series

def velocity_grad(velocity, velocity_dth, radius, deriv_mat, cycle_count, side_pts):
    inv_r = 1.0 / radius
    d_radial = radial_deriv(velocity, deriv_mat, cycle_count, side_pts)
    d_axial = axial_deriv(velocity, deriv_mat, side_pts)
    angular = velocity_dth * inv_r
    components = [d_radial[0], angular[0] - velocity[1] * inv_r, d_axial[0], d_radial[1], angular[1] + velocity[0] * inv_r, d_axial[1], d_radial[2], angular[2], d_axial[2]]
    return jnp.stack(components, axis=0)

def tendencies(velocity, logconf, logconf_dth, grad_proj, radius, deriv_mat, cycle_count, side_pts):
    inv_r = 1.0 / radius
    grad_mat = [[grad_proj[3 * row_at + col_at] for col_at in range(3)] for row_at in range(3)]
    members = [logconf[member] for member in range(6)]
    logc_mat = sym_full(members)
    conform = mat_exp(members)
    inverse = mat_exp([-member for member in members])
    d_radial = radial_deriv(logconf, deriv_mat, cycle_count, side_pts)
    d_axial = axial_deriv(logconf, deriv_mat, side_pts)
    hoop_rate = velocity[1] * inv_r
    curvature = [-2.0 * members[1], members[0] - members[3], -members[4], 2.0 * members[1], members[2]]
    spin_mat = [[0.5 * (grad_mat[row_at][col_at] - grad_mat[col_at][row_at]) for col_at in range(3)] for row_at in range(3)]
    rotate_a = mat_prod(spin_mat, logc_mat)
    rotate_b = mat_prod(logc_mat, spin_mat)
    new_logc = []
    stress = []
    for member, (row_at, col_at) in enumerate(PAIRS):
        unit_diag = 1.0 if row_at == col_at else 0.0
        advect = velocity[0] * d_radial[member] + hoop_rate * logconf_dth[member] + velocity[2] * d_axial[member]
        relaxing = -(1.0 / RELAX_TIME) * (unit_diag - inverse[row_at][col_at] + MOBILITY * (conform[row_at][col_at] - 2.0 * unit_diag + inverse[row_at][col_at]))
        tendency = -advect + (rotate_a[row_at][col_at] - rotate_b[row_at][col_at]) + (grad_mat[row_at][col_at] + grad_mat[col_at][row_at]) + relaxing
        if member < 5:
            tendency = tendency - hoop_rate * curvature[member]
        new_logc.append(tendency)
        stress.append(conform[row_at][col_at] - unit_diag)
    stress_arr = jnp.stack(stress, axis=0)
    stress_dr = radial_deriv(stress_arr, deriv_mat, cycle_count, side_pts)
    stress_dz = axial_deriv(stress_arr, deriv_mat, side_pts)
    convect = [grad_mat[row_at][0] * velocity[0] + grad_mat[row_at][1] * velocity[1] + grad_mat[row_at][2] * velocity[2] for row_at in range(3)]
    mom_r = -convect[0] + stress_dr[0] + stress_dz[2] + (stress[0] - stress[3]) * inv_r
    mom_t = -convect[1] + stress_dr[1] + stress_dz[4] + 2.0 * stress[1] * inv_r
    mom_z = -convect[2] + stress_dr[2] + stress_dz[5] + stress[2] * inv_r
    hoop_terms = [stress[1] * inv_r, stress[3] * inv_r, stress[4] * inv_r]
    return jnp.stack([mom_r, mom_t, mom_z] + new_logc + hoop_terms, axis=0)

def to_planes(coeffs, fourier, grid_index, layers, cycle_count, side_pts):
    values = jnp.einsum('fcm,pc->fmp', coeffs, fourier, precision=HIGHEST)
    values = jnp.take(values, grid_index, axis=1)
    return values.reshape(coeffs.shape[0], layers * side_pts, cycle_count * side_pts, coeffs.shape[1])

def to_coeffs(rate_grid, fourier, back_index):
    flattened = jnp.take(rate_grid.reshape(rate_grid.shape[0], -1, rate_grid.shape[-1]), back_index, axis=1)
    coeffs = jnp.einsum('fmp,pc->fcm', flattened, fourier, precision=HIGHEST)
    return jnp.concatenate([coeffs[0:3] + theta_deriv(coeffs[9:12], 1, 0), coeffs[3:9]], axis=0)

def finish_step(velocity, log_conf, rates, orientation, wall_speed, coef_ids, layers_all, cycle_count, side_pts):
    unused, inner_wall, outer_wall = stored_coords(orientation, layers_all, cycle_count, side_pts)
    on_wall = jnp.logical_or(inner_wall, outer_wall)[None, :]
    stepped = velocity + STEP_DT * rates[0:3]
    driven = jnp.where(jnp.logical_and(inner_wall[None, :], (coef_ids == 0)[:, None]), wall_speed[0], 0.0)
    radial_u = jnp.where(on_wall, 0.0, stepped[0])
    azimuth_u = jnp.where(on_wall, driven, stepped[1])
    axial_u = jnp.where(on_wall, 0.0, stepped[2])
    vel_next = jnp.stack([radial_u, azimuth_u, axial_u], axis=0)
    logc_next = log_conf + STEP_DT * rates[3:9]
    return (vel_next, logc_next)

def reference(velocity, log_conf, orientation, wall_speed):
    side_pts = NODE_1D
    cycle_count = CYCLES
    layers = LAYERS_DEV
    blocks = N_MODE
    planes = MODES
    block_nodes = layers * cycle_count * side_pts * side_pts
    radius, deriv_mat = cycle_radius(cycle_count, side_pts)
    fourier = fourier_basis(planes)
    orient_blocks = orientation.reshape(blocks, layers * cycle_count)
    vel_blocks = velocity.reshape(3, planes, blocks, block_nodes).transpose(2, 0, 1, 3)
    logc_blocks = log_conf.reshape(6, planes, blocks, block_nodes).transpose(2, 0, 1, 3)

    def planes_of(vel_c, logc_c, orient):
        grid_index = grid_to_stored(orient, layers, cycle_count, side_pts)
        coeffs = jnp.concatenate([vel_c, theta_deriv(vel_c, 1, 0), logc_c, theta_deriv(logc_c, 1, 0)], axis=0)
        return to_planes(coeffs, fourier, grid_index, layers, cycle_count, side_pts)

    def grad_mean(values):
        raw_grad = velocity_grad(values[0:3], values[3:6], radius, deriv_mat, cycle_count, side_pts)
        return radial_average(raw_grad, cycle_count, side_pts)

    def grad_faces(operands):
        radial_mean = grad_mean(planes_of(operands[0], operands[1], operands[2]))
        return jnp.stack([radial_mean[:, 0], radial_mean[:, -1]], axis=0)
    faces_one = lax.map(grad_faces, (vel_blocks, logc_blocks, orient_blocks))
    below_one = jnp.roll(faces_one[:, 1], 1, axis=0)
    above_one = jnp.roll(faces_one[:, 0], -1, axis=0)

    def combined_rates(operands):
        values = planes_of(operands[0], operands[1], operands[2])
        grad_proj = axial_average(grad_mean(values), operands[3], operands[4], side_pts)
        rate_phys = tendencies(values[0:3], values[6:12], values[12:18], grad_proj, radius, deriv_mat, cycle_count, side_pts)
        return radial_average(rate_phys, cycle_count, side_pts)

    def rate_faces(operands):
        radial_mean = combined_rates(operands)
        return jnp.stack([radial_mean[:, 0], radial_mean[:, -1]], axis=0)
    faces_two = lax.map(rate_faces, (vel_blocks, logc_blocks, orient_blocks, below_one, above_one))
    below_two = jnp.roll(faces_two[:, 1], 1, axis=0)
    above_two = jnp.roll(faces_two[:, 0], -1, axis=0)

    def block_rates(operands):
        rate_grid = axial_average(combined_rates(operands[0:5]), operands[5], operands[6], side_pts)
        back_index = stored_coords(operands[2], layers, cycle_count, side_pts)[0]
        return to_coeffs(rate_grid, fourier, back_index)
    rates_all = lax.map(block_rates, (vel_blocks, logc_blocks, orient_blocks, below_one, above_one, below_two, above_two))
    rates_all = rates_all.transpose(1, 2, 0, 3).reshape(9, planes, blocks * block_nodes)
    coef_ids = jnp.arange(planes, dtype=jnp.int32)
    return finish_step(velocity, log_conf, rates_all, orientation, wall_speed, coef_ids, layers * blocks, cycle_count, side_pts)
```

```python
import functools

import jax
import jax.numpy as jnp
import ml_dtypes
import numpy as np
from jax import lax
from jax.experimental import pallas as pl
from jax.experimental.pallas import tpu as pltpu
from jax.sharding import PartitionSpec as P

SIDE = 8
CYCLES = 2
RADIAL = SIDE * CYCLES
BLOCK = SIDE * RADIAL
STEP_DT = 0.002
RELAX_TIME = 0.02
MOBILITY = 0.3
LAYER_HEIGHT = 0.25
R_INNER = 1.0
MIB = 1 << 20
F32 = jnp.float32
BF16 = jnp.bfloat16


def split_table(table):
    high = np.asarray(table, np.float32).astype(ml_dtypes.bfloat16)
    low = (np.asarray(table, np.float64) - high.astype(np.float64)).astype(ml_dtypes.bfloat16)
    return high, low


def cheb_table(points):
    nodes_xi = -np.cos(np.pi * np.arange(points) / (points - 1))
    weights = np.ones(points)
    weights[0] = 2.0
    weights[-1] = 2.0
    weights = weights * (-1.0) ** np.arange(points)
    identity = np.eye(points)
    spacing = nodes_xi[:, None] - nodes_xi[None, :] + identity
    matrix = weights[:, None] / weights[None, :] / spacing
    matrix = matrix * (1.0 - identity)
    matrix = matrix - identity * matrix.sum(axis=1)[:, None]
    return nodes_xi, matrix


def fourier_tables(planes):
    phase = np.arange(planes)[:, None] * np.arange(planes // 2)[None, :] % planes
    angles = phase * (2.0 * np.pi / planes)
    cosine = np.cos(angles) * np.sqrt(2.0 / planes)
    sine = np.sin(angles) * np.sqrt(2.0 / planes)
    cosine[:, 0] = planes**-0.5
    sine[:, 0] = (-1.0) ** np.arange(planes) * planes**-0.5
    wavenums = np.arange(planes // 2)
    basis = np.stack([cosine, sine], axis=2).reshape(planes, planes)
    turned = np.stack([-wavenums * sine, wavenums * cosine], axis=2).reshape(planes, planes)
    return np.concatenate([basis, turned], axis=0)


def node_tables():
    nodes_xi, matrix = cheb_table(SIDE)
    radius = R_INNER + (np.arange(CYCLES)[:, None] + (nodes_xi[None, :] + 1.0) / 2.0) / CYCLES
    inv_r = 1.0 / radius.reshape(-1)
    radial_row = np.kron(np.eye(CYCLES), matrix.T * (2.0 * CYCLES))
    radial_mean = np.eye(RADIAL)
    for cycle in range(1, CYCLES):
        low, high = cycle * SIDE - 1, cycle * SIDE
        radial_mean[low : high + 1, low : high + 1] = 0.5
    d_radial = np.kron(np.eye(SIDE), radial_row)
    d_axial = np.kron(matrix.T * (2.0 / LAYER_HEIGHT), np.eye(RADIAL))
    own_weight = np.ones(SIDE)
    own_weight[[0, -1]] = 0.5
    average = np.kron(np.diag(own_weight), radial_mean)
    inv_r_nodes = np.tile(inv_r, SIDE)
    both = np.stack(
        [d_radial, d_axial, d_radial @ average, d_axial @ average, average * inv_r_nodes[None, :]]
    )
    faces = np.zeros((3, BLOCK, 2 * BLOCK))
    halos = np.zeros((9, 2 * BLOCK, BLOCK))
    for field in range(3):
        for side, row in ((0, SIDE - 1), (1, 0)):
            at_u = side * BLOCK + field * RADIAL
            at_dz = at_u + 3 * RADIAL
            face_nodes = slice(row * RADIAL, (row + 1) * RADIAL)
            faces[field, face_nodes, at_u : at_u + RADIAL] = np.eye(RADIAL)
            faces[field, :, at_dz : at_dz + RADIAL] = d_axial[:, face_nodes]
            here = SIDE - 1 - row
            out = slice(here * RADIAL, (here + 1) * RADIAL)
            halos[field, at_u : at_u + RADIAL, out] = 0.5 * radial_row @ radial_mean
            halos[3 + field, at_dz : at_dz + RADIAL, out] = 0.5 * radial_mean
            halos[6 + field, at_u : at_u + RADIAL, out] = 0.5 * radial_mean * inv_r[None, :]
    return both, faces, halos, inv_r_nodes


def split(values):
    high = values.astype(BF16)
    return high, (values - high.astype(F32)).astype(BF16)


def dot(left, right):
    return jnp.dot(left, right, preferred_element_type=F32)


def dot3(left, right):
    return dot(left[0], right[0]) + (dot(left[0], right[1]) + dot(left[1], right[0]))


def whole_spec():
    return pl.BlockSpec(memory_space=pltpu.VMEM)


def kernel_call(body, outs, count, scratch=(), vmem=40, flops=0, bytes_accessed=0, name=None):
    return pl.pallas_call(
        body,
        out_shape=outs,
        in_specs=[whole_spec()] * count,
        out_specs=jax.tree.map(lambda _: whole_spec(), outs),
        scratch_shapes=list(scratch),
        compiler_params=pltpu.CompilerParams(vmem_limit_bytes=vmem * MIB),
        cost_estimate=pl.CostEstimate(
            flops=flops, bytes_accessed=bytes_accessed, transcendentals=0
        ),
        name=name,
    )


def pack_body(in_ref, out_ref):
    for layer in range(out_ref.shape[0]):
        out_ref[layer] = in_ref[:, :, layer * BLOCK : (layer + 1) * BLOCK]


def pack(values):
    fields, local_modes, nodes = values.shape
    layers = nodes // BLOCK
    step = 4
    return pl.pallas_call(
        pack_body,
        grid=(layers // step,),
        in_specs=[pl.BlockSpec((fields, local_modes, step * BLOCK), lambda i: (0, 0, i))],
        out_specs=pl.BlockSpec((step, fields, local_modes, BLOCK), lambda i: (i, 0, 0, 0)),
        out_shape=jax.ShapeDtypeStruct((layers, fields, local_modes, BLOCK), F32),
        cost_estimate=pl.CostEstimate(
            flops=0, bytes_accessed=8 * values.size, transcendentals=0
        ),
        name="pack",
    )(values)


def exchange(blocks):
    return lax.all_to_all(blocks, "mode", split_axis=0, concat_axis=0, tiled=True)


def gathered(blocks):
    devices, fields, local_modes, nodes = blocks.shape
    if local_modes % 8 == 0:
        return blocks
    return blocks.transpose(1, 0, 2, 3).reshape(1, fields, devices * local_modes, nodes)


def field_of(ref, field):
    return ref[:, field].reshape(-1, BLOCK)


def order_body(to_grid, from_grid, both_ref, faces_ref, halos_ref, both_out, faces_out, halos_out):
    for at in range(both_ref.shape[0]):
        moved = dot(both_ref[at], from_grid[...]).astype(BF16)
        both_out[at] = dot(to_grid[...], moved).astype(BF16)
    for at in range(faces_ref.shape[0]):
        faces_out[at] = dot(to_grid[...], faces_ref[at]).astype(BF16)
    for at in range(halos_ref.shape[0]):
        halos_out[at] = dot(halos_ref[at], from_grid[...]).astype(BF16)


def face_body(vel_ref, faces_ref, up_ref, down_ref):
    total = None
    for field in range(3):
        own = split(field_of(vel_ref, field))
        part = dot3(own, (faces_ref[2 * field], faces_ref[2 * field + 1]))
        total = part if total is None else total + part
    up_ref[...] = total[:, :BLOCK]
    down_ref[...] = total[:, BLOCK:]


def velocity_body(
    vel_ref, below_ref, above_ref, high_ref, low_ref, both_ref, halos_ref, inv_r_ref,
    flow_ref, values,
):
    planes = high_ref.shape[1]
    table = (high_ref[...], low_ref[...])
    values[:, 0:256] = dot3(
        table, split(jnp.concatenate([field_of(vel_ref, 0), field_of(vel_ref, 1)], axis=1))
    )
    values[:, 256:384] = dot3(table, split(field_of(vel_ref, 2)))
    values[:, 384:640] = dot3(
        table, split(jnp.concatenate([below_ref[...], above_ref[...]], axis=1))
    )
    rows_step = 128

    def matrix(at):
        return both_ref[2 * at], both_ref[2 * at + 1]

    def halo(at):
        return halos_ref[2 * at], halos_ref[2 * at + 1]

    def chunk(step, carry):
        rows = pl.ds(pl.multiple_of(step * rows_step, rows_step), rows_step)
        turned = pl.ds(pl.multiple_of(planes + step * rows_step, rows_step), rows_step)
        u = [values[rows, f * BLOCK : (f + 1) * BLOCK] for f in range(3)]
        u_s = [split(v) for v in u]
        dth_s = [split(values[turned, f * BLOCK : (f + 1) * BLOCK]) for f in range(3)]
        edge = split(values[rows, 384:640])
        edge_dth = split(values[turned, 384:640])
        g_r = [dot3(u_s[f], matrix(2)) + dot3(edge, halo(f)) for f in range(3)]
        g_z = [dot3(u_s[f], matrix(3)) + dot3(edge, halo(3 + f)) for f in range(3)]
        g_t = [dot3(dth_s[f], matrix(4)) + dot3(edge_dth, halo(6 + f)) for f in range(3)]
        mean_r = dot3(u_s[0], matrix(4)) + dot3(edge, halo(6))
        mean_t = dot3(u_s[1], matrix(4)) + dot3(edge, halo(7))
        g_t[0] = g_t[0] - mean_t
        g_t[1] = g_t[1] + mean_r
        hoop_rate = u[1] * inv_r_ref[0:1, :]
        flow_ref[0, rows, :] = u[0]
        flow_ref[1, rows, :] = hoop_rate
        flow_ref[2, rows, :] = u[2]
        flow_ref[3, rows, :] = 0.5 * (g_t[0] - g_r[1]) + hoop_rate
        flow_ref[4, rows, :] = 0.5 * (g_z[0] - g_r[2])
        flow_ref[5, rows, :] = 0.5 * (g_z[1] - g_t[2])
        rest = (1.0 - 2.0 * MOBILITY) / RELAX_TIME
        flow_ref[6, rows, :] = 2.0 * g_r[0] - rest
        flow_ref[7, rows, :] = g_t[0] + g_r[1]
        flow_ref[8, rows, :] = g_z[0] + g_r[2]
        flow_ref[9, rows, :] = 2.0 * g_t[1] - rest
        flow_ref[10, rows, :] = g_z[1] + g_t[2]
        flow_ref[11, rows, :] = 2.0 * g_z[2] - rest
        for f in range(3):
            flow_ref[12 + f, rows, :] = -(g_r[f] * u[0] + g_t[f] * u[1] + g_z[f] * u[2])
        return carry

    lax.fori_loop(0, planes // rows_step, chunk, 0)


def square(m):
    a, b, c, d, e, f = m
    bb, cc, ee = b * b, c * c, e * e
    return (
        a * a + (bb + cc),
        b * (a + d) + c * e,
        c * (a + f) + b * e,
        d * d + (bb + ee),
        e * (d + f) + b * c,
        f * f + (cc + ee),
    )


def commuting_product(m, n):
    a, b, c, d, e, f = m
    p, q, r, s, t, u = n
    return (
        a * p + b * q + c * r,
        a * q + b * s + c * t,
        a * r + b * t + c * u,
        b * q + d * s + e * t,
        b * r + d * t + e * u,
        c * r + e * t + f * u,
    )


DIAGONAL = (0, 3, 5)


def plus_identity(m):
    return tuple(v + 1.0 if at in DIAGONAL else v for at, v in enumerate(m))


def exponentials(psi):
    x = tuple(v * 0.125 for v in psi)
    x2 = square(x)
    x4 = square(x2)
    even = plus_identity(tuple(v * 0.5 + w * (1.0 / 24.0) for v, w in zip(x2, x4)))
    odd = commuting_product(x, plus_identity(tuple(v * (1.0 / 6.0) for v in x2)))
    conform = tuple(v + w for v, w in zip(even, odd))
    inverse = tuple(v - w for v, w in zip(even, odd))
    for _ in range(3):
        conform = square(conform)
        inverse = square(inverse)
    return conform, inverse


def stress_body(
    psi_ref, flow_ref, high_ref, low_ref, back_high_ref, back_low_ref, both_ref, inv_r_ref,
    out_ref, psi_s, dth_s, grad_s, stress_h, stress_l, rate_h, rate_l, vel_h, vel_l, mom_s,
):
    planes = high_ref.shape[1]
    for pair in range(3):
        members = jnp.concatenate(
            [field_of(psi_ref, 2 * pair), field_of(psi_ref, 2 * pair + 1)], axis=1
        )
        values = dot3((high_ref[...], low_ref[...]), split(members))
        for at in range(2):
            psi_s[2 * pair + at] = values[:planes, at * BLOCK : (at + 1) * BLOCK]
            dth_s[2 * pair + at] = values[planes:, at * BLOCK : (at + 1) * BLOCK]
    gradient = tuple(
        jnp.concatenate([both_ref[at], both_ref[2 + at]], axis=1) for at in range(2)
    )
    for member in range(6):
        grad_s[member] = dot3(split(psi_s[member]), gradient)

    rows_step = 16
    inv_relax = 1.0 / RELAX_TIME

    def put(high, low, rows, lanes, value):
        value_h, value_l = split(value)
        high[rows, lanes] = value_h
        low[rows, lanes] = value_l

    def lanes_of(at):
        return slice(at * BLOCK, (at + 1) * BLOCK)

    def chunk(step, carry):
        rows = pl.ds(pl.multiple_of(step * rows_step, rows_step), rows_step)
        inv_r = inv_r_ref[0:1, :]
        psi = tuple(psi_s[member, rows, :] for member in range(6))
        conform, inverse = exponentials(psi)
        u_r, hoop_rate, u_z, p, q, s = (flow_ref[at, rows, :] for at in range(6))
        a, b, c, d, e, f = psi
        pb, qc, se = p * b, q * c, s * e
        turning = (
            2.0 * (pb + qc),
            p * (d - a) + (q * e + s * c),
            q * (f - a) + (p * e - s * b),
            2.0 * (se - pb),
            s * (f - d) - (p * c + q * b),
            -2.0 * (qc + se),
        )
        for member in range(6):
            advect = (
                u_r * grad_s[member, rows, 0:BLOCK]
                + hoop_rate * dth_s[member, rows, :]
                + u_z * grad_s[member, rows, BLOCK : 2 * BLOCK]
            )
            relaxing = ((1.0 - MOBILITY) * inv_relax) * inverse[member] - (
                MOBILITY * inv_relax
            ) * conform[member]
            rate = (turning[member] - advect) + (flow_ref[6 + member, rows, :] + relaxing)
            put(rate_h, rate_l, rows, lanes_of(member), rate)
        stress = tuple(v - 1.0 if at in DIAGONAL else v for at, v in enumerate(conform))
        for member in range(6):
            put(stress_h, stress_l, rows, lanes_of(member), stress[member])
        hoop = tuple(stress[at] * inv_r for at in (1, 3, 4))
        turned = pl.ds(pl.multiple_of(planes + step * rows_step, rows_step), rows_step)
        for at in range(3):
            put(vel_h, vel_l, turned, lanes_of(at), -hoop[at])
        mom_s[0, rows, :] = flow_ref[12, rows, :] + (stress[0] * inv_r - hoop[1])
        mom_s[1, rows, :] = flow_ref[13, rows, :] + 2.0 * hoop[0]
        mom_s[2, rows, :] = flow_ref[14, rows, :] + stress[2] * inv_r
        return carry

    lax.fori_loop(0, planes // rows_step, chunk, 0)

    divergence = tuple(
        jnp.concatenate([both_ref[at], both_ref[2 + at]], axis=0) for at in range(2)
    )
    for at, (radial, axial) in enumerate(((0, 2), (1, 4), (2, 5))):
        pair_s = tuple(
            jnp.concatenate([ref[:, lanes_of(radial)], ref[:, lanes_of(axial)]], axis=1)
            for ref in (stress_h, stress_l)
        )
        put(vel_h, vel_l, slice(0, planes), lanes_of(at), mom_s[at] + dot3(pair_s, divergence))
    blocks, local_modes = out_ref.shape[0], out_ref.shape[2]
    back = (back_high_ref[...], back_low_ref[...])
    for start, stop in ((0, 2), (2, 3)):
        lanes = slice(start * BLOCK, stop * BLOCK)
        coeffs = dot3(back, (vel_h[:, lanes], vel_l[:, lanes]))
        for at in range(start, stop):
            out_ref[:, at] = coeffs[:, lanes_of(at - start)].reshape(blocks, local_modes, BLOCK)
    back = (back_high_ref[:, :planes], back_low_ref[:, :planes])
    for pair in range(3):
        lanes = slice(2 * pair * BLOCK, (2 * pair + 2) * BLOCK)
        coeffs = dot3(back, (rate_h[:, lanes], rate_l[:, lanes]))
        for at in range(2):
            out_ref[:, 3 + 2 * pair + at] = coeffs[:, lanes_of(at)].reshape(
                blocks, local_modes, BLOCK
            )


def step_body(
    layers, step, rates_ref, mean_ref, place_ref, vel_ref, logc_ref, wall_ref, vel_out, logc_out
):
    fields, local_modes = rates_ref.shape[1], rates_ref.shape[2]
    merged = local_modes % 8 == 0
    first = pl.program_id(0) * step

    def averaged(index, at, field):
        below = lax.rem(index + (layers - 1), layers)
        above = lax.rem(index + 1, layers)
        total = None
        for number, layer in enumerate((below, index, above)):
            block = rates_ref[layer] if field is None else rates_ref[layer, field]
            high, low = split(block.reshape(-1, BLOCK))
            weights = mean_ref[at, number * BLOCK : (number + 1) * BLOCK, :]
            part = dot(high, weights) + dot(low, weights)
            total = part if total is None else total + part
        return total

    for at in range(step):
        index = first + at
        lanes = slice(at * BLOCK, (at + 1) * BLOCK)
        place = place_ref[at]
        inner = place % RADIAL == 0
        on_wall = jnp.logical_or(inner, place % RADIAL == RADIAL - 1)
        if merged:
            every = averaged(index, at, None)
            rates = [every[f * local_modes : (f + 1) * local_modes] for f in range(fields)]
        else:
            rates = [averaged(index, at, f) for f in range(fields)]
        shape = (local_modes, BLOCK)
        wall = jnp.broadcast_to(on_wall, shape)
        row_ids = lax.broadcasted_iota(jnp.int32, shape, 0)
        mean_row = jnp.logical_and(row_ids == 0, jnp.broadcast_to(inner, shape))
        driven = jnp.where(mean_row, wall_ref[0], 0.0)
        for field in range(3):
            stepped = vel_ref[field, :, lanes] + STEP_DT * rates[field]
            held = driven if field == 1 else 0.0
            vel_out[field, :, lanes] = jnp.where(wall, held, stepped)
        for field in range(6):
            logc_out[field, :, lanes] = logc_ref[field, :, lanes] + STEP_DT * rates[3 + field]


def advance(rates, means, place, velocity, log_conf, wall):
    layers, fields, local_modes, _ = rates.shape
    step = 4
    nodes = step * BLOCK
    return pl.pallas_call(
        functools.partial(step_body, layers, step),
        grid=(layers // step,),
        in_specs=[
            pl.BlockSpec(rates.shape, lambda i: (0, 0, 0, 0)),
            pl.BlockSpec((step, 3 * BLOCK, BLOCK), lambda i: (i, 0, 0)),
            pl.BlockSpec((step, 1, BLOCK), lambda i: (i, 0, 0)),
            pl.BlockSpec((3, local_modes, nodes), lambda i: (0, 0, i)),
            pl.BlockSpec((6, local_modes, nodes), lambda i: (0, 0, i)),
            pl.BlockSpec(memory_space=pltpu.SMEM),
        ],
        out_specs=[
            pl.BlockSpec((3, local_modes, nodes), lambda i: (0, 0, i)),
            pl.BlockSpec((6, local_modes, nodes), lambda i: (0, 0, i)),
        ],
        out_shape=[
            jax.ShapeDtypeStruct(velocity.shape, F32),
            jax.ShapeDtypeStruct(log_conf.shape, F32),
        ],
        compiler_params=pltpu.CompilerParams(vmem_limit_bytes=32 * MIB),
        name="advance",
    )(rates, means, place, velocity, log_conf, wall)


def grid_places(orientation):
    orient = orientation.reshape(-1, CYCLES, 1, 1)
    cycle = jnp.arange(CYCLES, dtype=jnp.int32).reshape(1, CYCLES, 1, 1)
    lead = jnp.arange(SIDE, dtype=jnp.int32).reshape(1, 1, SIDE, 1)
    trail = jnp.arange(SIDE, dtype=jnp.int32).reshape(1, 1, 1, SIDE)
    lead = jnp.where(orient % 2 == 1, SIDE - 1 - lead, lead)
    trail = jnp.where(orient // 2 % 2 == 1, SIDE - 1 - trail, trail)
    swapped = orient // 4 % 2 == 1
    row = jnp.where(swapped, trail, lead)
    col = jnp.where(swapped, lead, trail)
    return (row * RADIAL + cycle * SIDE + col).reshape(-1, BLOCK)


def mean_weights(place):
    below = jnp.roll(place, 1, axis=0)
    above = jnp.roll(place, -1, axis=0)
    source = jnp.stack([below, place, above], axis=1)[..., None]
    target = place[:, None, None, :]
    kind = jnp.arange(3, dtype=jnp.int32).reshape(1, 3, 1, 1)
    src_x, dst_x = source % RADIAL, target % RADIAL
    src_y, dst_y = source // RADIAL, target // RADIAL

    def near(x):
        inside = jnp.logical_and(x >= SIDE // 2, x < RADIAL - SIDE // 2)
        return jnp.logical_and(inside, jnp.logical_or(x % SIDE == 0, x % SIDE == SIDE - 1))

    both_near = jnp.logical_and(near(src_x), near(dst_x))
    joined = jnp.logical_and(both_near, (src_x + 1) // SIDE == (dst_x + 1) // SIDE)
    radial = jnp.where(joined, 0.5, jnp.where(src_x == dst_x, 1.0, 0.0))
    on_face = jnp.logical_or(dst_y == 0, dst_y == SIDE - 1)
    own = jnp.where(src_y == dst_y, jnp.where(on_face, 0.5, 1.0), 0.0)
    from_below = jnp.logical_and(dst_y == 0, src_y == SIDE - 1)
    from_above = jnp.logical_and(dst_y == SIDE - 1, src_y == 0)
    axial = jnp.where(
        kind == 1, own, jnp.where(jnp.where(kind == 0, from_below, from_above), 0.5, 0.0)
    )
    return (radial * axial).astype(BF16).reshape(-1, 3 * BLOCK, BLOCK)


def body(velocity, log_conf, orientation, wall_speed):
    devices = lax.axis_size("mode")
    device = lax.axis_index("mode")
    local_modes = velocity.shape[1]
    planes = local_modes * devices
    both, faces, halos, inv_r_nodes = node_tables()

    def parts(tables):
        return jnp.asarray(np.stack([half for table in tables for half in split_table(table)]))

    fourier = fourier_tables(planes)
    high, low = (jnp.asarray(half) for half in split_table(fourier))
    back_high, back_low = (jnp.asarray(half) for half in split_table(fourier.T))

    place = grid_places(orientation)
    own_place = lax.dynamic_slice_in_dim(place, device, 1)
    grid_ids = jnp.arange(BLOCK, dtype=jnp.int32)
    from_grid = (grid_ids[:, None] == own_place).astype(BF16)
    to_grid = (own_place.reshape(BLOCK, 1) == grid_ids[None, :]).astype(BF16)
    table_r = jnp.asarray(inv_r_nodes, F32)
    inv_r = jnp.sum(jnp.where(grid_ids[:, None] == own_place, table_r[:, None], 0.0), axis=0)
    inv_r = jnp.broadcast_to(inv_r[None, :], (8, BLOCK))

    vel_nodes = gathered(exchange(pack(velocity)))
    psi_nodes = gathered(exchange(pack(log_conf)))

    both_s, faces_s, halos_s = kernel_call(
        order_body,
        (
            jax.ShapeDtypeStruct((10, BLOCK, BLOCK), BF16),
            jax.ShapeDtypeStruct((6, BLOCK, 2 * BLOCK), BF16),
            jax.ShapeDtypeStruct((18, 2 * BLOCK, BLOCK), BF16),
        ),
        5,
        vmem=16,
        flops=2 * BLOCK**3 * 68,
        bytes_accessed=5 * MIB,
        name="order",
    )(to_grid, from_grid, parts(both), parts(faces), parts(halos))

    edge = jax.ShapeDtypeStruct((planes, BLOCK), F32)
    to_up, to_down = kernel_call(
        face_body, (edge, edge), 2, vmem=16, flops=2 * 3 * planes * 384 * 256,
        bytes_accessed=2 * MIB, name="faces",
    )(vel_nodes, faces_s)
    up = [(i, (i + 1) % devices) for i in range(devices)]
    below = lax.ppermute(to_up, "mode", up)
    above = lax.ppermute(to_down, "mode", [(j, i) for i, j in up])

    flow = kernel_call(
        velocity_body,
        jax.ShapeDtypeStruct((15, planes, BLOCK), F32),
        8,
        scratch=[pltpu.VMEM((2 * planes, 5 * BLOCK), F32)],
        vmem=32,
        flops=12 * 10**9,
        bytes_accessed=8 * MIB,
        name="velocity",
    )(vel_nodes, below, above, high, low, both_s, halos_s, inv_r)

    rates = kernel_call(
        stress_body,
        jax.ShapeDtypeStruct(psi_nodes.shape[:1] + (9,) + psi_nodes.shape[2:], F32),
        8,
        scratch=[
            pltpu.VMEM((6, planes, BLOCK), F32),
            pltpu.VMEM((6, planes, BLOCK), F32),
            pltpu.VMEM((6, planes, 2 * BLOCK), F32),
            pltpu.VMEM((planes, 6 * BLOCK), BF16),
            pltpu.VMEM((planes, 6 * BLOCK), BF16),
            pltpu.VMEM((planes, 6 * BLOCK), BF16),
            pltpu.VMEM((planes, 6 * BLOCK), BF16),
            pltpu.VMEM((2 * planes, 3 * BLOCK), BF16),
            pltpu.VMEM((2 * planes, 3 * BLOCK), BF16),
            pltpu.VMEM((3, planes, BLOCK), F32),
        ],
        vmem=50,
        flops=12 * 10**9,
        bytes_accessed=12 * MIB,
        name="stress",
    )(psi_nodes, flow, high, low, back_high, back_low, both_s, inv_r)

    if local_modes % 8:
        rates = rates.reshape(9, devices, local_modes, BLOCK).transpose(1, 0, 2, 3)
    mode_rates = exchange(rates)
    wall = jnp.where(device == 0, wall_speed, 0.0)
    return tuple(
        advance(mode_rates, mean_weights(place), place[:, None, :], velocity, log_conf, wall)
    )


def solution(mesh):
    in_specs = (P("ens", "mode", None), P("ens", "mode", None), P(), P("ens"))
    out_specs = (P("ens", "mode", None), P("ens", "mode", None))
    return jax.shard_map(body, mesh=mesh, in_specs=in_specs, out_specs=out_specs, check_vma=False)
```

```python
import functools

import jax
import jax.numpy as jnp
import ml_dtypes
import numpy as np
from jax import lax
from jax.experimental import pallas as pl
from jax.experimental.pallas import tpu as pltpu
from jax.sharding import PartitionSpec as P

SIDE = 8
CYCLES = 2
RADIAL = SIDE * CYCLES
BLOCK = SIDE * RADIAL
STEP_DT = 0.002
RELAX_TIME = 0.02
MOBILITY = 0.3
LAYER_HEIGHT = 0.25
R_INNER = 1.0
MIB = 1 << 20
F32 = jnp.float32
BF16 = jnp.bfloat16


def split_table(table):
    high = np.asarray(table, np.float32).astype(ml_dtypes.bfloat16)
    low = (np.asarray(table, np.float64) - high.astype(np.float64)).astype(ml_dtypes.bfloat16)
    return high, low


def cheb_table(points):
    nodes_xi = -np.cos(np.pi * np.arange(points) / (points - 1))
    weights = np.ones(points)
    weights[0] = 2.0
    weights[-1] = 2.0
    weights = weights * (-1.0) ** np.arange(points)
    identity = np.eye(points)
    spacing = nodes_xi[:, None] - nodes_xi[None, :] + identity
    matrix = weights[:, None] / weights[None, :] / spacing
    matrix = matrix * (1.0 - identity)
    matrix = matrix - identity * matrix.sum(axis=1)[:, None]
    return nodes_xi, matrix


def fourier_tables(planes):
    phase = np.arange(planes)[:, None] * np.arange(planes // 2)[None, :] % planes
    angles = phase * (2.0 * np.pi / planes)
    cosine = np.cos(angles) * np.sqrt(2.0 / planes)
    sine = np.sin(angles) * np.sqrt(2.0 / planes)
    cosine[:, 0] = planes**-0.5
    sine[:, 0] = (-1.0) ** np.arange(planes) * planes**-0.5
    wavenums = np.arange(planes // 2)
    basis = np.stack([cosine, sine], axis=2).reshape(planes, planes)
    turned = np.stack([-wavenums * sine, wavenums * cosine], axis=2).reshape(planes, planes)
    return np.concatenate([basis, turned], axis=0)


def node_tables():
    nodes_xi, matrix = cheb_table(SIDE)
    radius = R_INNER + (np.arange(CYCLES)[:, None] + (nodes_xi[None, :] + 1.0) / 2.0) / CYCLES
    inv_r = 1.0 / radius.reshape(-1)
    radial_row = np.kron(np.eye(CYCLES), matrix.T * (2.0 * CYCLES))
    radial_mean = np.eye(RADIAL)
    for cycle in range(1, CYCLES):
        low, high = cycle * SIDE - 1, cycle * SIDE
        radial_mean[low : high + 1, low : high + 1] = 0.5
    d_radial = np.kron(np.eye(SIDE), radial_row)
    d_axial = np.kron(matrix.T * (2.0 / LAYER_HEIGHT), np.eye(RADIAL))
    own_weight = np.ones(SIDE)
    own_weight[[0, -1]] = 0.5
    average = np.kron(np.diag(own_weight), radial_mean)
    inv_r_nodes = np.tile(inv_r, SIDE)
    both = np.stack(
        [d_radial, d_axial, d_radial @ average, d_axial @ average, average * inv_r_nodes[None, :]]
    )
    below = np.zeros((SIDE, SIDE))
    below[SIDE - 1, 0] = 0.5
    means = np.stack([np.kron(below, radial_mean), average, np.kron(below.T, radial_mean)])
    faces = np.zeros((3, BLOCK, 2 * BLOCK))
    halos = np.zeros((9, 2 * BLOCK, BLOCK))
    for field in range(3):
        for side, row in ((0, SIDE - 1), (1, 0)):
            at_u = side * BLOCK + field * RADIAL
            at_dz = at_u + 3 * RADIAL
            face_nodes = slice(row * RADIAL, (row + 1) * RADIAL)
            faces[field, face_nodes, at_u : at_u + RADIAL] = np.eye(RADIAL)
            faces[field, :, at_dz : at_dz + RADIAL] = d_axial[:, face_nodes]
            here = SIDE - 1 - row
            out = slice(here * RADIAL, (here + 1) * RADIAL)
            halos[field, at_u : at_u + RADIAL, out] = 0.5 * radial_row @ radial_mean
            halos[3 + field, at_dz : at_dz + RADIAL, out] = 0.5 * radial_mean
            halos[6 + field, at_u : at_u + RADIAL, out] = 0.5 * radial_mean * inv_r[None, :]
    return both, faces, halos, means, inv_r_nodes


def split(values):
    high = values.astype(BF16)
    return high, (values - high.astype(F32)).astype(BF16)


def dot(left, right):
    return jnp.dot(left, right, preferred_element_type=F32)


def dot3(left, right):
    return dot(left[0], right[0]) + (dot(left[0], right[1]) + dot(left[1], right[0]))


def whole_spec():
    return pl.BlockSpec(memory_space=pltpu.VMEM)


def kernel_call(
    body, outs, count, scalars=1, scratch=(), vmem=40, name=None
):
    return pl.pallas_call(
        body,
        out_shape=outs,
        in_specs=[pl.BlockSpec(memory_space=pltpu.SMEM)] * scalars + [whole_spec()] * count,
        out_specs=jax.tree.map(lambda _: whole_spec(), outs),
        scratch_shapes=list(scratch),
        compiler_params=pltpu.CompilerParams(vmem_limit_bytes=vmem * MIB),
        name=name,
    )


def lanes_of(at):
    return slice(at * BLOCK, (at + 1) * BLOCK)


def put(high, low, rows, lanes, value):
    value_h, value_l = split(value)
    high[rows, lanes] = value_h
    low[rows, lanes] = value_l


NEAR = 4


def swap(block, bits):
    devices = lax.axis_size("mode")
    return lax.ppermute(block, "mode", [(i, i ^ bits) for i in range(devices)])


def far_swaps(groups):
    return [groups[0]] + [swap(groups[s], NEAR * s) for s in (1, 2, 3)]


def near_swaps(groups):
    return [groups[0]] + [swap(groups[t], t) for t in (1, 2, 3)]


def regroup(groups):
    return [jnp.stack([group[at] for group in groups]) for at in range(NEAR)]


class Route:
    def __init__(self, devices, local_modes, far_first):
        self.staged = devices == NEAR * NEAR and local_modes % 16 == 0
        self.aligned = self.staged or local_modes % 16 == 0
        self.devices, self.local_modes, self.far_first = devices, local_modes, far_first
        self.modes = local_modes if self.aligned else local_modes * devices
        if not self.staged:
            self.pack = self.land = [(0, at, at) for at in range(devices)]
            self.leave = self.arrive = self.pack if self.aligned else [(0, 0, 0)]
            return
        far = [(s, t, NEAR * s + t) for s in range(NEAR) for t in range(NEAR)]
        near = [(t, s, NEAR * s + t) for s in range(NEAR) for t in range(NEAR)]
        self.pack = self.leave = far if far_first else near
        self.land = self.arrive = near if far_first else far

    def outs(self, blocks, *block):
        arrays, places = (1 + max(entry[at] for entry in blocks) for at in range(2))
        return [jax.ShapeDtypeStruct((places,) + block, F32)] * arrays

    def index(self, me_ref, rel):
        return (me_ref[0] ^ rel) if self.staged else rel

    def rows(self, me_ref, rel):
        start = self.index(me_ref, rel) * self.modes
        return pl.ds(pl.multiple_of(start, self.modes), self.modes)

    def load(self, me_ref, refs, high, low):
        for array, place, rel in self.arrive:
            rows = self.rows(me_ref, rel)
            for field in range(refs[array].shape[1]):
                put(high, low, rows, lanes_of(field), refs[array][place, field])

    def store(self, me_ref, refs, field, coeffs):
        for array, place, rel in self.leave:
            refs[array][place, field] = coeffs[self.rows(me_ref, rel), :]

    def packed(self, arrays):
        if self.aligned:
            return arrays
        _, fields, planes, nodes = arrays[0].shape
        blocks = arrays[0].reshape(fields, planes // self.local_modes, self.local_modes, nodes)
        return [blocks.transpose(1, 0, 2, 3)]

    def unpacked(self, arrays):
        if self.aligned:
            return arrays
        devices, fields, modes, nodes = arrays[0].shape
        return [arrays[0].transpose(1, 0, 2, 3).reshape(1, fields, devices * modes, nodes)]


def in_one(arrays):
    return [lax.all_to_all(arrays[0], "mode", split_axis=0, concat_axis=0, tiled=True)]


def pack(me, values, routes):
    outs, copies = [], []
    for at, (array, route) in enumerate(zip(values, routes)):
        fields, local_modes, _ = array.shape
        copies += [(at, len(outs) + out, place, rel) for out, place, rel in route.pack]
        outs += route.outs(route.pack, fields, local_modes, BLOCK)
    count = len(values)

    def body(me_ref, *refs):
        in_refs, out_refs, sems = refs[:count], refs[count:-1], refs[-1]
        started = []
        for number, (at, out, place, rel) in enumerate(copies):
            layer = routes[at].index(me_ref, rel)
            lanes = pl.ds(pl.multiple_of(layer * BLOCK, BLOCK), BLOCK)
            copy = pltpu.make_async_copy(
                in_refs[at].at[:, :, lanes], out_refs[out].at[place], sems.at[number]
            )
            copy.start()
            started.append(copy)
        for copy in started:
            copy.wait()

    packed = pl.pallas_call(
        body,
        in_specs=[pl.BlockSpec(memory_space=pltpu.SMEM)]
        + [pl.BlockSpec(memory_space=pl.ANY)] * count,
        out_specs=[whole_spec()] * len(outs),
        out_shape=outs,
        scratch_shapes=[pltpu.SemaphoreType.DMA((len(copies),))],
        name="pack",
    )(me, *values)
    first = len(routes[0].outs(routes[0].pack, 1))
    return packed[:first], packed[first:]


def places(orient_ref, layer, shape):
    lane = lax.broadcasted_iota(jnp.int32, shape, 1)
    cycle = lane // (SIDE * SIDE)
    orient = jnp.where(
        cycle == 0, orient_ref[CYCLES * layer], orient_ref[CYCLES * layer + 1]
    )
    lead, trail = lane // SIDE % SIDE, lane % SIDE
    lead = jnp.where(orient % 2 == 1, SIDE - 1 - lead, lead)
    trail = jnp.where(orient // 2 % 2 == 1, SIDE - 1 - trail, trail)
    swapped = orient // 4 % 2 == 1
    row = jnp.where(swapped, trail, lead)
    col = jnp.where(swapped, lead, trail)
    return row * RADIAL + cycle * SIDE + col


def from_grid(orient_ref, layer):
    shape = (BLOCK, BLOCK)
    grid_ids = lax.broadcasted_iota(jnp.int32, shape, 0)
    return (grid_ids == places(orient_ref, layer, shape)).astype(F32)


def order_body(
    me_ref, orient_ref, both_ref, faces_ref, halos_ref, inv_r_ref,
    both_out, faces_out, halos_out, inv_r_out,
):
    onto = from_grid(orient_ref, me_ref[0])
    inv_r_out[...] = jnp.broadcast_to(
        jnp.sum(onto * inv_r_ref[...], axis=0, keepdims=True), inv_r_out.shape
    )
    back = onto.T.astype(BF16)
    onto = onto.astype(BF16)
    for at in range(both_ref.shape[0]):
        moved = dot(both_ref[at], onto).astype(BF16)
        both_out[at] = dot(back, moved).astype(BF16)
    for at in range(faces_ref.shape[0]):
        faces_out[at] = dot(back, faces_ref[at]).astype(BF16)
    for at in range(halos_ref.shape[0]):
        halos_out[at] = dot(halos_ref[at], onto).astype(BF16)


def weights_body(layers, step, orient_ref, means_ref, out_ref):
    first = pl.program_id(0) * step
    for at in range(step):
        index = first + at
        onto = from_grid(orient_ref, index).astype(BF16)
        below = lax.rem(index + (layers - 1), layers)
        above = lax.rem(index + 1, layers)
        for number, layer in enumerate((below, index, above)):
            back = from_grid(orient_ref, layer).T.astype(BF16)
            moved = dot(means_ref[number], onto).astype(BF16)
            rows = slice(number * BLOCK, (number + 1) * BLOCK)
            out_ref[at, rows, :] = dot(back, moved).astype(BF16)


def mean_weights(orientation, means, layers):
    step = 4
    return pl.pallas_call(
        functools.partial(weights_body, layers, step),
        grid=(layers // step,),
        in_specs=[
            pl.BlockSpec(memory_space=pltpu.SMEM),
            pl.BlockSpec(means.shape, lambda i: (0, 0, 0)),
        ],
        out_specs=pl.BlockSpec((step, 3 * BLOCK, BLOCK), lambda i: (i, 0, 0)),
        out_shape=jax.ShapeDtypeStruct((layers, 3 * BLOCK, BLOCK), BF16),
        name="weights",
    )(orientation, means)


def face_body(route, count, me_ref, *refs):
    vel_refs, (faces_ref, up_ref, down_ref, high, low) = refs[:count], refs[count:]
    route.load(me_ref, vel_refs, high, low)
    total = None
    for field in range(3):
        lanes = lanes_of(field)
        own = (high[:, lanes], low[:, lanes])
        part = dot3(own, (faces_ref[2 * field], faces_ref[2 * field + 1]))
        total = part if total is None else total + part
    up_ref[...] = total[:, :BLOCK]
    down_ref[...] = total[:, BLOCK:]


def velocity_body(
    vel_h, vel_l, below_ref, above_ref, high_ref, low_ref, both_ref, halos_ref, inv_r_ref,
    flow_ref, values,
):
    planes = high_ref.shape[1]
    table = (high_ref[...], low_ref[...])
    values[:, 0:256] = dot3(table, (vel_h[:, 0:256], vel_l[:, 0:256]))
    values[:, 256:384] = dot3(table, (vel_h[:, 256:384], vel_l[:, 256:384]))
    values[:, 384:640] = dot3(
        table, split(jnp.concatenate([below_ref[...], above_ref[...]], axis=1))
    )
    rows_step = 128

    def matrix(at):
        return both_ref[2 * at], both_ref[2 * at + 1]

    def halo(at):
        return halos_ref[2 * at], halos_ref[2 * at + 1]

    def chunk(step, carry):
        rows = pl.ds(pl.multiple_of(step * rows_step, rows_step), rows_step)
        turned = pl.ds(pl.multiple_of(planes + step * rows_step, rows_step), rows_step)
        u = [values[rows, lanes_of(f)] for f in range(3)]
        u_s = [split(v) for v in u]
        dth_s = [split(values[turned, lanes_of(f)]) for f in range(3)]
        edge = split(values[rows, 384:640])
        edge_dth = split(values[turned, 384:640])
        g_r = [dot3(u_s[f], matrix(2)) + dot3(edge, halo(f)) for f in range(3)]
        g_z = [dot3(u_s[f], matrix(3)) + dot3(edge, halo(3 + f)) for f in range(3)]
        g_t = [dot3(dth_s[f], matrix(4)) + dot3(edge_dth, halo(6 + f)) for f in range(3)]
        mean_r = dot3(u_s[0], matrix(4)) + dot3(edge, halo(6))
        mean_t = dot3(u_s[1], matrix(4)) + dot3(edge, halo(7))
        g_t[0] = g_t[0] - mean_t
        g_t[1] = g_t[1] + mean_r
        hoop_rate = u[1] * inv_r_ref[0:1, :]
        flow_ref[0, rows, :] = u[0]
        flow_ref[1, rows, :] = hoop_rate
        flow_ref[2, rows, :] = u[2]
        flow_ref[3, rows, :] = 0.5 * (g_t[0] - g_r[1]) + hoop_rate
        flow_ref[4, rows, :] = 0.5 * (g_z[0] - g_r[2])
        flow_ref[5, rows, :] = 0.5 * (g_z[1] - g_t[2])
        rest = (1.0 - 2.0 * MOBILITY) / RELAX_TIME
        flow_ref[6, rows, :] = 2.0 * g_r[0] - rest
        flow_ref[7, rows, :] = g_t[0] + g_r[1]
        flow_ref[8, rows, :] = g_z[0] + g_r[2]
        flow_ref[9, rows, :] = 2.0 * g_t[1] - rest
        flow_ref[10, rows, :] = g_z[1] + g_t[2]
        flow_ref[11, rows, :] = 2.0 * g_z[2] - rest
        for f in range(3):
            flow_ref[12 + f, rows, :] = -(g_r[f] * u[0] + g_t[f] * u[1] + g_z[f] * u[2])
        return carry

    lax.fori_loop(0, planes // rows_step, chunk, 0)


def square(m):
    a, b, c, d, e, f = m
    bb, cc, ee = b * b, c * c, e * e
    return (
        a * a + (bb + cc),
        b * (a + d) + c * e,
        c * (a + f) + b * e,
        d * d + (bb + ee),
        e * (d + f) + b * c,
        f * f + (cc + ee),
    )


def commuting_product(m, n):
    a, b, c, d, e, f = m
    p, q, r, s, t, u = n
    return (
        a * p + b * q + c * r,
        a * q + b * s + c * t,
        a * r + b * t + c * u,
        b * q + d * s + e * t,
        b * r + d * t + e * u,
        c * r + e * t + f * u,
    )


DIAGONAL = (0, 3, 5)


def plus_identity(m):
    return tuple(v + 1.0 if at in DIAGONAL else v for at, v in enumerate(m))


def exponential(psi, sign):
    x = tuple(v * (sign * 0.125) for v in psi)
    x2 = square(x)
    x4 = square(x2)
    even = plus_identity(tuple(v * 0.5 + w * (1.0 / 24.0) for v, w in zip(x2, x4)))
    odd = commuting_product(x, plus_identity(tuple(v * (1.0 / 6.0) for v in x2)))
    total = tuple(v + w for v, w in zip(even, odd))
    for _ in range(3):
        total = square(total)
    return total


def row_chunks(planes, rows_step, body):
    def chunk(step, carry):
        body(pl.multiple_of(step * rows_step, rows_step))
        return carry

    lax.fori_loop(0, planes // rows_step, chunk, 0)


def momentum_body(route, count, out_route, out_count, me_ref, *refs):
    psi_refs, refs = refs[:count], refs[count:]
    flow_ref, high_ref, low_ref, back_high_ref, back_low_ref, both_ref, inv_r_ref = refs[:7]
    out_refs, refs = refs[7 : 7 + out_count], refs[7 + out_count :]
    coef_h, coef_l, psi_out, conform_out, stress_h, stress_l, vel_h, vel_l, mom_s, coeffs = refs
    planes = high_ref.shape[1]
    route.load(me_ref, psi_refs, coef_h, coef_l)
    table = (high_ref[:planes, :], low_ref[:planes, :])
    for pair in range(3):
        lanes = slice(2 * pair * BLOCK, (2 * pair + 2) * BLOCK)
        values = dot3(table, (coef_h[:, lanes], coef_l[:, lanes]))
        for at in range(2):
            psi_out[2 * pair + at] = values[:, lanes_of(at)]
    rows_step = 16

    def chunk(start):
        rows = pl.ds(start, rows_step)
        inv_r = inv_r_ref[0:1, :]
        conform = exponential(tuple(psi_out[member, rows, :] for member in range(6)), 1.0)
        for member in range(6):
            conform_out[member, rows, :] = conform[member]
        stress = tuple(v - 1.0 if at in DIAGONAL else v for at, v in enumerate(conform))
        for lane, member in enumerate((0, 2, 1, 4, 2, 5)):
            put(stress_h, stress_l, rows, lanes_of(lane), stress[member])
        hoop = tuple(stress[at] * inv_r for at in (1, 3, 4))
        turned = pl.ds(pl.multiple_of(planes + start, rows_step), rows_step)
        for at in range(3):
            put(vel_h, vel_l, turned, lanes_of(at), -hoop[at])
        mom_s[0, rows, :] = flow_ref[12, rows, :] + (stress[0] * inv_r - hoop[1])
        mom_s[1, rows, :] = flow_ref[13, rows, :] + 2.0 * hoop[0]
        mom_s[2, rows, :] = flow_ref[14, rows, :] + stress[2] * inv_r

    row_chunks(planes, rows_step, chunk)
    divergence = tuple(
        jnp.concatenate([both_ref[at], both_ref[2 + at]], axis=0) for at in range(2)
    )
    for at in range(3):
        lanes = slice(2 * at * BLOCK, (2 * at + 2) * BLOCK)
        force = dot3((stress_h[:, lanes], stress_l[:, lanes]), divergence)
        put(vel_h, vel_l, slice(0, planes), lanes_of(at), mom_s[at] + force)
    back = (back_high_ref[...], back_low_ref[...])
    for start, stop in ((0, 2), (2, 3)):
        lanes = slice(start * BLOCK, stop * BLOCK)
        coeffs[:, lanes] = dot3(back, (vel_h[:, lanes], vel_l[:, lanes]))
    for field in range(3):
        out_route.store(me_ref, out_refs, field, coeffs.at[:, lanes_of(field)])


def elastic_body(first_route, first_count, second_route, second_count, me_ref, *refs):
    (
        coef_h, coef_l, psi_ref, conform_ref, flow_ref, high_ref, low_ref,
        back_high_ref, back_low_ref, both_ref,
    ) = refs[:10]
    first_refs, refs = refs[10 : 10 + first_count], refs[10 + first_count :]
    second_refs, refs = refs[:second_count], refs[second_count:]
    dth_s, grad_s, rate_h, rate_l, coeffs = refs
    planes = high_ref.shape[1]
    table = (high_ref[planes:, :], low_ref[planes:, :])
    for pair in range(3):
        lanes = slice(2 * pair * BLOCK, (2 * pair + 2) * BLOCK)
        values = dot3(table, (coef_h[:, lanes], coef_l[:, lanes]))
        for at in range(2):
            dth_s[2 * pair + at] = values[:, lanes_of(at)]
    gradient = tuple(
        jnp.concatenate([both_ref[at], both_ref[2 + at]], axis=1) for at in range(2)
    )
    for member in range(6):
        grad_s[member] = dot3(split(psi_ref[member]), gradient)
    rows_step = 16
    inv_relax = 1.0 / RELAX_TIME

    def chunk(start):
        rows = pl.ds(start, rows_step)
        psi = tuple(psi_ref[member, rows, :] for member in range(6))
        inverse = exponential(psi, -1.0)
        u_r, hoop_rate, u_z, p, q, s = (flow_ref[at, rows, :] for at in range(6))
        a, b, c, d, e, f = psi
        pb, qc, se = p * b, q * c, s * e
        turning = (
            2.0 * (pb + qc),
            p * (d - a) + (q * e + s * c),
            q * (f - a) + (p * e - s * b),
            2.0 * (se - pb),
            s * (f - d) - (p * c + q * b),
            -2.0 * (qc + se),
        )
        for member in range(6):
            advect = (
                u_r * grad_s[member, rows, 0:BLOCK]
                + hoop_rate * dth_s[member, rows, :]
                + u_z * grad_s[member, rows, BLOCK : 2 * BLOCK]
            )
            relaxing = ((1.0 - MOBILITY) * inv_relax) * inverse[member] - (
                MOBILITY * inv_relax
            ) * conform_ref[member, rows, :]
            rate = (turning[member] - advect) + (flow_ref[6 + member, rows, :] + relaxing)
            put(rate_h, rate_l, rows, lanes_of(member), rate)

    row_chunks(planes, rows_step, chunk)
    back = (back_high_ref[:, :planes], back_low_ref[:, :planes])
    for pair in range(3):
        lanes = slice(2 * pair * BLOCK, (2 * pair + 2) * BLOCK)
        coeffs[:, lanes] = dot3(back, (rate_h[:, lanes], rate_l[:, lanes]))
    for field in range(3):
        first_route.store(me_ref, first_refs, field, coeffs.at[:, lanes_of(field)])
        second_route.store(me_ref, second_refs, field, coeffs.at[:, lanes_of(3 + field)])


def advance_body(layers, step, route, count, start, is_velocity, aliased, *refs):
    me_ref, orient_ref, wall_ref = refs[:3]
    rate_refs, refs = refs[3 : 3 + count], refs[3 + count :]
    mean_ref, old_ref = refs[:2]
    out_ref, rates = refs[2 + aliased :]
    fields, local_modes = old_ref.shape[0], old_ref.shape[1]

    @pl.when(pl.program_id(0) == 0)
    def _():
        for array, place, rel in route.land:
            rates[route.index(me_ref, rel)] = rate_refs[array][place, start : start + fields]

    first = pl.program_id(0) * step
    merged = local_modes % 8 == 0

    def averaged(index, at, field):
        below = lax.rem(index + (layers - 1), layers)
        above = lax.rem(index + 1, layers)
        total = None
        for number, layer in enumerate((below, index, above)):
            block = rates[layer] if field is None else rates[layer, field]
            high, low = split(block.reshape(-1, BLOCK))
            weights = mean_ref[at, number * BLOCK : (number + 1) * BLOCK, :]
            part = dot(high, weights) + dot(low, weights)
            total = part if total is None else total + part
        return total

    for at in range(step):
        index = first + at
        lanes = lanes_of(at)
        if merged:
            every = averaged(index, at, None)
            change = [every[f * local_modes : (f + 1) * local_modes] for f in range(fields)]
        else:
            change = [averaged(index, at, f) for f in range(fields)]
        shape = (local_modes, BLOCK)
        column = places(orient_ref, index, shape) % RADIAL
        inner = column == 0
        on_wall = jnp.logical_or(inner, column == RADIAL - 1)
        mean_row = jnp.logical_and(lax.broadcasted_iota(jnp.int32, shape, 0) == 0, inner)
        driven = jnp.where(mean_row, wall_ref[0], 0.0)
        for field in range(fields):
            stepped = old_ref[field, :, lanes] + STEP_DT * change[field]
            if is_velocity:
                stepped = jnp.where(on_wall, driven if field == 1 else 0.0, stepped)
            out_ref[field, :, lanes] = stepped


def whole_block(array):
    return pl.BlockSpec(array.shape, lambda i: (0,) * array.ndim)


def advance(rates, start, route, weights, old, half, into, me, orientation, wall):
    _, local_modes, nodes = old.shape
    layers = nodes // BLOCK
    step = 4
    fields = 3
    aliased = 0 if into is None else 1
    block = pl.BlockSpec((fields, local_modes, step * BLOCK), lambda i: (half, 0, i))
    scalar = pl.BlockSpec(memory_space=pltpu.SMEM)
    is_velocity = old.shape[0] == fields
    operands = [me, orientation, wall, *rates, weights, old] + ([into] if aliased else [])
    return pl.pallas_call(
        functools.partial(
            advance_body, layers, step, route, len(rates), start, is_velocity, aliased
        ),
        grid=(layers // step,),
        in_specs=[scalar] * 3
        + [whole_block(part) for part in rates]
        + [pl.BlockSpec((step, 3 * BLOCK, BLOCK), lambda i: (i, 0, 0)), block]
        + [pl.BlockSpec(memory_space=pl.ANY)] * aliased,
        out_specs=block,
        out_shape=jax.ShapeDtypeStruct(old.shape, F32),
        scratch_shapes=[pltpu.VMEM((layers, fields, local_modes, BLOCK), F32)],
        input_output_aliases={len(operands) - 1: 0} if aliased else {},
        compiler_params=pltpu.CompilerParams(vmem_limit_bytes=24 * MIB),
        name="advance",
    )(*operands)


def body(velocity, log_conf, orientation, wall_speed):
    devices = lax.axis_size("mode")
    device = lax.axis_index("mode").astype(jnp.int32)
    me = device.reshape(1)
    local_modes = velocity.shape[1]
    layers = velocity.shape[2] // BLOCK
    planes = local_modes * devices
    far_first = Route(devices, local_modes, True)
    near_first = Route(devices, local_modes, False)
    barrier = lax.optimization_barrier
    staged = far_first.staged
    both, faces, halos, means, inv_r_nodes = node_tables()

    def parts(tables):
        return jnp.asarray(np.stack([half for table in tables for half in split_table(table)]))

    fourier = fourier_tables(planes)
    high, low = (jnp.asarray(half) for half in split_table(fourier))
    back_high, back_low = (jnp.asarray(half) for half in split_table(fourier.T))
    inv_r_table = jnp.asarray(np.tile(inv_r_nodes[:, None], (1, BLOCK)), F32)

    both_s, faces_s, halos_s, inv_r = kernel_call(
        order_body,
        (
            jax.ShapeDtypeStruct((10, BLOCK, BLOCK), BF16),
            jax.ShapeDtypeStruct((6, BLOCK, 2 * BLOCK), BF16),
            jax.ShapeDtypeStruct((18, 2 * BLOCK, BLOCK), BF16),
            jax.ShapeDtypeStruct((8, BLOCK), F32),
        ),
        4,
        scalars=2,
        vmem=16,
        name="order",
    )(me, orientation, parts(both), parts(faces), parts(halos), inv_r_table)
    weights = mean_weights(orientation, jnp.asarray(means, BF16), layers)

    vel_nodes, psi_nodes = pack(me, (velocity, log_conf), (far_first, near_first))
    if staged:
        vel_nodes, psi_nodes, (both_s, faces_s, halos_s, inv_r) = barrier(
            (far_swaps(vel_nodes), near_swaps(psi_nodes), (both_s, faces_s, halos_s, inv_r))
        )
        psi_nodes = far_swaps(regroup(psi_nodes))
        vel_nodes = near_swaps(regroup(vel_nodes))
    else:
        vel_nodes = far_first.unpacked(in_one(vel_nodes))
        psi_nodes = near_first.unpacked(in_one(psi_nodes))

    edge = jax.ShapeDtypeStruct((planes, BLOCK), F32)
    vel_half = jax.ShapeDtypeStruct((planes, 3 * BLOCK), BF16)
    to_up, to_down, vel_h, vel_l = kernel_call(
        functools.partial(face_body, far_first, len(vel_nodes)),
        (edge, edge, vel_half, vel_half),
        len(vel_nodes) + 1,
        vmem=16,
        name="faces",
    )(me, *vel_nodes, faces_s)
    up = [(i, (i + 1) % devices) for i in range(devices)]
    below = lax.ppermute(to_up, "mode", up)
    above = lax.ppermute(to_down, "mode", [(j, i) for i, j in up])

    flow = kernel_call(
        velocity_body,
        jax.ShapeDtypeStruct((15, planes, BLOCK), F32),
        9,
        scalars=0,
        scratch=[pltpu.VMEM((2 * planes, 5 * BLOCK), F32)],
        vmem=20,
        name="velocity",
    )(vel_h, vel_l, below, above, high, low, both_s, halos_s, inv_r)

    def leaves(route):
        return route.outs(route.leave, 3, route.modes, BLOCK)

    far_outs, near_outs = leaves(far_first), leaves(near_first)
    psi_half = jax.ShapeDtypeStruct((planes, 6 * BLOCK), BF16)
    field6 = jax.ShapeDtypeStruct((6, planes, BLOCK), F32)
    *vel_rates, psi_h, psi_l, psi, conform = kernel_call(
        functools.partial(
            momentum_body, near_first, len(psi_nodes), far_first, len(far_outs)
        ),
        (*far_outs, psi_half, psi_half, field6, field6),
        len(psi_nodes) + 7,
        scratch=[
            pltpu.VMEM((planes, 6 * BLOCK), BF16),
            pltpu.VMEM((planes, 6 * BLOCK), BF16),
            pltpu.VMEM((2 * planes, 3 * BLOCK), BF16),
            pltpu.VMEM((2 * planes, 3 * BLOCK), BF16),
            pltpu.VMEM((3, planes, BLOCK), F32),
            pltpu.VMEM((planes, 3 * BLOCK), F32),
        ],
        vmem=24,
        name="momentum",
    )(me, *psi_nodes, flow, high, low, back_high, back_low, both_s, inv_r)
    vel_rates = far_first.packed(vel_rates)
    psi_rates = kernel_call(
        functools.partial(
            elastic_body, far_first, len(far_outs), near_first, len(near_outs)
        ),
        (*far_outs, *near_outs),
        10,
        scratch=[
            pltpu.VMEM((6, planes, BLOCK), F32),
            pltpu.VMEM((6, planes, 2 * BLOCK), F32),
            pltpu.VMEM((planes, 6 * BLOCK), BF16),
            pltpu.VMEM((planes, 6 * BLOCK), BF16),
            pltpu.VMEM((planes, 6 * BLOCK), F32),
        ],
        vmem=24,
        name="elastic",
    )(me, psi_h, psi_l, psi, conform, flow, high, low, back_high, back_low, both_s)

    first_rates = far_first.packed(psi_rates[: len(far_outs)])
    second_rates = near_first.packed(psi_rates[len(far_outs) :])
    if staged:
        vel_rates, first_rates, second_rates = barrier(
            (far_swaps(vel_rates), first_rates, second_rates)
        )
        joined = [
            jnp.concatenate(pair, axis=1) for pair in zip(regroup(vel_rates), second_rates)
        ]
        first_rates, vel_rates, weights = barrier(
            (far_swaps(first_rates), near_swaps(joined), weights)
        )
        second_rates = far_swaps(regroup([group[:, 3:] for group in vel_rates]))
        first_rates = near_swaps(regroup(first_rates))
    else:
        vel_rates, first_rates, second_rates = (
            in_one(rates) for rates in (vel_rates, first_rates, second_rates)
        )
    wall = jnp.where(device == 0, wall_speed, 0.0)
    fixed = (me, orientation, wall)
    vel_next = advance(vel_rates, 0, far_first, weights, velocity, 0, None, *fixed)
    logc_next = advance(first_rates, 0, far_first, weights, log_conf, 0, None, *fixed)
    logc_next = advance(second_rates, 0, near_first, weights, log_conf, 1, logc_next, *fixed)
    return vel_next, logc_next


def solution(mesh):
    in_specs = (P("ens", "mode", None), P("ens", "mode", None), P(), P("ens"))
    out_specs = (P("ens", "mode", None), P("ens", "mode", None))
    return jax.shard_map(body, mesh=mesh, in_specs=in_specs, out_specs=out_specs, check_vma=False)
```

```python
import functools

import jax
import jax.numpy as jnp
import ml_dtypes
import numpy as np
from jax import lax
from jax.experimental import pallas as pl
from jax.experimental.pallas import tpu as pltpu
from jax.sharding import PartitionSpec as P

SIDE = 8
CYCLES = 2
RADIAL = SIDE * CYCLES
BLOCK = SIDE * RADIAL
STEP_DT = 0.002
RELAX_TIME = 0.02
MOBILITY = 0.3
LAYER_HEIGHT = 0.25
R_INNER = 1.0
MIB = 1 << 20
F32 = jnp.float32
BF16 = jnp.bfloat16


def split_table(table):
    high = np.asarray(table, np.float32).astype(ml_dtypes.bfloat16)
    low = (np.asarray(table, np.float64) - high.astype(np.float64)).astype(ml_dtypes.bfloat16)
    return high, low


def cheb_table(points):
    nodes_xi = -np.cos(np.pi * np.arange(points) / (points - 1))
    weights = np.ones(points)
    weights[0] = 2.0
    weights[-1] = 2.0
    weights = weights * (-1.0) ** np.arange(points)
    identity = np.eye(points)
    spacing = nodes_xi[:, None] - nodes_xi[None, :] + identity
    matrix = weights[:, None] / weights[None, :] / spacing
    matrix = matrix * (1.0 - identity)
    matrix = matrix - identity * matrix.sum(axis=1)[:, None]
    return nodes_xi, matrix


def fourier_tables(planes):
    phase = np.arange(planes)[:, None] * np.arange(planes // 2)[None, :] % planes
    angles = phase * (2.0 * np.pi / planes)
    cosine = np.cos(angles) * np.sqrt(2.0 / planes)
    sine = np.sin(angles) * np.sqrt(2.0 / planes)
    cosine[:, 0] = planes**-0.5
    sine[:, 0] = (-1.0) ** np.arange(planes) * planes**-0.5
    wavenums = np.arange(planes // 2)
    basis = np.stack([cosine, sine], axis=2).reshape(planes, planes)
    turned = np.stack([-wavenums * sine, wavenums * cosine], axis=2).reshape(planes, planes)
    return np.concatenate([basis, turned], axis=0)


def node_tables():
    nodes_xi, matrix = cheb_table(SIDE)
    radius = R_INNER + (np.arange(CYCLES)[:, None] + (nodes_xi[None, :] + 1.0) / 2.0) / CYCLES
    inv_r = 1.0 / radius.reshape(-1)
    radial_row = np.kron(np.eye(CYCLES), matrix.T * (2.0 * CYCLES))
    radial_mean = np.eye(RADIAL)
    for cycle in range(1, CYCLES):
        low, high = cycle * SIDE - 1, cycle * SIDE
        radial_mean[low : high + 1, low : high + 1] = 0.5
    d_radial = np.kron(np.eye(SIDE), radial_row)
    d_axial = np.kron(matrix.T * (2.0 / LAYER_HEIGHT), np.eye(RADIAL))
    own_weight = np.ones(SIDE)
    own_weight[[0, -1]] = 0.5
    average = np.kron(np.diag(own_weight), radial_mean)
    inv_r_nodes = np.tile(inv_r, SIDE)
    both = np.stack(
        [d_radial, d_axial, d_radial @ average, d_axial @ average, average * inv_r_nodes[None, :]]
    )
    below = np.zeros((SIDE, SIDE))
    below[SIDE - 1, 0] = 0.5
    means = np.stack([np.kron(below, radial_mean), average, np.kron(below.T, radial_mean)])
    faces = np.zeros((3, BLOCK, 2 * BLOCK))
    halos = np.zeros((9, 2 * BLOCK, BLOCK))
    for field in range(3):
        for side, row in ((0, SIDE - 1), (1, 0)):
            at_u = side * BLOCK + field * RADIAL
            at_dz = at_u + 3 * RADIAL
            face_nodes = slice(row * RADIAL, (row + 1) * RADIAL)
            faces[field, face_nodes, at_u : at_u + RADIAL] = np.eye(RADIAL)
            faces[field, :, at_dz : at_dz + RADIAL] = d_axial[:, face_nodes]
            here = SIDE - 1 - row
            out = slice(here * RADIAL, (here + 1) * RADIAL)
            halos[field, at_u : at_u + RADIAL, out] = 0.5 * radial_row @ radial_mean
            halos[3 + field, at_dz : at_dz + RADIAL, out] = 0.5 * radial_mean
            halos[6 + field, at_u : at_u + RADIAL, out] = 0.5 * radial_mean * inv_r[None, :]
    used = 6 * RADIAL
    packed = [faces]
    for number in range(3):
        variant = np.zeros_like(faces)
        for side in (0, BLOCK):
            group = slice(side + number * (BLOCK - used), side + (number + 1) * (BLOCK - used))
            variant[:, :, side + used : side + BLOCK] = faces[:, :, group]
        packed.append(variant)
    return both, np.concatenate(packed), halos, means, inv_r_nodes


def free_places():
    used = 6 * RADIAL
    free = BLOCK - used
    moves = np.zeros((3, BLOCK, BLOCK))
    for number in range(3):
        moves[number, used:, number * free : (number + 1) * free] = np.eye(free)
    return moves


def split(values):
    high = values.astype(BF16)
    return high, (values - high.astype(F32)).astype(BF16)


def dot(left, right):
    return jnp.dot(left, right, preferred_element_type=F32)


def dot3(left, right):
    return dot(left[0], right[0]) + (dot(left[0], right[1]) + dot(left[1], right[0]))


def whole_spec():
    return pl.BlockSpec(memory_space=pltpu.VMEM)


def kernel_call(
    body, outs, count, scalars=1, scratch=(), vmem=40, name=None
):
    return pl.pallas_call(
        body,
        out_shape=outs,
        in_specs=[pl.BlockSpec(memory_space=pltpu.SMEM)] * scalars + [whole_spec()] * count,
        out_specs=jax.tree.map(lambda _: whole_spec(), outs),
        scratch_shapes=list(scratch),
        compiler_params=pltpu.CompilerParams(vmem_limit_bytes=vmem * MIB),
        name=name,
    )


def lanes_of(at):
    return slice(at * BLOCK, (at + 1) * BLOCK)


def put(high, low, rows, lanes, value):
    value_h, value_l = split(value)
    high[rows, lanes] = value_h
    low[rows, lanes] = value_l


NEAR = 4


def swap(block, bits):
    devices = lax.axis_size("mode")
    return lax.ppermute(block, "mode", [(i, i ^ bits) for i in range(devices)])


def after(block, token):
    return lax.optimization_barrier((block, token))[0]


def near_swaps(groups):
    return [groups[0]] + [swap(groups[t], t) for t in (1, 2, 3)]


def far_swaps(groups, beside=None):
    first = groups[1] if beside is None else after(groups[1], beside[1])
    return [groups[0], swap(first, NEAR)] + [swap(groups[s], NEAR * s) for s in (2, 3)]


def regroup(groups):
    return [jnp.stack([group[at] for group in groups]) for at in range(NEAR)]


def turn(groups):
    every = [(s, t) for s in range(NEAR) for t in range(NEAR)]

    def body(*refs):
        in_refs, out_refs, sems = refs[:NEAR], refs[NEAR : 2 * NEAR], refs[-1]
        copies = []
        for number, (s, t) in enumerate(every):
            copy = pltpu.make_async_copy(in_refs[t].at[s], out_refs[s].at[t], sems.at[number])
            copy.start()
            copies.append(copy)
        for copy in copies:
            copy.wait()

    return pl.pallas_call(
        body,
        in_specs=[pl.BlockSpec(memory_space=pl.ANY)] * NEAR,
        out_specs=[pl.BlockSpec(memory_space=pl.ANY)] * NEAR,
        out_shape=[jax.ShapeDtypeStruct(group.shape, F32) for group in groups],
        scratch_shapes=[pltpu.SemaphoreType.DMA((len(every),))],
        compiler_params=pltpu.CompilerParams(vmem_limit_bytes=4 * MIB),
        name="turn",
    )(*groups)


class Route:
    def __init__(self, devices, local_modes, far_first, staged=True):
        self.staged = staged and devices == NEAR * NEAR and local_modes % 16 == 0
        self.aligned = self.staged or local_modes % 16 == 0
        self.devices, self.local_modes, self.far_first = devices, local_modes, far_first
        self.modes = local_modes if self.aligned else local_modes * devices
        if not self.staged:
            self.pack = self.land = [(0, at, at) for at in range(devices)]
            self.leave = self.arrive = self.pack if self.aligned else [(0, 0, 0)]
            return
        far = [(s, t, NEAR * s + t) for s in range(NEAR) for t in range(NEAR)]
        near = [(t, s, NEAR * s + t) for s in range(NEAR) for t in range(NEAR)]
        self.pack = self.leave = far if far_first else near
        self.land = self.arrive = near if far_first else far

    def outs(self, blocks, *block):
        arrays, places = (1 + max(entry[at] for entry in blocks) for at in range(2))
        return [jax.ShapeDtypeStruct((places,) + block, F32)] * arrays

    def index(self, me_ref, rel):
        return (me_ref[0] ^ rel) if self.staged else rel

    def rows(self, me_ref, rel):
        start = self.index(me_ref, rel) * self.modes
        return pl.ds(pl.multiple_of(start, self.modes), self.modes)

    def load(self, me_ref, refs, high, low):
        for array, place, rel in self.arrive:
            rows = self.rows(me_ref, rel)
            for field in range(refs[array].shape[1]):
                put(high, low, rows, lanes_of(field), refs[array][place, field])

    def store(self, me_ref, refs, field, coeffs):
        for array, place, rel in self.leave:
            refs[array][place, field] = coeffs[self.rows(me_ref, rel), :]

    def packed(self, arrays):
        if self.aligned:
            return arrays
        _, fields, planes, nodes = arrays[0].shape
        blocks = arrays[0].reshape(fields, planes // self.local_modes, self.local_modes, nodes)
        return [blocks.transpose(1, 0, 2, 3)]

    def unpacked(self, arrays):
        if self.aligned:
            return arrays
        devices, fields, modes, nodes = arrays[0].shape
        return [arrays[0].transpose(1, 0, 2, 3).reshape(1, fields, devices * modes, nodes)]


def in_one(arrays):
    return [lax.all_to_all(arrays[0], "mode", split_axis=0, concat_axis=0, tiled=True)]


def pack(me, values, routes):
    outs, copies = [], []
    for at, (array, route) in enumerate(zip(values, routes)):
        fields, local_modes, _ = array.shape
        copies += [(at, len(outs) + out, place, rel) for out, place, rel in route.pack]
        outs += route.outs(route.pack, fields, local_modes, BLOCK)
    count = len(values)

    def body(me_ref, *refs):
        in_refs, out_refs, sems = refs[:count], refs[count:-1], refs[-1]
        started = []
        for number, (at, out, place, rel) in enumerate(copies):
            layer = routes[at].index(me_ref, rel)
            lanes = pl.ds(pl.multiple_of(layer * BLOCK, BLOCK), BLOCK)
            copy = pltpu.make_async_copy(
                in_refs[at].at[:, :, lanes], out_refs[out].at[place], sems.at[number]
            )
            copy.start()
            started.append(copy)
        for copy in started:
            copy.wait()

    packed = pl.pallas_call(
        body,
        in_specs=[pl.BlockSpec(memory_space=pltpu.SMEM)]
        + [pl.BlockSpec(memory_space=pl.ANY)] * count,
        out_specs=[whole_spec()] * len(outs),
        out_shape=outs,
        scratch_shapes=[pltpu.SemaphoreType.DMA((len(copies),))],
        name="pack",
    )(me, *values)
    first = len(routes[0].outs(routes[0].pack, 1))
    return packed[:first], packed[first:]


def places(orient_ref, layer, shape):
    lane = lax.broadcasted_iota(jnp.int32, shape, 1)
    cycle = lane >> 6
    orient = jnp.where(
        cycle == 0, orient_ref[CYCLES * layer], orient_ref[CYCLES * layer + 1]
    )
    lead, trail = (lane >> 3) & 7, lane & 7
    lead = jnp.where((orient & 1) == 1, SIDE - 1 - lead, lead)
    trail = jnp.where((orient & 2) == 2, SIDE - 1 - trail, trail)
    swapped = (orient & 4) == 4
    row = jnp.where(swapped, trail, lead)
    col = jnp.where(swapped, lead, trail)
    return row * RADIAL + cycle * SIDE + col


def from_grid(orient_ref, layer):
    shape = (BLOCK, BLOCK)
    grid_ids = lax.broadcasted_iota(jnp.int32, shape, 0)
    return (grid_ids == places(orient_ref, layer, shape)).astype(F32)


def order_body(
    me_ref, orient_ref, both_ref, faces_ref, halos_ref, inv_r_ref,
    both_out, faces_out, halos_out, inv_r_out,
):
    onto = from_grid(orient_ref, me_ref[0])
    inv_r_out[...] = jnp.broadcast_to(
        jnp.sum(onto * inv_r_ref[...], axis=0, keepdims=True), inv_r_out.shape
    )
    back = onto.T.astype(BF16)
    onto = onto.astype(BF16)
    for at in range(both_ref.shape[0]):
        moved = dot(both_ref[at], onto).astype(BF16)
        both_out[at] = dot(back, moved).astype(BF16)
    for at in range(faces_ref.shape[0]):
        faces_out[at] = dot(back, faces_ref[at]).astype(BF16)
    for at in range(halos_ref.shape[0]):
        halos_out[at] = dot(halos_ref[at], onto).astype(BF16)


def weights_body(layers, orient_ref, means_ref, out_ref):
    def one(index, carry):
        onto = from_grid(orient_ref, index).astype(BF16)
        below = lax.rem(index + (layers - 1), layers)
        above = lax.rem(index + 1, layers)
        for number, layer in enumerate((below, index, above)):
            back = from_grid(orient_ref, layer).T.astype(BF16)
            moved = dot(means_ref[number], onto).astype(BF16)
            out_ref[index, number * BLOCK : (number + 1) * BLOCK, :] = dot(back, moved).astype(BF16)
        return carry

    lax.fori_loop(0, layers, one, 0)


def face_body(route, count, me_ref, *refs):
    vel_refs, (faces_ref, up_ref, down_ref, high, low) = refs[:count], refs[count:]
    route.load(me_ref, vel_refs, high, low)
    quarter = high.shape[0] // 4

    def faces(rows, variant):
        total = None
        for field in range(3):
            lanes, at = lanes_of(field), 6 * variant + 2 * field
            part = dot3((high[rows, lanes], low[rows, lanes]), (faces_ref[at], faces_ref[at + 1]))
            total = part if total is None else total + part
        return total

    for number in range(3):
        rows = slice(number * quarter, (number + 1) * quarter)
        total = faces(rows, 0) + faces(slice(3 * quarter, 4 * quarter), 1 + number)
        up_ref[rows, :] = total[:, :BLOCK]
        down_ref[rows, :] = total[:, BLOCK:]


def flow_parts(g_r, g_t, g_z, u):
    return (
        0.5 * (g_t[0] - g_r[1]),
        0.5 * (g_z[0] - g_r[2]),
        0.5 * (g_z[1] - g_t[2]),
        2.0 * g_r[0],
        g_t[0] + g_r[1],
        g_z[0] + g_r[2],
        2.0 * g_t[1],
        g_z[1] + g_t[2],
        2.0 * g_z[2],
        -(g_r[0] * u[0] + g_t[0] * u[1] + g_z[0] * u[2]),
        -(g_r[1] * u[0] + g_t[1] * u[1] + g_z[1] * u[2]),
        -(g_r[2] * u[0] + g_t[2] * u[1] + g_z[2] * u[2]),
    )


def matrix_of(ref, at):
    return ref[2 * at], ref[2 * at + 1]


def velocity_body(
    vel_h, vel_l, high_ref, low_ref, both_ref, inv_r_ref, vel_ref, flow_ref, values
):
    planes = high_ref.shape[1]
    table = (high_ref[...], low_ref[...])
    values[:, 0:256] = dot3(table, (vel_h[:, 0:256], vel_l[:, 0:256]))
    values[:, 256:384] = dot3(table, (vel_h[:, 256:384], vel_l[:, 256:384]))
    rows_step = 128

    def chunk(start):
        rows = pl.ds(start, rows_step)
        turned = pl.ds(pl.multiple_of(planes + start, rows_step), rows_step)
        u = [values[rows, lanes_of(f)] for f in range(3)]
        u_s = [split(v) for v in u]
        dth_s = [split(values[turned, lanes_of(f)]) for f in range(3)]
        g_r = [dot3(u_s[f], matrix_of(both_ref, 2)) for f in range(3)]
        g_z = [dot3(u_s[f], matrix_of(both_ref, 3)) for f in range(3)]
        g_t = [dot3(dth_s[f], matrix_of(both_ref, 4)) for f in range(3)]
        g_t[0] = g_t[0] - dot3(u_s[1], matrix_of(both_ref, 4))
        g_t[1] = g_t[1] + dot3(u_s[0], matrix_of(both_ref, 4))
        hoop_rate = u[1] * inv_r_ref[0:1, :]
        parts = flow_parts(g_r, g_t, g_z, u)
        rest = (1.0 - 2.0 * MOBILITY) / RELAX_TIME
        for f in range(3):
            vel_ref[f, rows, :] = u[f]
        for at, part in enumerate((u[0], hoop_rate, u[2]) + parts):
            if at == 3:
                part = part + hoop_rate
            if at - 6 in DIAGONAL:
                part = part - rest
            flow_ref[at, rows, :] = part

    row_chunks(planes, rows_step, chunk)


def halo_body(
    below_ref, above_ref, vel_ref, own_ref, high_ref, low_ref, halos_ref, places_ref,
    flow_ref, values,
):
    planes = high_ref.shape[1]
    quarter = planes // 4
    edges = []
    for ref in (below_ref, above_ref):
        last = None
        for number in range(3):
            part = split(ref[number * quarter : (number + 1) * quarter, :])
            part = dot(part[0], places_ref[number]) + dot(part[1], places_ref[number])
            last = part if last is None else last + part
        edges.append(jnp.concatenate([ref[...], last], axis=0))
    values[...] = dot3(
        (high_ref[...], low_ref[...]), split(jnp.concatenate(edges, axis=1))
    )
    rows_step = 128

    def chunk(start):
        rows = pl.ds(start, rows_step)
        turned = pl.ds(pl.multiple_of(planes + start, rows_step), rows_step)
        edge, edge_dth = split(values[rows, :]), split(values[turned, :])
        g_r = [dot3(edge, matrix_of(halos_ref, f)) for f in range(3)]
        g_z = [dot3(edge, matrix_of(halos_ref, 3 + f)) for f in range(3)]
        g_t = [dot3(edge_dth, matrix_of(halos_ref, 6 + f)) for f in range(3)]
        g_t[0] = g_t[0] - dot3(edge, matrix_of(halos_ref, 7))
        g_t[1] = g_t[1] + dot3(edge, matrix_of(halos_ref, 6))
        u = [vel_ref[f, rows, :] for f in range(3)]
        for at in range(3):
            flow_ref[at, rows, :] = own_ref[at, rows, :]
        for at, part in enumerate(flow_parts(g_r, g_t, g_z, u)):
            flow_ref[3 + at, rows, :] = own_ref[3 + at, rows, :] + part

    row_chunks(planes, rows_step, chunk)


def square(m):
    a, b, c, d, e, f = m
    bb, cc, ee = b * b, c * c, e * e
    return (
        a * a + (bb + cc),
        b * (a + d) + c * e,
        c * (a + f) + b * e,
        d * d + (bb + ee),
        e * (d + f) + b * c,
        f * f + (cc + ee),
    )


def commuting_product(m, n):
    a, b, c, d, e, f = m
    p, q, r, s, t, u = n
    return (
        a * p + b * q + c * r,
        a * q + b * s + c * t,
        a * r + b * t + c * u,
        b * q + d * s + e * t,
        b * r + d * t + e * u,
        c * r + e * t + f * u,
    )


DIAGONAL = (0, 3, 5)


def plus_identity(m):
    return tuple(v + 1.0 if at in DIAGONAL else v for at, v in enumerate(m))


def exponential(psi, sign):
    x = tuple(v * (sign * 0.125) for v in psi)
    x2 = square(x)
    x4 = square(x2)
    even = plus_identity(tuple(v * 0.5 + w * (1.0 / 24.0) for v, w in zip(x2, x4)))
    odd = commuting_product(x, plus_identity(tuple(v * (1.0 / 6.0) for v in x2)))
    total = tuple(v + w for v, w in zip(even, odd))
    for _ in range(3):
        total = square(total)
    return total


def row_chunks(planes, rows_step, body):
    def chunk(step, carry):
        body(pl.multiple_of(step * rows_step, rows_step))
        return carry

    lax.fori_loop(0, planes // rows_step, chunk, 0)


def transform(high_ref, low_ref, rows, coef_h, coef_l, out_ref):
    table = (high_ref[rows, :], low_ref[rows, :])
    for start, stop in ((0, 2), (2, 3)):
        lanes = slice(start * BLOCK, stop * BLOCK)
        values = dot3(table, (coef_h[:, lanes], coef_l[:, lanes]))
        for at in range(start, stop):
            out_ref[at] = values[:, lanes_of(at - start)]


def values_body(route, count, me_ref, *refs):
    psi_refs, (high_ref, low_ref, coef_h, coef_l, psi_out) = refs[:count], refs[count:]
    route.load(me_ref, psi_refs, coef_h, coef_l)
    transform(high_ref, low_ref, slice(0, high_ref.shape[1]), coef_h, coef_l, psi_out)


def momentum_body(route, count, out_route, out_count, me_ref, *refs):
    psi_refs, refs = refs[:count], refs[count:]
    first_ref, flow_ref, high_ref, low_ref, back_high_ref, back_low_ref, both_ref, inv_r_ref = (
        refs[:8]
    )
    out_refs, refs = refs[8 : 8 + out_count], refs[8 + out_count :]
    coef_h, coef_l, psi_out, conform_out, stress_h, stress_l, vel_h, vel_l, mom_s, coeffs = refs
    planes = high_ref.shape[1]
    route.load(me_ref, psi_refs, coef_h, coef_l)
    transform(high_ref, low_ref, slice(0, planes), coef_h, coef_l, psi_out)
    rows_step = 16

    def chunk(start):
        rows = pl.ds(start, rows_step)
        inv_r = inv_r_ref[0:1, :]
        psi = [ref[member, rows, :] for ref in (first_ref, psi_out) for member in range(3)]
        conform = exponential(psi, 1.0)
        for member in range(6):
            conform_out[member, rows, :] = conform[member]
        stress = tuple(v - 1.0 if at in DIAGONAL else v for at, v in enumerate(conform))
        for lane, member in enumerate((0, 2, 1, 4, 2, 5)):
            put(stress_h, stress_l, rows, lanes_of(lane), stress[member])
        hoop = tuple(stress[at] * inv_r for at in (1, 3, 4))
        turned = pl.ds(pl.multiple_of(planes + start, rows_step), rows_step)
        for at in range(3):
            put(vel_h, vel_l, turned, lanes_of(at), -hoop[at])
        mom_s[0, rows, :] = flow_ref[12, rows, :] + (stress[0] * inv_r - hoop[1])
        mom_s[1, rows, :] = flow_ref[13, rows, :] + 2.0 * hoop[0]
        mom_s[2, rows, :] = flow_ref[14, rows, :] + stress[2] * inv_r

    row_chunks(planes, rows_step, chunk)
    divergence = tuple(
        jnp.concatenate([both_ref[at], both_ref[2 + at]], axis=0) for at in range(2)
    )
    for at in range(3):
        lanes = slice(2 * at * BLOCK, (2 * at + 2) * BLOCK)
        force = dot3((stress_h[:, lanes], stress_l[:, lanes]), divergence)
        put(vel_h, vel_l, slice(0, planes), lanes_of(at), mom_s[at] + force)
    back = (back_high_ref[...], back_low_ref[...])
    for start, stop in ((0, 2), (2, 3)):
        lanes = slice(start * BLOCK, stop * BLOCK)
        coeffs[:, lanes] = dot3(back, (vel_h[:, lanes], vel_l[:, lanes]))
    for field in range(3):
        out_route.store(me_ref, out_refs, field, coeffs.at[:, lanes_of(field)])


def elastic_body(route, me_ref, *refs):
    (
        first_h, first_l, second_h, second_l, first_ref, second_ref, conform_ref, flow_ref,
        high_ref, low_ref, back_high_ref, back_low_ref, both_ref,
    ) = refs[:13]
    out_ref, dth_s, grad_s, rate_h, rate_l, coeffs = refs[13:]
    planes = high_ref.shape[1]
    turned = slice(planes, 2 * planes)
    transform(high_ref, low_ref, turned, first_h, first_l, dth_s.at[pl.ds(0, 3)])
    transform(high_ref, low_ref, turned, second_h, second_l, dth_s.at[pl.ds(3, 3)])
    gradient = tuple(
        jnp.concatenate([both_ref[at], both_ref[2 + at]], axis=1) for at in range(2)
    )
    for member in range(6):
        psi_ref = first_ref if member < 3 else second_ref
        grad_s[member] = dot3(split(psi_ref[member % 3]), gradient)
    rows_step = 16
    inv_relax = 1.0 / RELAX_TIME

    def chunk(start):
        rows = pl.ds(start, rows_step)
        psi = [ref[member, rows, :] for ref in (first_ref, second_ref) for member in range(3)]
        inverse = exponential(psi, -1.0)
        u_r, hoop_rate, u_z, p, q, s = (flow_ref[at, rows, :] for at in range(6))
        a, b, c, d, e, f = psi
        pb, qc, se = p * b, q * c, s * e
        turning = (
            2.0 * (pb + qc),
            p * (d - a) + (q * e + s * c),
            q * (f - a) + (p * e - s * b),
            2.0 * (se - pb),
            s * (f - d) - (p * c + q * b),
            -2.0 * (qc + se),
        )
        for member in range(6):
            advect = (
                u_r * grad_s[member, rows, 0:BLOCK]
                + hoop_rate * dth_s[member, rows, :]
                + u_z * grad_s[member, rows, BLOCK : 2 * BLOCK]
            )
            relaxing = ((1.0 - MOBILITY) * inv_relax) * inverse[member] - (
                MOBILITY * inv_relax
            ) * conform_ref[member, rows, :]
            rate = (turning[member] - advect) + (flow_ref[6 + member, rows, :] + relaxing)
            put(rate_h, rate_l, rows, lanes_of(member), rate)

    row_chunks(planes, rows_step, chunk)
    back = (back_high_ref[:, :planes], back_low_ref[:, :planes])
    for pair in range(3):
        lanes = slice(2 * pair * BLOCK, (2 * pair + 2) * BLOCK)
        coeffs[:, lanes] = dot3(back, (rate_h[:, lanes], rate_l[:, lanes]))
    for field in range(6):
        route.store(me_ref, [out_ref], field, coeffs.at[:, lanes_of(field)])


def advance_body(layers, step, route, count, *refs):
    me_ref, orient_ref, wall_ref = refs[:3]
    rate_refs, (mean_ref, old_ref, out_ref, rates) = refs[3 : 3 + count], refs[3 + count :]
    fields, local_modes = old_ref.shape[0], old_ref.shape[1]

    @pl.when(pl.program_id(0) == 0)
    def _():
        for array, place, rel in route.land:
            rates[route.index(me_ref, rel)] = rate_refs[array][place]

    first = pl.program_id(0) * step
    merged = local_modes % 8 == 0

    def averaged(index, at, field):
        below = lax.rem(index + (layers - 1), layers)
        above = lax.rem(index + 1, layers)
        total = None
        for number, layer in enumerate((below, index, above)):
            block = rates[layer] if field is None else rates[layer, field]
            high, low = split(block.reshape(-1, BLOCK))
            weights = mean_ref[at, number * BLOCK : (number + 1) * BLOCK, :]
            part = dot(high, weights) + dot(low, weights)
            total = part if total is None else total + part
        return total

    for at in range(step):
        index = first + at
        lanes = lanes_of(at)
        if merged:
            every = averaged(index, at, None)
            change = [every[f * local_modes : (f + 1) * local_modes] for f in range(fields)]
        else:
            change = [averaged(index, at, f) for f in range(fields)]
        shape = (local_modes, BLOCK)
        column = places(orient_ref, index, shape) & (RADIAL - 1)
        inner = column == 0
        on_wall = jnp.logical_or(inner, column == RADIAL - 1)
        mean_row = jnp.logical_and(lax.broadcasted_iota(jnp.int32, shape, 0) == 0, inner)
        driven = jnp.where(mean_row, wall_ref[0], 0.0)
        for field in range(fields):
            stepped = old_ref[field, :, lanes] + STEP_DT * change[field]
            if fields == 3:
                stepped = jnp.where(on_wall, driven if field == 1 else 0.0, stepped)
            out_ref[field, :, lanes] = stepped


def advance(rates, route, weights, old, me, orientation, wall):
    fields, local_modes, nodes = old.shape
    layers = nodes // BLOCK
    step = 4
    block = pl.BlockSpec((fields, local_modes, step * BLOCK), lambda i: (0, 0, i))
    scalar = pl.BlockSpec(memory_space=pltpu.SMEM)
    return pl.pallas_call(
        functools.partial(advance_body, layers, step, route, len(rates)),
        grid=(layers // step,),
        in_specs=[scalar] * 3
        + [pl.BlockSpec(part.shape, lambda i: (0, 0, 0, 0)) for part in rates]
        + [pl.BlockSpec((step, 3 * BLOCK, BLOCK), lambda i: (i, 0, 0)), block],
        out_specs=block,
        out_shape=jax.ShapeDtypeStruct(old.shape, F32),
        scratch_shapes=[pltpu.VMEM((layers, fields, local_modes, BLOCK), F32)],
        compiler_params=pltpu.CompilerParams(vmem_limit_bytes=24 * MIB),
        name="advance",
    )(me, orientation, wall, *rates, weights, old)


def body(velocity, log_conf, orientation, wall_speed):
    devices = lax.axis_size("mode")
    device = lax.axis_index("mode").astype(jnp.int32)
    me = device.reshape(1)
    local_modes = velocity.shape[1]
    layers = velocity.shape[2] // BLOCK
    planes = local_modes * devices
    far_first = Route(devices, local_modes, True)
    near_first = Route(devices, local_modes, False)
    whole = Route(devices, local_modes, False, False)
    barrier = lax.optimization_barrier
    staged = far_first.staged
    both, faces, halos, means, inv_r_nodes = node_tables()

    def parts(tables):
        return jnp.asarray(np.stack([half for table in tables for half in split_table(table)]))

    fourier = fourier_tables(planes)
    high, low = (jnp.asarray(half) for half in split_table(fourier))
    back_high, back_low = (jnp.asarray(half) for half in split_table(fourier.T))
    inv_r_table = jnp.asarray(np.tile(inv_r_nodes[:, None], (1, BLOCK)), F32)

    both_s, faces_s, halos_s, inv_r = kernel_call(
        order_body,
        (
            jax.ShapeDtypeStruct((10, BLOCK, BLOCK), BF16),
            jax.ShapeDtypeStruct((24, BLOCK, 2 * BLOCK), BF16),
            jax.ShapeDtypeStruct((18, 2 * BLOCK, BLOCK), BF16),
            jax.ShapeDtypeStruct((8, BLOCK), F32),
        ),
        4,
        scalars=2,
        vmem=16,
        name="order",
    )(me, orientation, parts(both), parts(faces), parts(halos), inv_r_table)
    weights = kernel_call(
        functools.partial(weights_body, layers),
        jax.ShapeDtypeStruct((layers, 3 * BLOCK, BLOCK), BF16),
        1,
        vmem=8 + layers // 8,
        name="weights",
    )(orientation, jnp.asarray(means, BF16))

    vel_nodes, psi_nodes = pack(me, (velocity, log_conf), (far_first, near_first))
    fixed = (both_s, faces_s, halos_s, inv_r, weights)
    if staged:
        psi_nodes = near_swaps(psi_nodes)
        vel_nodes = far_swaps(vel_nodes, psi_nodes)
        vel_nodes, psi_nodes, fixed = barrier((vel_nodes, psi_nodes, fixed))
        vel_nodes = near_swaps(regroup(vel_nodes))
        first_nodes = far_swaps(regroup([group[:, :3] for group in psi_nodes]), vel_nodes)
        second_nodes = regroup([group[:, 3:] for group in psi_nodes])
    else:
        vel_nodes = far_first.unpacked(in_one(vel_nodes))
        psi_nodes = near_first.unpacked(in_one(psi_nodes))
        first_nodes = [group[:, :3] for group in psi_nodes]
        second_nodes = [group[:, 3:] for group in psi_nodes]

    both_s, faces_s, halos_s, inv_r, weights = fixed
    edge = jax.ShapeDtypeStruct((planes // 4 * 3, BLOCK), F32)
    vel_half = jax.ShapeDtypeStruct((planes, 3 * BLOCK), BF16)
    to_up, to_down, vel_h, vel_l = kernel_call(
        functools.partial(face_body, far_first, len(vel_nodes)),
        (edge, edge, vel_half, vel_half),
        len(vel_nodes) + 1,
        vmem=16,
        name="faces",
    )(me, *vel_nodes, faces_s)
    up = [(i, (i + 1) % devices) for i in range(devices)]
    below = lax.ppermute(to_up, "mode", up)
    above = lax.ppermute(to_down, "mode", [(j, i) for i, j in up])

    if staged:
        second_nodes, below, above = barrier((second_nodes, below, above))
        second_nodes = far_swaps(second_nodes)

    vel, own_flow = kernel_call(
        velocity_body,
        (
            jax.ShapeDtypeStruct((3, planes, BLOCK), F32),
            jax.ShapeDtypeStruct((15, planes, BLOCK), F32),
        ),
        6,
        scalars=0,
        scratch=[pltpu.VMEM((2 * planes, 3 * BLOCK), F32)],
        vmem=20,
        name="velocity",
    )(vel_h, vel_l, high, low, both_s, inv_r)
    flow = kernel_call(
        halo_body,
        jax.ShapeDtypeStruct((15, planes, BLOCK), F32),
        8,
        scalars=0,
        scratch=[pltpu.VMEM((2 * planes, 2 * BLOCK), F32)],
        vmem=20,
        name="halo",
    )(below, above, vel, own_flow, high, low, halos_s, jnp.asarray(free_places(), BF16))

    far_outs = far_first.outs(far_first.leave, 3, far_first.modes, BLOCK)
    psi_outs = whole.outs(whole.leave, 6, whole.modes, BLOCK)
    half = jax.ShapeDtypeStruct((planes, 3 * BLOCK), BF16)
    field3 = jax.ShapeDtypeStruct((3, planes, BLOCK), F32)
    field6 = jax.ShapeDtypeStruct((6, planes, BLOCK), F32)
    first_h, first_l, first = kernel_call(
        functools.partial(values_body, near_first, len(first_nodes)),
        (half, half, field3),
        len(first_nodes) + 2,
        vmem=10,
        name="values",
    )(me, *first_nodes, high, low)
    *vel_rates, second_h, second_l, second, conform = kernel_call(
        functools.partial(
            momentum_body, near_first, len(second_nodes), far_first, len(far_outs)
        ),
        (*far_outs, half, half, field3, field6),
        len(second_nodes) + 8,
        scratch=[
            pltpu.VMEM((planes, 6 * BLOCK), BF16),
            pltpu.VMEM((planes, 6 * BLOCK), BF16),
            pltpu.VMEM((2 * planes, 3 * BLOCK), BF16),
            pltpu.VMEM((2 * planes, 3 * BLOCK), BF16),
            pltpu.VMEM((3, planes, BLOCK), F32),
            pltpu.VMEM((planes, 3 * BLOCK), F32),
        ],
        vmem=24,
        name="momentum",
    )(me, *second_nodes, first, flow, high, low, back_high, back_low, both_s, inv_r)
    vel_rates = far_first.packed(vel_rates)
    psi_rates = kernel_call(
        functools.partial(elastic_body, whole),
        (*psi_outs,),
        13,
        scratch=[
            pltpu.VMEM((6, planes, BLOCK), F32),
            pltpu.VMEM((6, planes, 2 * BLOCK), F32),
            pltpu.VMEM((planes, 6 * BLOCK), BF16),
            pltpu.VMEM((planes, 6 * BLOCK), BF16),
            pltpu.VMEM((planes, 6 * BLOCK), F32),
        ],
        vmem=24,
        name="elastic",
    )(
        me, first_h, first_l, second_h, second_l, first, second, conform, flow, high, low,
        back_high, back_low, both_s,
    )

    psi_rates = whole.packed(psi_rates)
    if staged:
        vel_rates, psi_rates = barrier((far_swaps(vel_rates), psi_rates))
        vel_rates = near_swaps(turn(vel_rates))
    else:
        vel_rates = in_one(vel_rates)
    psi_rates = in_one(psi_rates)
    wall = jnp.where(device == 0, wall_speed, 0.0)
    at_walls = (me, orientation, wall)
    vel_next = advance(vel_rates, far_first, weights, velocity, *at_walls)
    logc_next = advance(psi_rates, whole, weights, log_conf, *at_walls)
    return vel_next, logc_next


def solution(mesh):
    in_specs = (P("ens", "mode", None), P("ens", "mode", None), P(), P("ens"))
    out_specs = (P("ens", "mode", None), P("ens", "mode", None))
    return jax.shard_map(body, mesh=mesh, in_specs=in_specs, out_specs=out_specs, check_vma=False)
```

```python
import functools

import jax
import jax.numpy as jnp
import ml_dtypes
import numpy as np
from jax import lax
from jax.experimental import pallas as pl
from jax.experimental.pallas import tpu as pltpu
from jax.sharding import PartitionSpec as P

SIDE = 8
CYCLES = 2
RADIAL = SIDE * CYCLES
BLOCK = SIDE * RADIAL
STEP_DT = 0.002
RELAX_TIME = 0.02
MOBILITY = 0.3
LAYER_HEIGHT = 0.25
R_INNER = 1.0
MIB = 1 << 20
F32 = jnp.float32
BF16 = jnp.bfloat16


def split_table(table):
    high = np.asarray(table, np.float32).astype(ml_dtypes.bfloat16)
    low = (np.asarray(table, np.float64) - high.astype(np.float64)).astype(ml_dtypes.bfloat16)
    return high, low


def cheb_table(points):
    nodes_xi = -np.cos(np.pi * np.arange(points) / (points - 1))
    weights = np.ones(points)
    weights[0] = 2.0
    weights[-1] = 2.0
    weights = weights * (-1.0) ** np.arange(points)
    identity = np.eye(points)
    spacing = nodes_xi[:, None] - nodes_xi[None, :] + identity
    matrix = weights[:, None] / weights[None, :] / spacing
    matrix = matrix * (1.0 - identity)
    matrix = matrix - identity * matrix.sum(axis=1)[:, None]
    return nodes_xi, matrix


def fourier_tables(planes):
    phase = np.arange(planes)[:, None] * np.arange(planes // 2)[None, :] % planes
    angles = phase * (2.0 * np.pi / planes)
    cosine = np.cos(angles) * np.sqrt(2.0 / planes)
    sine = np.sin(angles) * np.sqrt(2.0 / planes)
    cosine[:, 0] = planes**-0.5
    sine[:, 0] = (-1.0) ** np.arange(planes) * planes**-0.5
    wavenums = np.arange(planes // 2)
    basis = np.stack([cosine, sine], axis=2).reshape(planes, planes)
    turned = np.stack([-wavenums * sine, wavenums * cosine], axis=2).reshape(planes, planes)
    return np.concatenate([basis, turned], axis=0)


def node_tables():
    nodes_xi, matrix = cheb_table(SIDE)
    radius = R_INNER + (np.arange(CYCLES)[:, None] + (nodes_xi[None, :] + 1.0) / 2.0) / CYCLES
    inv_r = 1.0 / radius.reshape(-1)
    radial_row = np.kron(np.eye(CYCLES), matrix.T * (2.0 * CYCLES))
    radial_mean = np.eye(RADIAL)
    for cycle in range(1, CYCLES):
        low, high = cycle * SIDE - 1, cycle * SIDE
        radial_mean[low : high + 1, low : high + 1] = 0.5
    d_radial = np.kron(np.eye(SIDE), radial_row)
    d_axial = np.kron(matrix.T * (2.0 / LAYER_HEIGHT), np.eye(RADIAL))
    own_weight = np.ones(SIDE)
    own_weight[[0, -1]] = 0.5
    average = np.kron(np.diag(own_weight), radial_mean)
    inv_r_nodes = np.tile(inv_r, SIDE)
    both = np.stack(
        [d_radial, d_axial, d_radial @ average, d_axial @ average, average * inv_r_nodes[None, :]]
    )
    below = np.zeros((SIDE, SIDE))
    below[SIDE - 1, 0] = 0.5
    means = np.stack([np.kron(below, radial_mean), average, np.kron(below.T, radial_mean)])
    faces = np.zeros((3, BLOCK, 2 * BLOCK))
    halos = np.zeros((9, 2 * BLOCK, BLOCK))
    for field in range(3):
        for side, row in ((0, SIDE - 1), (1, 0)):
            at_u = side * BLOCK + field * RADIAL
            at_dz = at_u + 3 * RADIAL
            face_nodes = slice(row * RADIAL, (row + 1) * RADIAL)
            faces[field, face_nodes, at_u : at_u + RADIAL] = np.eye(RADIAL)
            faces[field, :, at_dz : at_dz + RADIAL] = d_axial[:, face_nodes]
            here = SIDE - 1 - row
            out = slice(here * RADIAL, (here + 1) * RADIAL)
            halos[field, at_u : at_u + RADIAL, out] = 0.5 * radial_row @ radial_mean
            halos[3 + field, at_dz : at_dz + RADIAL, out] = 0.5 * radial_mean
            halos[6 + field, at_u : at_u + RADIAL, out] = 0.5 * radial_mean * inv_r[None, :]
    used = 6 * RADIAL
    packed = [faces]
    for number in range(3):
        variant = np.zeros_like(faces)
        for side in (0, BLOCK):
            group = slice(side + number * (BLOCK - used), side + (number + 1) * (BLOCK - used))
            variant[:, :, side + used : side + BLOCK] = faces[:, :, group]
        packed.append(variant)
    return both, np.concatenate(packed), halos, means, inv_r_nodes


def free_places():
    used = 6 * RADIAL
    free = BLOCK - used
    moves = np.zeros((3, BLOCK, BLOCK))
    for number in range(3):
        moves[number, used:, number * free : (number + 1) * free] = np.eye(free)
    return moves


def split(values):
    high = values.astype(BF16)
    return high, (values - high.astype(F32)).astype(BF16)


def dot(left, right):
    return jnp.dot(left, right, preferred_element_type=F32)


def dot3(left, right):
    return dot(left[0], right[0]) + (dot(left[0], right[1]) + dot(left[1], right[0]))


def whole_spec():
    return pl.BlockSpec(memory_space=pltpu.VMEM)


def kernel_call(
    body, outs, count, scalars=1, scratch=(), vmem=40, name=None
):
    return pl.pallas_call(
        body,
        out_shape=outs,
        in_specs=[pl.BlockSpec(memory_space=pltpu.SMEM)] * scalars + [whole_spec()] * count,
        out_specs=jax.tree.map(lambda _: whole_spec(), outs),
        scratch_shapes=list(scratch),
        compiler_params=pltpu.CompilerParams(vmem_limit_bytes=vmem * MIB),
        name=name,
    )


def lanes_of(at):
    return slice(at * BLOCK, (at + 1) * BLOCK)


def put(high, low, rows, lanes, value):
    value_h, value_l = split(value)
    high[rows, lanes] = value_h
    low[rows, lanes] = value_l


NEAR = 4


def swap(block, bits):
    devices = lax.axis_size("mode")
    return lax.ppermute(block, "mode", [(i, i ^ bits) for i in range(devices)])


def after(block, token):
    return lax.optimization_barrier((block, token))[0]


def near_swaps(groups):
    return [groups[0]] + [swap(groups[t], t) for t in (1, 2, 3)]


def far_swaps(groups, beside=None):
    first = groups[1] if beside is None else after(groups[1], beside[1])
    return [groups[0], swap(first, NEAR)] + [swap(groups[s], NEAR * s) for s in (2, 3)]


def regroup(groups):
    return [jnp.stack([group[at] for group in groups]) for at in range(NEAR)]


def turn(groups):
    every = [(s, t) for s in range(NEAR) for t in range(NEAR)]

    def body(*refs):
        in_refs, out_refs, sems = refs[:NEAR], refs[NEAR : 2 * NEAR], refs[-1]
        copies = []
        for number, (s, t) in enumerate(every):
            copy = pltpu.make_async_copy(in_refs[t].at[s], out_refs[s].at[t], sems.at[number])
            copy.start()
            copies.append(copy)
        for copy in copies:
            copy.wait()

    return pl.pallas_call(
        body,
        in_specs=[pl.BlockSpec(memory_space=pl.ANY)] * NEAR,
        out_specs=[pl.BlockSpec(memory_space=pl.ANY)] * NEAR,
        out_shape=[jax.ShapeDtypeStruct(group.shape, F32) for group in groups],
        scratch_shapes=[pltpu.SemaphoreType.DMA((len(every),))],
        compiler_params=pltpu.CompilerParams(vmem_limit_bytes=4 * MIB),
        name="turn",
    )(*groups)


class Route:
    def __init__(self, devices, local_modes, far_first, staged=True):
        self.staged = staged and devices == NEAR * NEAR and local_modes % 16 == 0
        self.aligned = self.staged or local_modes % 16 == 0
        self.devices, self.local_modes, self.far_first = devices, local_modes, far_first
        self.modes = local_modes if self.aligned else local_modes * devices
        if not self.staged:
            self.pack = self.land = [(0, at, at) for at in range(devices)]
            self.leave = self.arrive = self.pack if self.aligned else [(0, 0, 0)]
            return
        far = [(s, t, NEAR * s + t) for s in range(NEAR) for t in range(NEAR)]
        near = [(t, s, NEAR * s + t) for s in range(NEAR) for t in range(NEAR)]
        self.pack = self.leave = far if far_first else near
        self.land = self.arrive = near if far_first else far

    def outs(self, blocks, *block):
        arrays, places = (1 + max(entry[at] for entry in blocks) for at in range(2))
        return [jax.ShapeDtypeStruct((places,) + block, F32)] * arrays

    def index(self, me_ref, rel):
        return (me_ref[0] ^ rel) if self.staged else rel

    def rows(self, me_ref, rel):
        start = self.index(me_ref, rel) * self.modes
        return pl.ds(pl.multiple_of(start, self.modes), self.modes)

    def load(self, me_ref, refs, high, low):
        for array, place, rel in self.arrive:
            rows = self.rows(me_ref, rel)
            for field in range(refs[array].shape[1]):
                put(high, low, rows, lanes_of(field), refs[array][place, field])

    def store(self, me_ref, refs, field, coeffs):
        for array, place, rel in self.leave:
            refs[array][place, field] = coeffs[self.rows(me_ref, rel), :]

    def packed(self, arrays):
        if self.aligned:
            return arrays
        _, fields, planes, nodes = arrays[0].shape
        blocks = arrays[0].reshape(fields, planes // self.local_modes, self.local_modes, nodes)
        return [blocks.transpose(1, 0, 2, 3)]

    def unpacked(self, arrays):
        if self.aligned:
            return arrays
        devices, fields, modes, nodes = arrays[0].shape
        return [arrays[0].transpose(1, 0, 2, 3).reshape(1, fields, devices * modes, nodes)]


def in_one(arrays):
    return [lax.all_to_all(arrays[0], "mode", split_axis=0, concat_axis=0, tiled=True)]


def pack(me, values, routes):
    outs, copies = [], []
    for at, (array, route) in enumerate(zip(values, routes)):
        fields, local_modes, _ = array.shape
        copies += [(at, len(outs) + out, place, rel) for out, place, rel in route.pack]
        outs += route.outs(route.pack, fields, local_modes, BLOCK)
    count = len(values)

    def body(me_ref, *refs):
        in_refs, out_refs, sems = refs[:count], refs[count:-1], refs[-1]
        started = []
        for number, (at, out, place, rel) in enumerate(copies):
            layer = routes[at].index(me_ref, rel)
            lanes = pl.ds(pl.multiple_of(layer * BLOCK, BLOCK), BLOCK)
            copy = pltpu.make_async_copy(
                in_refs[at].at[:, :, lanes], out_refs[out].at[place], sems.at[number]
            )
            copy.start()
            started.append(copy)
        for copy in started:
            copy.wait()

    packed = pl.pallas_call(
        body,
        in_specs=[pl.BlockSpec(memory_space=pltpu.SMEM)]
        + [pl.BlockSpec(memory_space=pl.ANY)] * count,
        out_specs=[whole_spec()] * len(outs),
        out_shape=outs,
        scratch_shapes=[pltpu.SemaphoreType.DMA((len(copies),))],
        name="pack",
    )(me, *values)
    first = len(routes[0].outs(routes[0].pack, 1))
    return packed[:first], packed[first:]


def places(orient_ref, layer, shape):
    lane = lax.broadcasted_iota(jnp.int32, shape, 1)
    cycle = lane >> 6
    orient = jnp.where(
        cycle == 0, orient_ref[CYCLES * layer], orient_ref[CYCLES * layer + 1]
    )
    lead, trail = (lane >> 3) & 7, lane & 7
    lead = jnp.where((orient & 1) == 1, SIDE - 1 - lead, lead)
    trail = jnp.where((orient & 2) == 2, SIDE - 1 - trail, trail)
    swapped = (orient & 4) == 4
    row = jnp.where(swapped, trail, lead)
    col = jnp.where(swapped, lead, trail)
    return row * RADIAL + cycle * SIDE + col


def from_grid(orient_ref, layer):
    shape = (BLOCK, BLOCK)
    grid_ids = lax.broadcasted_iota(jnp.int32, shape, 0)
    return (grid_ids == places(orient_ref, layer, shape)).astype(F32)


def order_body(
    me_ref, orient_ref, both_ref, faces_ref, halos_ref, inv_r_ref,
    both_out, faces_out, halos_out, inv_r_out,
):
    onto = from_grid(orient_ref, me_ref[0])
    inv_r_out[...] = jnp.broadcast_to(
        jnp.sum(onto * inv_r_ref[...], axis=0, keepdims=True), inv_r_out.shape
    )
    back = onto.T.astype(BF16)
    onto = onto.astype(BF16)
    for at in range(both_ref.shape[0]):
        moved = dot(both_ref[at], onto).astype(BF16)
        both_out[at] = dot(back, moved).astype(BF16)
    for at in range(faces_ref.shape[0]):
        faces_out[at] = dot(back, faces_ref[at]).astype(BF16)
    pairs = ((0, 3), (1, 4), (2, 5), (6, 7), (8, 8))
    for at, pair in enumerate(pairs):
        for half in range(2):
            for side in range(2):
                placed = dot(halos_ref[2 * pair[side] + half], onto).astype(BF16)
                halos_out[2 * at + half, :, side * BLOCK : (side + 1) * BLOCK] = placed


def weights_body(layers, orient_ref, means_ref, out_ref):
    def one(index, carry):
        onto = from_grid(orient_ref, index).astype(BF16)
        below = lax.rem(index + (layers - 1), layers)
        above = lax.rem(index + 1, layers)
        for number, layer in enumerate((below, index, above)):
            back = from_grid(orient_ref, layer).T.astype(BF16)
            moved = dot(means_ref[number], onto).astype(BF16)
            out_ref[index, number * BLOCK : (number + 1) * BLOCK, :] = dot(back, moved).astype(BF16)
        return carry

    lax.fori_loop(0, layers, one, 0)


def face_body(route, count, me_ref, *refs):
    vel_refs, (faces_ref, up_ref, down_ref, high, low) = refs[:count], refs[count:]
    route.load(me_ref, vel_refs, high, low)
    quarter = high.shape[0] // 4

    def faces(rows, variant):
        total = None
        for field in range(3):
            lanes, at = lanes_of(field), 6 * variant + 2 * field
            part = dot3((high[rows, lanes], low[rows, lanes]), (faces_ref[at], faces_ref[at + 1]))
            total = part if total is None else total + part
        return total

    for number in range(3):
        rows = slice(number * quarter, (number + 1) * quarter)
        total = faces(rows, 0) + faces(slice(3 * quarter, 4 * quarter), 1 + number)
        up_ref[rows, :] = total[:, :BLOCK]
        down_ref[rows, :] = total[:, BLOCK:]


FIRST = 3


def members_of(first_ref, second_ref, rows):
    return [ref[at, rows, :] for ref in (first_ref, second_ref) for at in range(ref.shape[0])]


def transform(high_ref, low_ref, rows, coef_h, coef_l, out_ref):
    table = (high_ref[rows, :], low_ref[rows, :])
    fields = out_ref.shape[0]
    for start in range(0, fields, 2):
        stop = min(start + 2, fields)
        lanes = slice(start * BLOCK, stop * BLOCK)
        values = dot3(table, (coef_h[:, lanes], coef_l[:, lanes]))
        for at in range(start, stop):
            out_ref[at] = values[:, lanes_of(at - start)]


def flow_parts(g_r, g_t, g_z, u):
    return (
        0.5 * (g_t[0] - g_r[1]),
        0.5 * (g_z[0] - g_r[2]),
        0.5 * (g_z[1] - g_t[2]),
        2.0 * g_r[0],
        g_t[0] + g_r[1],
        g_z[0] + g_r[2],
        2.0 * g_t[1],
        g_z[1] + g_t[2],
        2.0 * g_z[2],
        -(g_r[0] * u[0] + g_t[0] * u[1] + g_z[0] * u[2]),
        -(g_r[1] * u[0] + g_t[1] * u[1] + g_z[1] * u[2]),
        -(g_r[2] * u[0] + g_t[2] * u[1] + g_z[2] * u[2]),
    )


def matrix_of(ref, at):
    return ref[2 * at], ref[2 * at + 1]


def velocity_body(route, count, me_ref, *refs):
    psi_refs, refs = refs[:count], refs[count:]
    vel_h, vel_l, high_ref, low_ref, both_ref, inv_r_ref, vel_ref, flow_ref = refs[:8]
    coef_h, coef_l, psi_out, values = refs[8:]
    planes = high_ref.shape[1]
    route.load(me_ref, psi_refs, coef_h, coef_l)
    transform(high_ref, low_ref, slice(0, planes), coef_h, coef_l, psi_out)
    table = (high_ref[...], low_ref[...])
    values[:, 0:256] = dot3(table, (vel_h[:, 0:256], vel_l[:, 0:256]))
    values[:, 256:384] = dot3(table, (vel_h[:, 256:384], vel_l[:, 256:384]))
    rows_step = 128

    def chunk(start):
        rows = pl.ds(start, rows_step)
        turned = pl.ds(pl.multiple_of(planes + start, rows_step), rows_step)
        u = [values[rows, lanes_of(f)] for f in range(3)]
        u_s = [split(v) for v in u]
        dth_s = [split(values[turned, lanes_of(f)]) for f in range(3)]
        g_r = [dot3(u_s[f], matrix_of(both_ref, 2)) for f in range(3)]
        g_z = [dot3(u_s[f], matrix_of(both_ref, 3)) for f in range(3)]
        g_t = [dot3(dth_s[f], matrix_of(both_ref, 4)) for f in range(3)]
        g_t[0] = g_t[0] - dot3(u_s[1], matrix_of(both_ref, 4))
        g_t[1] = g_t[1] + dot3(u_s[0], matrix_of(both_ref, 4))
        hoop_rate = u[1] * inv_r_ref[0:1, :]
        parts = flow_parts(g_r, g_t, g_z, u)
        rest = (1.0 - 2.0 * MOBILITY) / RELAX_TIME
        for f in range(3):
            vel_ref[f, rows, :] = u[f]
        for at, part in enumerate((u[0], hoop_rate, u[2]) + parts):
            if at == 3:
                part = part + hoop_rate
            if at - 6 in DIAGONAL:
                part = part - rest
            flow_ref[at, rows, :] = part

    row_chunks(planes, rows_step, chunk)


def halo_body(
    below_ref, above_ref, vel_ref, high_ref, low_ref, halos_ref, places_ref, part_ref, values
):
    planes = high_ref.shape[1]
    quarter = planes // 4
    edges = []
    for ref in (below_ref, above_ref):
        last = None
        for number in range(3):
            part = split(ref[number * quarter : (number + 1) * quarter, :])
            part = dot(part[0], places_ref[number]) + dot(part[1], places_ref[number])
            last = part if last is None else last + part
        edges.append(jnp.concatenate([ref[...], last], axis=0))
    values[...] = dot3((high_ref[...], low_ref[...]), split(jnp.concatenate(edges, axis=1)))
    rows_step = planes // 2

    def chunk(start):
        rows = pl.ds(start, rows_step)
        turned = pl.ds(pl.multiple_of(planes + start, rows_step), rows_step)
        edge, edge_dth = split(values[rows, :]), split(values[turned, :])
        g_r, g_z = zip(*(halved(dot3(edge, matrix_of(halos_ref, f))) for f in range(3)))
        g_t = [
            *halved(dot3(edge_dth, matrix_of(halos_ref, 3))),
            dot3(edge_dth, (halos_ref[8, :, :BLOCK], halos_ref[9, :, :BLOCK])),
        ]
        mean_r, mean_t = halved(dot3(edge, matrix_of(halos_ref, 3)))
        g_t[0] = g_t[0] - mean_t
        g_t[1] = g_t[1] + mean_r
        u = [vel_ref[f, rows, :] for f in range(3)]
        for at, part in enumerate(flow_parts(g_r, g_t, g_z, u)):
            part_ref[at, rows, :] = part

    row_chunks(planes, rows_step, chunk)


def halved(pair):
    return pair[:, :BLOCK], pair[:, BLOCK:]


def square(m):
    a, b, c, d, e, f = m
    bb, cc, ee = b * b, c * c, e * e
    return (
        a * a + (bb + cc),
        b * (a + d) + c * e,
        c * (a + f) + b * e,
        d * d + (bb + ee),
        e * (d + f) + b * c,
        f * f + (cc + ee),
    )


def commuting_product(m, n):
    a, b, c, d, e, f = m
    p, q, r, s, t, u = n
    return (
        a * p + b * q + c * r,
        a * q + b * s + c * t,
        a * r + b * t + c * u,
        b * q + d * s + e * t,
        b * r + d * t + e * u,
        c * r + e * t + f * u,
    )


DIAGONAL = (0, 3, 5)


def plus_identity(m):
    return tuple(v + 1.0 if at in DIAGONAL else v for at, v in enumerate(m))


def exponential(psi, sign):
    x = tuple(v * (sign * 0.125) for v in psi)
    x2 = square(x)
    x4 = square(x2)
    even = plus_identity(tuple(v * 0.5 + w * (1.0 / 24.0) for v, w in zip(x2, x4)))
    odd = commuting_product(x, plus_identity(tuple(v * (1.0 / 6.0) for v in x2)))
    total = tuple(v + w for v, w in zip(even, odd))
    for _ in range(3):
        total = square(total)
    return total


def row_chunks(planes, rows_step, body):
    def chunk(step, carry):
        body(pl.multiple_of(step * rows_step, rows_step))
        return carry

    lax.fori_loop(0, planes // rows_step, chunk, 0)


def momentum_body(route, count, out_route, out_count, me_ref, *refs):
    psi_refs, refs = refs[:count], refs[count:]
    first_ref, flow_ref, halo_ref, high_ref, low_ref = refs[:5]
    back_high_ref, back_low_ref, both_ref, inv_r_ref = refs[5:9]
    out_refs, refs = refs[9 : 9 + out_count], refs[9 + out_count :]
    coef_h, coef_l, psi_out, conform_out, stress_h, stress_l, vel_h, vel_l, mom_s, coeffs = refs
    planes = high_ref.shape[1]
    route.load(me_ref, psi_refs, coef_h, coef_l)
    transform(high_ref, low_ref, slice(0, planes), coef_h, coef_l, psi_out)
    rows_step = 16

    def chunk(start):
        rows = pl.ds(start, rows_step)
        inv_r = inv_r_ref[0:1, :]
        psi = members_of(first_ref, psi_out, rows)
        conform = exponential(psi, 1.0)
        for member in range(6):
            conform_out[member, rows, :] = conform[member]
        stress = tuple(v - 1.0 if at in DIAGONAL else v for at, v in enumerate(conform))
        for lane, member in enumerate((0, 2, 1, 4, 2, 5)):
            put(stress_h, stress_l, rows, lanes_of(lane), stress[member])
        hoop = tuple(stress[at] * inv_r for at in (1, 3, 4))
        turned = pl.ds(pl.multiple_of(planes + start, rows_step), rows_step)
        for at in range(3):
            put(vel_h, vel_l, turned, lanes_of(at), -hoop[at])
        carried = [flow_ref[12 + at, rows, :] + halo_ref[9 + at, rows, :] for at in range(3)]
        mom_s[0, rows, :] = carried[0] + (stress[0] * inv_r - hoop[1])
        mom_s[1, rows, :] = carried[1] + 2.0 * hoop[0]
        mom_s[2, rows, :] = carried[2] + stress[2] * inv_r

    row_chunks(planes, rows_step, chunk)
    divergence = tuple(
        jnp.concatenate([both_ref[at], both_ref[2 + at]], axis=0) for at in range(2)
    )
    for at in range(3):
        lanes = slice(2 * at * BLOCK, (2 * at + 2) * BLOCK)
        force = dot3((stress_h[:, lanes], stress_l[:, lanes]), divergence)
        put(vel_h, vel_l, slice(0, planes), lanes_of(at), mom_s[at] + force)
    back = (back_high_ref[...], back_low_ref[...])
    for start, stop in ((0, 2), (2, 3)):
        lanes = slice(start * BLOCK, stop * BLOCK)
        coeffs[:, lanes] = dot3(back, (vel_h[:, lanes], vel_l[:, lanes]))
    for field in range(3):
        out_route.store(me_ref, out_refs, field, coeffs.at[:, lanes_of(field)])


def elastic_body(route, me_ref, *refs):
    (
        first_h, first_l, second_h, second_l, first_ref, second_ref, conform_ref, flow_ref,
        halo_ref, high_ref, low_ref, back_high_ref, back_low_ref, both_ref,
    ) = refs[:14]
    out_ref, dth_s, grad_s, rate_h, rate_l, coeffs = refs[14:]
    planes = high_ref.shape[1]
    turned = slice(planes, 2 * planes)
    transform(high_ref, low_ref, turned, first_h, first_l, dth_s.at[pl.ds(0, FIRST)])
    transform(high_ref, low_ref, turned, second_h, second_l, dth_s.at[pl.ds(FIRST, 6 - FIRST)])
    gradient = tuple(
        jnp.concatenate([both_ref[at], both_ref[2 + at]], axis=1) for at in range(2)
    )
    for member in range(6):
        psi_ref = first_ref if member < FIRST else second_ref
        grad_s[member] = dot3(split(psi_ref[member % FIRST]), gradient)
    rows_step = 16
    inv_relax = 1.0 / RELAX_TIME

    def chunk(start):
        rows = pl.ds(start, rows_step)
        psi = members_of(first_ref, second_ref, rows)
        inverse = exponential(psi, -1.0)
        u_r, hoop_rate, u_z = (flow_ref[at, rows, :] for at in range(3))
        p, q, s, *strain = (
            flow_ref[3 + at, rows, :] + halo_ref[at, rows, :] for at in range(9)
        )
        a, b, c, d, e, f = psi
        pb, qc, se = p * b, q * c, s * e
        turning = (
            2.0 * (pb + qc),
            p * (d - a) + (q * e + s * c),
            q * (f - a) + (p * e - s * b),
            2.0 * (se - pb),
            s * (f - d) - (p * c + q * b),
            -2.0 * (qc + se),
        )
        for member in range(6):
            advect = (
                u_r * grad_s[member, rows, 0:BLOCK]
                + hoop_rate * dth_s[member, rows, :]
                + u_z * grad_s[member, rows, BLOCK : 2 * BLOCK]
            )
            relaxing = ((1.0 - MOBILITY) * inv_relax) * inverse[member] - (
                MOBILITY * inv_relax
            ) * conform_ref[member, rows, :]
            rate = (turning[member] - advect) + (strain[member] + relaxing)
            put(rate_h, rate_l, rows, lanes_of(member), rate)

    row_chunks(planes, rows_step, chunk)
    back = (back_high_ref[:, :planes], back_low_ref[:, :planes])
    for pair in range(3):
        lanes = slice(2 * pair * BLOCK, (2 * pair + 2) * BLOCK)
        coeffs[:, lanes] = dot3(back, (rate_h[:, lanes], rate_l[:, lanes]))
    for field in range(6):
        route.store(me_ref, [out_ref], field, coeffs.at[:, lanes_of(field)])


def advance_body(layers, step, route, count, *refs):
    me_ref, orient_ref, wall_ref = refs[:3]
    rate_refs, (mean_ref, old_ref, out_ref, rates) = refs[3 : 3 + count], refs[3 + count :]
    fields, local_modes = old_ref.shape[0], old_ref.shape[1]

    @pl.when(pl.program_id(0) == 0)
    def _():
        for array, place, rel in route.land:
            rates[route.index(me_ref, rel)] = rate_refs[array][place]

    first = pl.program_id(0) * step
    merged = local_modes % 8 == 0

    def averaged(index, at, field):
        below = lax.rem(index + (layers - 1), layers)
        above = lax.rem(index + 1, layers)
        total = None
        for number, layer in enumerate((below, index, above)):
            block = rates[layer] if field is None else rates[layer, field]
            high, low = split(block.reshape(-1, BLOCK))
            weights = mean_ref[at, number * BLOCK : (number + 1) * BLOCK, :]
            part = dot(high, weights) + dot(low, weights)
            total = part if total is None else total + part
        return total

    for at in range(step):
        index = first + at
        lanes = lanes_of(at)
        if merged:
            every = averaged(index, at, None)
            change = [every[f * local_modes : (f + 1) * local_modes] for f in range(fields)]
        else:
            change = [averaged(index, at, f) for f in range(fields)]
        shape = (local_modes, BLOCK)
        column = places(orient_ref, index, shape) & (RADIAL - 1)
        inner = column == 0
        on_wall = jnp.logical_or(inner, column == RADIAL - 1)
        mean_row = jnp.logical_and(lax.broadcasted_iota(jnp.int32, shape, 0) == 0, inner)
        driven = jnp.where(mean_row, wall_ref[0], 0.0)
        for field in range(fields):
            stepped = old_ref[field, :, lanes] + STEP_DT * change[field]
            if fields == 3:
                stepped = jnp.where(on_wall, driven if field == 1 else 0.0, stepped)
            out_ref[field, :, lanes] = stepped


def advance(rates, route, weights, old, me, orientation, wall):
    fields, local_modes, nodes = old.shape
    layers = nodes // BLOCK
    step = 4
    block = pl.BlockSpec((fields, local_modes, step * BLOCK), lambda i: (0, 0, i))
    scalar = pl.BlockSpec(memory_space=pltpu.SMEM)
    return pl.pallas_call(
        functools.partial(advance_body, layers, step, route, len(rates)),
        grid=(layers // step,),
        in_specs=[scalar] * 3
        + [pl.BlockSpec(part.shape, lambda i: (0, 0, 0, 0)) for part in rates]
        + [pl.BlockSpec((step, 3 * BLOCK, BLOCK), lambda i: (i, 0, 0)), block],
        out_specs=block,
        out_shape=jax.ShapeDtypeStruct(old.shape, F32),
        scratch_shapes=[pltpu.VMEM((layers, fields, local_modes, BLOCK), F32)],
        compiler_params=pltpu.CompilerParams(vmem_limit_bytes=24 * MIB),
        name="advance",
    )(me, orientation, wall, *rates, weights, old)


def body(velocity, log_conf, orientation, wall_speed):
    devices = lax.axis_size("mode")
    device = lax.axis_index("mode").astype(jnp.int32)
    me = device.reshape(1)
    local_modes = velocity.shape[1]
    layers = velocity.shape[2] // BLOCK
    planes = local_modes * devices
    far_first = Route(devices, local_modes, True)
    near_first = Route(devices, local_modes, False)
    whole = Route(devices, local_modes, False, False)
    barrier = lax.optimization_barrier
    staged = far_first.staged
    both, faces, halos, means, inv_r_nodes = node_tables()

    def parts(tables):
        return jnp.asarray(np.stack([half for table in tables for half in split_table(table)]))

    fourier = fourier_tables(planes)
    high, low = (jnp.asarray(half) for half in split_table(fourier))
    back_high, back_low = (jnp.asarray(half) for half in split_table(fourier.T))
    inv_r_table = jnp.asarray(np.tile(inv_r_nodes[:, None], (1, BLOCK)), F32)

    both_s, faces_s, halos_s, inv_r = kernel_call(
        order_body,
        (
            jax.ShapeDtypeStruct((10, BLOCK, BLOCK), BF16),
            jax.ShapeDtypeStruct((24, BLOCK, 2 * BLOCK), BF16),
            jax.ShapeDtypeStruct((10, 2 * BLOCK, 2 * BLOCK), BF16),
            jax.ShapeDtypeStruct((8, BLOCK), F32),
        ),
        4,
        scalars=2,
        vmem=16,
        name="order",
    )(me, orientation, parts(both), parts(faces), parts(halos), inv_r_table)
    weights = kernel_call(
        functools.partial(weights_body, layers),
        jax.ShapeDtypeStruct((layers, 3 * BLOCK, BLOCK), BF16),
        1,
        vmem=8 + layers // 8,
        name="weights",
    )(orientation, jnp.asarray(means, BF16))

    vel_nodes, psi_nodes = pack(me, (velocity, log_conf), (far_first, near_first))
    fixed = (both_s, faces_s, halos_s, inv_r, weights)
    if staged:
        psi_nodes = near_swaps(psi_nodes)
        vel_nodes = far_swaps(vel_nodes, psi_nodes)
        vel_nodes, psi_nodes, fixed = barrier((vel_nodes, psi_nodes, fixed))
        vel_nodes = near_swaps(regroup(vel_nodes))
        first_nodes = far_swaps(regroup([group[:, :FIRST] for group in psi_nodes]), vel_nodes)
        second_nodes = regroup([group[:, FIRST:] for group in psi_nodes])
    else:
        vel_nodes = far_first.unpacked(in_one(vel_nodes))
        psi_nodes = near_first.unpacked(in_one(psi_nodes))
        first_nodes = [group[:, :FIRST] for group in psi_nodes]
        second_nodes = [group[:, FIRST:] for group in psi_nodes]

    both_s, faces_s, halos_s, inv_r, weights = fixed
    edge = jax.ShapeDtypeStruct((planes // 4 * 3, BLOCK), F32)
    vel_half = jax.ShapeDtypeStruct((planes, 3 * BLOCK), BF16)
    to_up, to_down, vel_h, vel_l = kernel_call(
        functools.partial(face_body, far_first, len(vel_nodes)),
        (edge, edge, vel_half, vel_half),
        len(vel_nodes) + 1,
        vmem=16,
        name="faces",
    )(me, *vel_nodes, faces_s)
    up = [(i, (i + 1) % devices) for i in range(devices)]
    below = lax.ppermute(to_up, "mode", up)
    above = lax.ppermute(to_down, "mode", [(j, i) for i, j in up])

    def halves(fields):
        return (
            jax.ShapeDtypeStruct((planes, fields * BLOCK), BF16),
            jax.ShapeDtypeStruct((planes, fields * BLOCK), BF16),
            jax.ShapeDtypeStruct((fields, planes, BLOCK), F32),
        )

    vel, own_flow, first_h, first_l, first = kernel_call(
        functools.partial(velocity_body, near_first, len(first_nodes)),
        (
            jax.ShapeDtypeStruct((3, planes, BLOCK), F32),
            jax.ShapeDtypeStruct((15, planes, BLOCK), F32),
            *halves(FIRST),
        ),
        len(first_nodes) + 6,
        scratch=[pltpu.VMEM((2 * planes, 3 * BLOCK), F32)],
        vmem=20,
        name="velocity",
    )(me, *first_nodes, vel_h, vel_l, high, low, both_s, inv_r)
    if staged:
        early = second_nodes
        second_nodes, below, above, vel = barrier((second_nodes, below, above, vel))
        second_nodes = far_swaps([early[0], second_nodes[1], early[2], early[3]])
    halo_flow = kernel_call(
        halo_body,
        jax.ShapeDtypeStruct((12, planes, BLOCK), F32),
        7,
        scalars=0,
        scratch=[pltpu.VMEM((2 * planes, 2 * BLOCK), F32)],
        vmem=24,
        name="halo",
    )(below, above, vel, high, low, halos_s, jnp.asarray(free_places(), BF16))

    far_outs = far_first.outs(far_first.leave, 3, far_first.modes, BLOCK)
    psi_outs = whole.outs(whole.leave, 6, whole.modes, BLOCK)
    field6 = jax.ShapeDtypeStruct((6, planes, BLOCK), F32)
    *vel_rates, second_h, second_l, second, conform = kernel_call(
        functools.partial(
            momentum_body, near_first, len(second_nodes), far_first, len(far_outs)
        ),
        (*far_outs, *halves(6 - FIRST), field6),
        len(second_nodes) + 9,
        scratch=[
            pltpu.VMEM((planes, 6 * BLOCK), BF16),
            pltpu.VMEM((planes, 6 * BLOCK), BF16),
            pltpu.VMEM((2 * planes, 3 * BLOCK), BF16),
            pltpu.VMEM((2 * planes, 3 * BLOCK), BF16),
            pltpu.VMEM((3, planes, BLOCK), F32),
            pltpu.VMEM((planes, 3 * BLOCK), F32),
        ],
        vmem=24,
        name="momentum",
    )(me, *second_nodes, first, own_flow, halo_flow, high, low, back_high, back_low, both_s, inv_r)
    vel_rates = far_first.packed(vel_rates)
    psi_rates = kernel_call(
        functools.partial(elastic_body, whole),
        (*psi_outs,),
        14,
        scratch=[
            pltpu.VMEM((6, planes, BLOCK), F32),
            pltpu.VMEM((6, planes, 2 * BLOCK), F32),
            pltpu.VMEM((planes, 6 * BLOCK), BF16),
            pltpu.VMEM((planes, 6 * BLOCK), BF16),
            pltpu.VMEM((planes, 6 * BLOCK), F32),
        ],
        vmem=24,
        name="elastic",
    )(
        me, first_h, first_l, second_h, second_l, first, second, conform, own_flow, halo_flow, high, low,
        back_high, back_low, both_s,
    )

    psi_rates = whole.packed(psi_rates)
    if staged:
        vel_rates, psi_rates = barrier((far_swaps(vel_rates), psi_rates))
        vel_rates = near_swaps(turn(vel_rates))
    else:
        vel_rates = in_one(vel_rates)
    psi_rates = in_one(psi_rates)
    wall = jnp.where(device == 0, wall_speed, 0.0)
    at_walls = (me, orientation, wall)
    vel_next = advance(vel_rates, far_first, weights, velocity, *at_walls)
    logc_next = advance(psi_rates, whole, weights, log_conf, *at_walls)
    return vel_next, logc_next


def solution(mesh):
    in_specs = (P("ens", "mode", None), P("ens", "mode", None), P(), P("ens"))
    out_specs = (P("ens", "mode", None), P("ens", "mode", None))
    return jax.shard_map(body, mesh=mesh, in_specs=in_specs, out_specs=out_specs, check_vma=False)
```

```python
import functools

import jax
import jax.numpy as jnp
import ml_dtypes
import numpy as np
from jax import lax
from jax.experimental import pallas as pl
from jax.experimental.pallas import tpu as pltpu
from jax.sharding import PartitionSpec as P

SIDE = 8
CYCLES = 2
RADIAL = SIDE * CYCLES
BLOCK = SIDE * RADIAL
STEP_DT = 0.002
RELAX_TIME = 0.02
MOBILITY = 0.3
LAYER_HEIGHT = 0.25
R_INNER = 1.0
MIB = 1 << 20
F32 = jnp.float32
BF16 = jnp.bfloat16


def split_table(table):
    high = np.asarray(table, np.float32).astype(ml_dtypes.bfloat16)
    low = (np.asarray(table, np.float64) - high.astype(np.float64)).astype(ml_dtypes.bfloat16)
    return high, low


def cheb_table(points):
    nodes_xi = -np.cos(np.pi * np.arange(points) / (points - 1))
    weights = np.ones(points)
    weights[0] = 2.0
    weights[-1] = 2.0
    weights = weights * (-1.0) ** np.arange(points)
    identity = np.eye(points)
    spacing = nodes_xi[:, None] - nodes_xi[None, :] + identity
    matrix = weights[:, None] / weights[None, :] / spacing
    matrix = matrix * (1.0 - identity)
    matrix = matrix - identity * matrix.sum(axis=1)[:, None]
    return nodes_xi, matrix


def fourier_tables(planes):
    phase = np.arange(planes)[:, None] * np.arange(planes // 2)[None, :] % planes
    angles = phase * (2.0 * np.pi / planes)
    cosine = np.cos(angles) * np.sqrt(2.0 / planes)
    sine = np.sin(angles) * np.sqrt(2.0 / planes)
    cosine[:, 0] = planes**-0.5
    sine[:, 0] = (-1.0) ** np.arange(planes) * planes**-0.5
    wavenums = np.arange(planes // 2)
    basis = np.stack([cosine, sine], axis=2).reshape(planes, planes)
    turned = np.stack([-wavenums * sine, wavenums * cosine], axis=2).reshape(planes, planes)
    return np.concatenate([basis, turned], axis=0)


def node_tables():
    nodes_xi, matrix = cheb_table(SIDE)
    radius = R_INNER + (np.arange(CYCLES)[:, None] + (nodes_xi[None, :] + 1.0) / 2.0) / CYCLES
    inv_r = 1.0 / radius.reshape(-1)
    radial_row = np.kron(np.eye(CYCLES), matrix.T * (2.0 * CYCLES))
    radial_mean = np.eye(RADIAL)
    for cycle in range(1, CYCLES):
        low, high = cycle * SIDE - 1, cycle * SIDE
        radial_mean[low : high + 1, low : high + 1] = 0.5
    d_radial = np.kron(np.eye(SIDE), radial_row)
    d_axial = np.kron(matrix.T * (2.0 / LAYER_HEIGHT), np.eye(RADIAL))
    own_weight = np.ones(SIDE)
    own_weight[[0, -1]] = 0.5
    average = np.kron(np.diag(own_weight), radial_mean)
    inv_r_nodes = np.tile(inv_r, SIDE)
    both = np.stack(
        [d_radial, d_axial, d_radial @ average, d_axial @ average, average * inv_r_nodes[None, :]]
    )
    below = np.zeros((SIDE, SIDE))
    below[SIDE - 1, 0] = 0.5
    means = np.stack([np.kron(below, radial_mean), average, np.kron(below.T, radial_mean)])
    faces = np.zeros((3, BLOCK, 2 * BLOCK))
    halos = np.zeros((9, 2 * BLOCK, BLOCK))
    for field in range(3):
        for side, row in ((0, SIDE - 1), (1, 0)):
            at_u = side * BLOCK + field * RADIAL
            at_dz = at_u + 3 * RADIAL
            face_nodes = slice(row * RADIAL, (row + 1) * RADIAL)
            faces[field, face_nodes, at_u : at_u + RADIAL] = np.eye(RADIAL)
            faces[field, :, at_dz : at_dz + RADIAL] = d_axial[:, face_nodes]
            here = SIDE - 1 - row
            out = slice(here * RADIAL, (here + 1) * RADIAL)
            halos[field, at_u : at_u + RADIAL, out] = 0.5 * radial_row @ radial_mean
            halos[3 + field, at_dz : at_dz + RADIAL, out] = 0.5 * radial_mean
            halos[6 + field, at_u : at_u + RADIAL, out] = 0.5 * radial_mean * inv_r[None, :]
    used = 6 * RADIAL
    packed = [faces]
    for number in range(3):
        variant = np.zeros_like(faces)
        for side in (0, BLOCK):
            group = slice(side + number * (BLOCK - used), side + (number + 1) * (BLOCK - used))
            variant[:, :, side + used : side + BLOCK] = faces[:, :, group]
        packed.append(variant)
    return both, np.concatenate(packed), halos, means, inv_r_nodes


def free_places():
    used = 6 * RADIAL
    free = BLOCK - used
    moves = np.zeros((3, BLOCK, BLOCK))
    for number in range(3):
        moves[number, used:, number * free : (number + 1) * free] = np.eye(free)
    return moves


def split(values):
    high = values.astype(BF16)
    return high, (values - high.astype(F32)).astype(BF16)


def dot(left, right):
    return jnp.dot(left, right, preferred_element_type=F32)


def dot3(left, right):
    width = right[0].shape[1]
    if width > BLOCK:
        return dot(left[0], right[0]) + (dot(left[0], right[1]) + dot(left[1], right[0]))
    both = dot(left[0], jnp.concatenate(right, axis=1))
    return both[:, :width] + (both[:, width:] + dot(left[1], right[0]))


def whole_spec():
    return pl.BlockSpec(memory_space=pltpu.VMEM)


def kernel_call(
    body, outs, count, scalars=1, scratch=(), vmem=40, name=None
):
    return pl.pallas_call(
        body,
        out_shape=outs,
        in_specs=[pl.BlockSpec(memory_space=pltpu.SMEM)] * scalars + [whole_spec()] * count,
        out_specs=jax.tree.map(lambda _: whole_spec(), outs),
        scratch_shapes=list(scratch),
        compiler_params=pltpu.CompilerParams(vmem_limit_bytes=vmem * MIB),
        name=name,
    )


def lanes_of(at):
    return slice(at * BLOCK, (at + 1) * BLOCK)


def put(high, low, rows, lanes, value):
    value_h, value_l = split(value)
    high[rows, lanes] = value_h
    low[rows, lanes] = value_l


NEAR = 4


def swap(block, bits):
    devices = lax.axis_size("mode")
    return lax.ppermute(block, "mode", [(i, i ^ bits) for i in range(devices)])


def after(block, token):
    return lax.optimization_barrier((block, token))[0]


def near_swaps(groups):
    return [groups[0]] + [swap(groups[t], t) for t in (1, 2, 3)]


def far_swaps(groups, beside=None):
    first = groups[1] if beside is None else after(groups[1], beside[1])
    return [groups[0], swap(first, NEAR)] + [swap(groups[s], NEAR * s) for s in (2, 3)]


def regroup(groups):
    return [jnp.stack([group[at] for group in groups]) for at in range(NEAR)]


def turn(groups):
    every = [(s, t) for s in range(NEAR) for t in range(NEAR)]

    def body(*refs):
        in_refs, out_refs, sems = refs[:NEAR], refs[NEAR : 2 * NEAR], refs[-1]
        copies = []
        for number, (s, t) in enumerate(every):
            copy = pltpu.make_async_copy(in_refs[t].at[s], out_refs[s].at[t], sems.at[number])
            copy.start()
            copies.append(copy)
        for copy in copies:
            copy.wait()

    return pl.pallas_call(
        body,
        in_specs=[pl.BlockSpec(memory_space=pl.ANY)] * NEAR,
        out_specs=[pl.BlockSpec(memory_space=pl.ANY)] * NEAR,
        out_shape=[jax.ShapeDtypeStruct(group.shape, F32) for group in groups],
        scratch_shapes=[pltpu.SemaphoreType.DMA((len(every),))],
        compiler_params=pltpu.CompilerParams(vmem_limit_bytes=4 * MIB),
        name="turn",
    )(*groups)


class Route:
    def __init__(self, devices, local_modes, far_first, staged=True):
        self.staged = staged and devices == NEAR * NEAR and local_modes % 16 == 0
        self.aligned = self.staged or local_modes % 16 == 0
        self.devices, self.local_modes, self.far_first = devices, local_modes, far_first
        self.modes = local_modes if self.aligned else local_modes * devices
        if not self.staged:
            self.pack = self.land = [(0, at, at) for at in range(devices)]
            self.leave = self.arrive = self.pack if self.aligned else [(0, 0, 0)]
            return
        far = [(s, t, NEAR * s + t) for s in range(NEAR) for t in range(NEAR)]
        near = [(t, s, NEAR * s + t) for s in range(NEAR) for t in range(NEAR)]
        self.pack = self.leave = far if far_first else near
        self.land = self.arrive = near if far_first else far

    def outs(self, blocks, *block):
        arrays, places = (1 + max(entry[at] for entry in blocks) for at in range(2))
        return [jax.ShapeDtypeStruct((places,) + block, F32)] * arrays

    def index(self, me_ref, rel):
        return (me_ref[0] ^ rel) if self.staged else rel

    def rows(self, me_ref, rel):
        start = self.index(me_ref, rel) * self.modes
        return pl.ds(pl.multiple_of(start, self.modes), self.modes)

    def load(self, me_ref, refs, high, low):
        for array, place, rel in self.arrive:
            rows = self.rows(me_ref, rel)
            for field in range(refs[array].shape[1]):
                put(high, low, rows, lanes_of(field), refs[array][place, field])

    def store(self, me_ref, refs, field, coeffs):
        for array, place, rel in self.leave:
            refs[array][place, field] = coeffs[self.rows(me_ref, rel), :]

    def packed(self, arrays):
        if self.aligned:
            return arrays
        _, fields, planes, nodes = arrays[0].shape
        blocks = arrays[0].reshape(fields, planes // self.local_modes, self.local_modes, nodes)
        return [blocks.transpose(1, 0, 2, 3)]

    def unpacked(self, arrays):
        if self.aligned:
            return arrays
        devices, fields, modes, nodes = arrays[0].shape
        return [arrays[0].transpose(1, 0, 2, 3).reshape(1, fields, devices * modes, nodes)]


def in_one(arrays):
    return [lax.all_to_all(arrays[0], "mode", split_axis=0, concat_axis=0, tiled=True)]


def pack(me, values, routes):
    outs, copies = [], []
    for at, (array, route) in enumerate(zip(values, routes)):
        fields, local_modes, _ = array.shape
        copies += [(at, len(outs) + out, place, rel) for out, place, rel in route.pack]
        outs += route.outs(route.pack, fields, local_modes, BLOCK)
    count = len(values)

    def body(me_ref, *refs):
        in_refs, out_refs, sems = refs[:count], refs[count:-1], refs[-1]
        started = []
        for number, (at, out, place, rel) in enumerate(copies):
            layer = routes[at].index(me_ref, rel)
            lanes = pl.ds(pl.multiple_of(layer * BLOCK, BLOCK), BLOCK)
            copy = pltpu.make_async_copy(
                in_refs[at].at[:, :, lanes], out_refs[out].at[place], sems.at[number]
            )
            copy.start()
            started.append(copy)
        for copy in started:
            copy.wait()

    packed = pl.pallas_call(
        body,
        in_specs=[pl.BlockSpec(memory_space=pltpu.SMEM)]
        + [pl.BlockSpec(memory_space=pl.ANY)] * count,
        out_specs=[whole_spec()] * len(outs),
        out_shape=outs,
        scratch_shapes=[pltpu.SemaphoreType.DMA((len(copies),))],
        name="pack",
    )(me, *values)
    first = len(routes[0].outs(routes[0].pack, 1))
    return packed[:first], packed[first:]


def places(orient_ref, layer, shape):
    lane = lax.broadcasted_iota(jnp.int32, shape, 1)
    cycle = lane >> 6
    orient = jnp.where(
        cycle == 0, orient_ref[CYCLES * layer], orient_ref[CYCLES * layer + 1]
    )
    lead, trail = (lane >> 3) & 7, lane & 7
    lead = jnp.where((orient & 1) == 1, SIDE - 1 - lead, lead)
    trail = jnp.where((orient & 2) == 2, SIDE - 1 - trail, trail)
    swapped = (orient & 4) == 4
    row = jnp.where(swapped, trail, lead)
    col = jnp.where(swapped, lead, trail)
    return row * RADIAL + cycle * SIDE + col


def from_grid(orient_ref, layer):
    shape = (BLOCK, BLOCK)
    grid_ids = lax.broadcasted_iota(jnp.int32, shape, 0)
    return (grid_ids == places(orient_ref, layer, shape)).astype(F32)


def order_body(
    me_ref, orient_ref, both_ref, faces_ref, halos_ref, inv_r_ref,
    both_out, faces_out, halos_out, inv_r_out,
):
    onto = from_grid(orient_ref, me_ref[0])
    inv_r_out[...] = jnp.broadcast_to(
        jnp.sum(onto * inv_r_ref[...], axis=0, keepdims=True), inv_r_out.shape
    )
    back = onto.T.astype(BF16)
    onto = onto.astype(BF16)
    for at in range(both_ref.shape[0]):
        moved = dot(both_ref[at], onto).astype(BF16)
        both_out[at] = dot(back, moved).astype(BF16)
    for at in range(faces_ref.shape[0]):
        faces_out[at] = dot(back, faces_ref[at]).astype(BF16)
    pairs = ((0, 3), (1, 4), (2, 5), (6, 7), (8, 8))
    for at, pair in enumerate(pairs):
        for half in range(2):
            for side in range(2):
                placed = dot(halos_ref[2 * pair[side] + half], onto).astype(BF16)
                halos_out[2 * at + half, :, side * BLOCK : (side + 1) * BLOCK] = placed


def weights_body(layers, orient_ref, means_ref, out_ref):
    def one(index, carry):
        onto = from_grid(orient_ref, index).astype(BF16)
        below = lax.rem(index + (layers - 1), layers)
        above = lax.rem(index + 1, layers)
        for number, layer in enumerate((below, index, above)):
            back = from_grid(orient_ref, layer).T.astype(BF16)
            moved = dot(means_ref[number], onto).astype(BF16)
            out_ref[index, number * BLOCK : (number + 1) * BLOCK, :] = dot(back, moved).astype(BF16)
        return carry

    lax.fori_loop(0, layers, one, 0)


def face_body(route, count, me_ref, *refs):
    vel_refs, (faces_ref, up_ref, down_ref, high, low) = refs[:count], refs[count:]
    route.load(me_ref, vel_refs, high, low)
    quarter = high.shape[0] // 4

    def faces(rows, variant):
        total = None
        for field in range(3):
            lanes, at = lanes_of(field), 6 * variant + 2 * field
            part = dot3((high[rows, lanes], low[rows, lanes]), (faces_ref[at], faces_ref[at + 1]))
            total = part if total is None else total + part
        return total

    for number in range(3):
        rows = slice(number * quarter, (number + 1) * quarter)
        total = faces(rows, 0) + faces(slice(3 * quarter, 4 * quarter), 1 + number)
        up_ref[rows, :] = total[:, :BLOCK]
        down_ref[rows, :] = total[:, BLOCK:]


FIRST = 3


def members_of(first_ref, second_ref, rows):
    return [ref[at, rows, :] for ref in (first_ref, second_ref) for at in range(ref.shape[0])]


def transform(high_ref, low_ref, rows, coef_h, coef_l, out_ref):
    table = (high_ref[rows, :], low_ref[rows, :])
    fields = out_ref.shape[0]
    for start in range(0, fields, 2):
        stop = min(start + 2, fields)
        lanes = slice(start * BLOCK, stop * BLOCK)
        values = dot3(table, (coef_h[:, lanes], coef_l[:, lanes]))
        for at in range(start, stop):
            out_ref[at] = values[:, lanes_of(at - start)]


def flow_parts(g_r, g_t, g_z, u):
    return (
        0.5 * (g_t[0] - g_r[1]),
        0.5 * (g_z[0] - g_r[2]),
        0.5 * (g_z[1] - g_t[2]),
        2.0 * g_r[0],
        g_t[0] + g_r[1],
        g_z[0] + g_r[2],
        2.0 * g_t[1],
        g_z[1] + g_t[2],
        2.0 * g_z[2],
        -(g_r[0] * u[0] + g_t[0] * u[1] + g_z[0] * u[2]),
        -(g_r[1] * u[0] + g_t[1] * u[1] + g_z[1] * u[2]),
        -(g_r[2] * u[0] + g_t[2] * u[1] + g_z[2] * u[2]),
    )


def matrix_of(ref, at):
    return ref[2 * at], ref[2 * at + 1]


def velocity_body(route, count, me_ref, *refs):
    psi_refs, refs = refs[:count], refs[count:]
    vel_h, vel_l, high_ref, low_ref, both_ref, inv_r_ref, vel_ref, flow_ref = refs[:8]
    coef_h, coef_l, psi_out, values = refs[8:]
    planes = high_ref.shape[1]
    route.load(me_ref, psi_refs, coef_h, coef_l)
    transform(high_ref, low_ref, slice(0, planes), coef_h, coef_l, psi_out)
    table = (high_ref[...], low_ref[...])
    values[:, 0:256] = dot3(table, (vel_h[:, 0:256], vel_l[:, 0:256]))
    values[:, 256:384] = dot3(table, (vel_h[:, 256:384], vel_l[:, 256:384]))
    rows_step = 128

    def chunk(start):
        rows = pl.ds(start, rows_step)
        turned = pl.ds(pl.multiple_of(planes + start, rows_step), rows_step)
        u = [values[rows, lanes_of(f)] for f in range(3)]
        u_s = [split(v) for v in u]
        dth_s = [split(values[turned, lanes_of(f)]) for f in range(3)]
        g_r = [dot3(u_s[f], matrix_of(both_ref, 2)) for f in range(3)]
        g_z = [dot3(u_s[f], matrix_of(both_ref, 3)) for f in range(3)]
        g_t = [dot3(dth_s[f], matrix_of(both_ref, 4)) for f in range(3)]
        g_t[0] = g_t[0] - dot3(u_s[1], matrix_of(both_ref, 4))
        g_t[1] = g_t[1] + dot3(u_s[0], matrix_of(both_ref, 4))
        hoop_rate = u[1] * inv_r_ref[0:1, :]
        parts = flow_parts(g_r, g_t, g_z, u)
        rest = (1.0 - 2.0 * MOBILITY) / RELAX_TIME
        for f in range(3):
            vel_ref[f, rows, :] = u[f]
        for at, part in enumerate((u[0], hoop_rate, u[2]) + parts):
            if at == 3:
                part = part + hoop_rate
            if at - 6 in DIAGONAL:
                part = part - rest
            flow_ref[at, rows, :] = part

    row_chunks(planes, rows_step, chunk)


def halo_body(
    below_ref, above_ref, vel_ref, high_ref, low_ref, halos_ref, places_ref, part_ref, values
):
    planes = high_ref.shape[1]
    quarter = planes // 4
    edges = []
    for ref in (below_ref, above_ref):
        last = None
        for number in range(3):
            part = split(ref[number * quarter : (number + 1) * quarter, :])
            part = dot(part[0], places_ref[number]) + dot(part[1], places_ref[number])
            last = part if last is None else last + part
        edges.append(jnp.concatenate([ref[...], last], axis=0))
    values[...] = dot3((high_ref[...], low_ref[...]), split(jnp.concatenate(edges, axis=1)))
    rows_step = planes // 2

    def chunk(start):
        rows = pl.ds(start, rows_step)
        turned = pl.ds(pl.multiple_of(planes + start, rows_step), rows_step)
        edge, edge_dth = split(values[rows, :]), split(values[turned, :])
        g_r, g_z = zip(*(halved(dot3(edge, matrix_of(halos_ref, f))) for f in range(3)))
        g_t = [
            *halved(dot3(edge_dth, matrix_of(halos_ref, 3))),
            dot3(edge_dth, (halos_ref[8, :, :BLOCK], halos_ref[9, :, :BLOCK])),
        ]
        mean_r, mean_t = halved(dot3(edge, matrix_of(halos_ref, 3)))
        g_t[0] = g_t[0] - mean_t
        g_t[1] = g_t[1] + mean_r
        u = [vel_ref[f, rows, :] for f in range(3)]
        for at, part in enumerate(flow_parts(g_r, g_t, g_z, u)):
            part_ref[at, rows, :] = part

    row_chunks(planes, rows_step, chunk)


def halved(pair):
    return pair[:, :BLOCK], pair[:, BLOCK:]


def square(m):
    a, b, c, d, e, f = m
    bb, cc, ee = b * b, c * c, e * e
    return (
        a * a + (bb + cc),
        b * (a + d) + c * e,
        c * (a + f) + b * e,
        d * d + (bb + ee),
        e * (d + f) + b * c,
        f * f + (cc + ee),
    )


def commuting_product(m, n):
    a, b, c, d, e, f = m
    p, q, r, s, t, u = n
    return (
        a * p + b * q + c * r,
        a * q + b * s + c * t,
        a * r + b * t + c * u,
        b * q + d * s + e * t,
        b * r + d * t + e * u,
        c * r + e * t + f * u,
    )


DIAGONAL = (0, 3, 5)


def plus_identity(m):
    return tuple(v + 1.0 if at in DIAGONAL else v for at, v in enumerate(m))


def exponential(psi, sign):
    x = tuple(v * (sign * 0.125) for v in psi)
    x2 = square(x)
    x4 = square(x2)
    even = plus_identity(tuple(v * 0.5 + w * (1.0 / 24.0) for v, w in zip(x2, x4)))
    odd = commuting_product(x, plus_identity(tuple(v * (1.0 / 6.0) for v in x2)))
    total = tuple(v + w for v, w in zip(even, odd))
    for _ in range(3):
        total = square(total)
    return total


def row_chunks(planes, rows_step, body):
    def chunk(step, carry):
        body(pl.multiple_of(step * rows_step, rows_step))
        return carry

    lax.fori_loop(0, planes // rows_step, chunk, 0)


def momentum_body(route, count, out_route, out_count, me_ref, *refs):
    psi_refs, refs = refs[:count], refs[count:]
    first_ref, flow_ref, halo_ref, high_ref, low_ref = refs[:5]
    back_high_ref, back_low_ref, both_ref, inv_r_ref = refs[5:9]
    out_refs, refs = refs[9 : 9 + out_count], refs[9 + out_count :]
    coef_h, coef_l, psi_out, conform_out, stress_h, stress_l, vel_h, vel_l, mom_s, coeffs = refs
    planes = high_ref.shape[1]
    route.load(me_ref, psi_refs, coef_h, coef_l)
    transform(high_ref, low_ref, slice(0, planes), coef_h, coef_l, psi_out)
    rows_step = 16

    def chunk(start):
        rows = pl.ds(start, rows_step)
        inv_r = inv_r_ref[0:1, :]
        psi = members_of(first_ref, psi_out, rows)
        conform = exponential(psi, 1.0)
        for member in range(6):
            conform_out[member, rows, :] = conform[member]
        stress = tuple(v - 1.0 if at in DIAGONAL else v for at, v in enumerate(conform))
        for lane, member in enumerate((0, 2, 1, 4, 2, 5)):
            put(stress_h, stress_l, rows, lanes_of(lane), stress[member])
        hoop = tuple(stress[at] * inv_r for at in (1, 3, 4))
        turned = pl.ds(pl.multiple_of(planes + start, rows_step), rows_step)
        for at in range(3):
            put(vel_h, vel_l, turned, lanes_of(at), -hoop[at])
        carried = [flow_ref[12 + at, rows, :] + halo_ref[9 + at, rows, :] for at in range(3)]
        mom_s[0, rows, :] = carried[0] + (stress[0] * inv_r - hoop[1])
        mom_s[1, rows, :] = carried[1] + 2.0 * hoop[0]
        mom_s[2, rows, :] = carried[2] + stress[2] * inv_r

    row_chunks(planes, rows_step, chunk)
    divergence = tuple(
        jnp.concatenate([both_ref[at], both_ref[2 + at]], axis=0) for at in range(2)
    )
    for at in range(3):
        lanes = slice(2 * at * BLOCK, (2 * at + 2) * BLOCK)
        force = dot3((stress_h[:, lanes], stress_l[:, lanes]), divergence)
        put(vel_h, vel_l, slice(0, planes), lanes_of(at), mom_s[at] + force)
    back = (back_high_ref[...], back_low_ref[...])
    for start, stop in ((0, 2), (2, 3)):
        lanes = slice(start * BLOCK, stop * BLOCK)
        coeffs[:, lanes] = dot3(back, (vel_h[:, lanes], vel_l[:, lanes]))
    for field in range(3):
        out_route.store(me_ref, out_refs, field, coeffs.at[:, lanes_of(field)])


def elastic_body(route, me_ref, *refs):
    (
        first_h, first_l, second_h, second_l, first_ref, second_ref, conform_ref, flow_ref,
        halo_ref, high_ref, low_ref, back_high_ref, back_low_ref, both_ref,
    ) = refs[:14]
    out_ref, dth_s, grad_s, rate_h, rate_l, coeffs = refs[14:]
    planes = high_ref.shape[1]
    turned = slice(planes, 2 * planes)
    transform(high_ref, low_ref, turned, first_h, first_l, dth_s.at[pl.ds(0, FIRST)])
    transform(high_ref, low_ref, turned, second_h, second_l, dth_s.at[pl.ds(FIRST, 6 - FIRST)])
    gradient = tuple(
        jnp.concatenate([both_ref[at], both_ref[2 + at]], axis=1) for at in range(2)
    )
    for member in range(6):
        psi_ref = first_ref if member < FIRST else second_ref
        grad_s[member] = dot3(split(psi_ref[member % FIRST]), gradient)
    rows_step = 16
    inv_relax = 1.0 / RELAX_TIME

    def chunk(start):
        rows = pl.ds(start, rows_step)
        psi = members_of(first_ref, second_ref, rows)
        inverse = exponential(psi, -1.0)
        u_r, hoop_rate, u_z = (flow_ref[at, rows, :] for at in range(3))
        p, q, s, *strain = (
            flow_ref[3 + at, rows, :] + halo_ref[at, rows, :] for at in range(9)
        )
        a, b, c, d, e, f = psi
        pb, qc, se = p * b, q * c, s * e
        turning = (
            2.0 * (pb + qc),
            p * (d - a) + (q * e + s * c),
            q * (f - a) + (p * e - s * b),
            2.0 * (se - pb),
            s * (f - d) - (p * c + q * b),
            -2.0 * (qc + se),
        )
        for member in range(6):
            advect = (
                u_r * grad_s[member, rows, 0:BLOCK]
                + hoop_rate * dth_s[member, rows, :]
                + u_z * grad_s[member, rows, BLOCK : 2 * BLOCK]
            )
            relaxing = ((1.0 - MOBILITY) * inv_relax) * inverse[member] - (
                MOBILITY * inv_relax
            ) * conform_ref[member, rows, :]
            rate = (turning[member] - advect) + (strain[member] + relaxing)
            put(rate_h, rate_l, rows, lanes_of(member), rate)

    row_chunks(planes, rows_step, chunk)
    back = (back_high_ref[:, :planes], back_low_ref[:, :planes])
    for pair in range(3):
        lanes = slice(2 * pair * BLOCK, (2 * pair + 2) * BLOCK)
        coeffs[:, lanes] = dot3(back, (rate_h[:, lanes], rate_l[:, lanes]))
    for field in range(6):
        route.store(me_ref, [out_ref], field, coeffs.at[:, lanes_of(field)])


def advance_body(layers, step, route, count, *refs):
    me_ref, orient_ref, wall_ref = refs[:3]
    rate_refs, (mean_ref, old_ref, out_ref, rates) = refs[3 : 3 + count], refs[3 + count :]
    fields, local_modes = old_ref.shape[0], old_ref.shape[1]

    @pl.when(pl.program_id(0) == 0)
    def _():
        for array, place, rel in route.land:
            rates[route.index(me_ref, rel)] = rate_refs[array][place]

    first = pl.program_id(0) * step
    merged = local_modes % 8 == 0

    def averaged(index, at, field):
        below = lax.rem(index + (layers - 1), layers)
        above = lax.rem(index + 1, layers)
        total = None
        for number, layer in enumerate((below, index, above)):
            block = rates[layer] if field is None else rates[layer, field]
            high, low = split(block.reshape(-1, BLOCK))
            weights = mean_ref[at, number * BLOCK : (number + 1) * BLOCK, :]
            part = dot(high, weights) + dot(low, weights)
            total = part if total is None else total + part
        return total

    for at in range(step):
        index = first + at
        lanes = lanes_of(at)
        if merged:
            every = averaged(index, at, None)
            change = [every[f * local_modes : (f + 1) * local_modes] for f in range(fields)]
        else:
            change = [averaged(index, at, f) for f in range(fields)]
        shape = (local_modes, BLOCK)
        column = places(orient_ref, index, shape) & (RADIAL - 1)
        inner = column == 0
        on_wall = jnp.logical_or(inner, column == RADIAL - 1)
        mean_row = jnp.logical_and(lax.broadcasted_iota(jnp.int32, shape, 0) == 0, inner)
        driven = jnp.where(mean_row, wall_ref[0], 0.0)
        for field in range(fields):
            stepped = old_ref[field, :, lanes] + STEP_DT * change[field]
            if fields == 3:
                stepped = jnp.where(on_wall, driven if field == 1 else 0.0, stepped)
            out_ref[field, :, lanes] = stepped


def advance(rates, route, weights, old, me, orientation, wall):
    fields, local_modes, nodes = old.shape
    layers = nodes // BLOCK
    step = 4
    block = pl.BlockSpec((fields, local_modes, step * BLOCK), lambda i: (0, 0, i))
    scalar = pl.BlockSpec(memory_space=pltpu.SMEM)
    return pl.pallas_call(
        functools.partial(advance_body, layers, step, route, len(rates)),
        grid=(layers // step,),
        in_specs=[scalar] * 3
        + [pl.BlockSpec(part.shape, lambda i: (0, 0, 0, 0)) for part in rates]
        + [pl.BlockSpec((step, 3 * BLOCK, BLOCK), lambda i: (i, 0, 0)), block],
        out_specs=block,
        out_shape=jax.ShapeDtypeStruct(old.shape, F32),
        scratch_shapes=[pltpu.VMEM((layers, fields, local_modes, BLOCK), F32)],
        compiler_params=pltpu.CompilerParams(vmem_limit_bytes=24 * MIB),
        name="advance",
    )(me, orientation, wall, *rates, weights, old)


def body(velocity, log_conf, orientation, wall_speed):
    devices = lax.axis_size("mode")
    device = lax.axis_index("mode").astype(jnp.int32)
    me = device.reshape(1)
    local_modes = velocity.shape[1]
    layers = velocity.shape[2] // BLOCK
    planes = local_modes * devices
    far_first = Route(devices, local_modes, True)
    near_first = Route(devices, local_modes, False)
    whole = Route(devices, local_modes, False, False)
    barrier = lax.optimization_barrier
    staged = far_first.staged
    both, faces, halos, means, inv_r_nodes = node_tables()

    def parts(tables):
        return jnp.asarray(np.stack([half for table in tables for half in split_table(table)]))

    fourier = fourier_tables(planes)
    high, low = (jnp.asarray(half) for half in split_table(fourier))
    back_high, back_low = (jnp.asarray(half) for half in split_table(fourier.T))
    inv_r_table = jnp.asarray(np.tile(inv_r_nodes[:, None], (1, BLOCK)), F32)

    both_s, faces_s, halos_s, inv_r = kernel_call(
        order_body,
        (
            jax.ShapeDtypeStruct((10, BLOCK, BLOCK), BF16),
            jax.ShapeDtypeStruct((24, BLOCK, 2 * BLOCK), BF16),
            jax.ShapeDtypeStruct((10, 2 * BLOCK, 2 * BLOCK), BF16),
            jax.ShapeDtypeStruct((8, BLOCK), F32),
        ),
        4,
        scalars=2,
        vmem=16,
        name="order",
    )(me, orientation, parts(both), parts(faces), parts(halos), inv_r_table)
    weights = kernel_call(
        functools.partial(weights_body, layers),
        jax.ShapeDtypeStruct((layers, 3 * BLOCK, BLOCK), BF16),
        1,
        vmem=8 + layers // 8,
        name="weights",
    )(orientation, jnp.asarray(means, BF16))

    vel_nodes, psi_nodes = pack(me, (velocity, log_conf), (far_first, near_first))
    fixed = (both_s, faces_s, halos_s, inv_r, weights)
    if staged:
        psi_nodes = near_swaps(psi_nodes)
        vel_nodes = far_swaps(vel_nodes, psi_nodes)
        vel_nodes, psi_nodes, fixed = barrier((vel_nodes, psi_nodes, fixed))
        vel_nodes = near_swaps(regroup(vel_nodes))
        first_nodes = far_swaps(regroup([group[:, :FIRST] for group in psi_nodes]))
        second_nodes = regroup([group[:, FIRST:] for group in psi_nodes])
    else:
        vel_nodes = far_first.unpacked(in_one(vel_nodes))
        psi_nodes = near_first.unpacked(in_one(psi_nodes))
        first_nodes = [group[:, :FIRST] for group in psi_nodes]
        second_nodes = [group[:, FIRST:] for group in psi_nodes]

    both_s, faces_s, halos_s, inv_r, weights = fixed
    edge = jax.ShapeDtypeStruct((planes // 4 * 3, BLOCK), F32)
    vel_half = jax.ShapeDtypeStruct((planes, 3 * BLOCK), BF16)
    to_up, to_down, vel_h, vel_l = kernel_call(
        functools.partial(face_body, far_first, len(vel_nodes)),
        (edge, edge, vel_half, vel_half),
        len(vel_nodes) + 1,
        vmem=16,
        name="faces",
    )(me, *vel_nodes, faces_s)
    up = [(i, (i + 1) % devices) for i in range(devices)]
    below = lax.ppermute(to_up, "mode", up)
    above = lax.ppermute(to_down, "mode", [(j, i) for i, j in up])

    def halves(fields):
        return (
            jax.ShapeDtypeStruct((planes, fields * BLOCK), BF16),
            jax.ShapeDtypeStruct((planes, fields * BLOCK), BF16),
            jax.ShapeDtypeStruct((fields, planes, BLOCK), F32),
        )

    vel, own_flow, first_h, first_l, first = kernel_call(
        functools.partial(velocity_body, near_first, len(first_nodes)),
        (
            jax.ShapeDtypeStruct((3, planes, BLOCK), F32),
            jax.ShapeDtypeStruct((15, planes, BLOCK), F32),
            *halves(FIRST),
        ),
        len(first_nodes) + 6,
        scratch=[pltpu.VMEM((2 * planes, 3 * BLOCK), F32)],
        vmem=20,
        name="velocity",
    )(me, *first_nodes, vel_h, vel_l, high, low, both_s, inv_r)
    if staged:
        early = second_nodes
        second_nodes, below, above, vel = barrier((second_nodes, below, above, vel))
        second_nodes = far_swaps([early[0], second_nodes[1], early[2], early[3]])
    halo_flow = kernel_call(
        halo_body,
        jax.ShapeDtypeStruct((12, planes, BLOCK), F32),
        7,
        scalars=0,
        scratch=[pltpu.VMEM((2 * planes, 2 * BLOCK), F32)],
        vmem=24,
        name="halo",
    )(below, above, vel, high, low, halos_s, jnp.asarray(free_places(), BF16))

    far_outs = far_first.outs(far_first.leave, 3, far_first.modes, BLOCK)
    psi_outs = whole.outs(whole.leave, 6, whole.modes, BLOCK)
    field6 = jax.ShapeDtypeStruct((6, planes, BLOCK), F32)
    *vel_rates, second_h, second_l, second, conform = kernel_call(
        functools.partial(
            momentum_body, near_first, len(second_nodes), far_first, len(far_outs)
        ),
        (*far_outs, *halves(6 - FIRST), field6),
        len(second_nodes) + 9,
        scratch=[
            pltpu.VMEM((planes, 6 * BLOCK), BF16),
            pltpu.VMEM((planes, 6 * BLOCK), BF16),
            pltpu.VMEM((2 * planes, 3 * BLOCK), BF16),
            pltpu.VMEM((2 * planes, 3 * BLOCK), BF16),
            pltpu.VMEM((3, planes, BLOCK), F32),
            pltpu.VMEM((planes, 3 * BLOCK), F32),
        ],
        vmem=24,
        name="momentum",
    )(me, *second_nodes, first, own_flow, halo_flow, high, low, back_high, back_low, both_s, inv_r)
    vel_rates = far_first.packed(vel_rates)
    psi_rates = kernel_call(
        functools.partial(elastic_body, whole),
        (*psi_outs,),
        14,
        scratch=[
            pltpu.VMEM((6, planes, BLOCK), F32),
            pltpu.VMEM((6, planes, 2 * BLOCK), F32),
            pltpu.VMEM((planes, 6 * BLOCK), BF16),
            pltpu.VMEM((planes, 6 * BLOCK), BF16),
            pltpu.VMEM((planes, 6 * BLOCK), F32),
        ],
        vmem=24,
        name="elastic",
    )(
        me, first_h, first_l, second_h, second_l, first, second, conform, own_flow, halo_flow, high, low,
        back_high, back_low, both_s,
    )

    psi_rates = whole.packed(psi_rates)
    if staged:
        vel_rates, psi_rates = barrier((far_swaps(vel_rates), psi_rates))
        vel_rates = near_swaps(turn(vel_rates))
    else:
        vel_rates = in_one(vel_rates)
    psi_rates = in_one(psi_rates)
    wall = jnp.where(device == 0, wall_speed, 0.0)
    at_walls = (me, orientation, wall)
    vel_next = advance(vel_rates, far_first, weights, velocity, *at_walls)
    logc_next = advance(psi_rates, whole, weights, log_conf, *at_walls)
    return vel_next, logc_next


def solution(mesh):
    in_specs = (P("ens", "mode", None), P("ens", "mode", None), P(), P("ens"))
    out_specs = (P("ens", "mode", None), P("ens", "mode", None))
    return jax.shard_map(body, mesh=mesh, in_specs=in_specs, out_specs=out_specs, check_vma=False)
```

```python
import functools

import jax
import jax.numpy as jnp
import ml_dtypes
import numpy as np
from jax import lax
from jax.experimental import pallas as pl
from jax.experimental.pallas import tpu as pltpu
from jax.sharding import PartitionSpec as P

SIDE = 8
CYCLES = 2
RADIAL = SIDE * CYCLES
BLOCK = SIDE * RADIAL
STEP_DT = 0.002
RELAX_TIME = 0.02
MOBILITY = 0.3
LAYER_HEIGHT = 0.25
R_INNER = 1.0
MIB = 1 << 20
F32 = jnp.float32
BF16 = jnp.bfloat16


def split_table(table):
    high = np.asarray(table, np.float32).astype(ml_dtypes.bfloat16)
    low = (np.asarray(table, np.float64) - high.astype(np.float64)).astype(ml_dtypes.bfloat16)
    return high, low


def cheb_table(points):
    nodes_xi = -np.cos(np.pi * np.arange(points) / (points - 1))
    weights = np.ones(points)
    weights[0] = 2.0
    weights[-1] = 2.0
    weights = weights * (-1.0) ** np.arange(points)
    identity = np.eye(points)
    spacing = nodes_xi[:, None] - nodes_xi[None, :] + identity
    matrix = weights[:, None] / weights[None, :] / spacing
    matrix = matrix * (1.0 - identity)
    matrix = matrix - identity * matrix.sum(axis=1)[:, None]
    return nodes_xi, matrix


def fourier_tables(planes):
    phase = np.arange(planes)[:, None] * np.arange(planes // 2)[None, :] % planes
    angles = phase * (2.0 * np.pi / planes)
    cosine = np.cos(angles) * np.sqrt(2.0 / planes)
    sine = np.sin(angles) * np.sqrt(2.0 / planes)
    cosine[:, 0] = planes**-0.5
    sine[:, 0] = (-1.0) ** np.arange(planes) * planes**-0.5
    wavenums = np.arange(planes // 2)
    basis = np.stack([cosine, sine], axis=2).reshape(planes, planes)
    turned = np.stack([-wavenums * sine, wavenums * cosine], axis=2).reshape(planes, planes)
    return np.concatenate([basis, turned], axis=0)


def node_tables():
    nodes_xi, matrix = cheb_table(SIDE)
    radius = R_INNER + (np.arange(CYCLES)[:, None] + (nodes_xi[None, :] + 1.0) / 2.0) / CYCLES
    inv_r = 1.0 / radius.reshape(-1)
    radial_row = np.kron(np.eye(CYCLES), matrix.T * (2.0 * CYCLES))
    radial_mean = np.eye(RADIAL)
    for cycle in range(1, CYCLES):
        low, high = cycle * SIDE - 1, cycle * SIDE
        radial_mean[low : high + 1, low : high + 1] = 0.5
    d_radial = np.kron(np.eye(SIDE), radial_row)
    d_axial = np.kron(matrix.T * (2.0 / LAYER_HEIGHT), np.eye(RADIAL))
    own_weight = np.ones(SIDE)
    own_weight[[0, -1]] = 0.5
    average = np.kron(np.diag(own_weight), radial_mean)
    inv_r_nodes = np.tile(inv_r, SIDE)
    both = np.stack(
        [d_radial, d_axial, d_radial @ average, d_axial @ average, average * inv_r_nodes[None, :]]
    )
    below = np.zeros((SIDE, SIDE))
    below[SIDE - 1, 0] = 0.5
    means = np.stack([np.kron(below, radial_mean), average, np.kron(below.T, radial_mean)])
    faces = np.zeros((3, BLOCK, 2 * BLOCK))
    halos = np.zeros((9, 2 * BLOCK, BLOCK))
    for field in range(3):
        for side, row in ((0, SIDE - 1), (1, 0)):
            at_u = side * BLOCK + field * RADIAL
            at_dz = at_u + 3 * RADIAL
            face_nodes = slice(row * RADIAL, (row + 1) * RADIAL)
            faces[field, face_nodes, at_u : at_u + RADIAL] = np.eye(RADIAL)
            faces[field, :, at_dz : at_dz + RADIAL] = d_axial[:, face_nodes]
            here = SIDE - 1 - row
            out = slice(here * RADIAL, (here + 1) * RADIAL)
            halos[field, at_u : at_u + RADIAL, out] = 0.5 * radial_row @ radial_mean
            halos[3 + field, at_dz : at_dz + RADIAL, out] = 0.5 * radial_mean
            halos[6 + field, at_u : at_u + RADIAL, out] = 0.5 * radial_mean * inv_r[None, :]
    used = 6 * RADIAL
    packed = [faces]
    for number in range(3):
        variant = np.zeros_like(faces)
        for side in (0, BLOCK):
            group = slice(side + number * (BLOCK - used), side + (number + 1) * (BLOCK - used))
            variant[:, :, side + used : side + BLOCK] = faces[:, :, group]
        packed.append(variant)
    return both, np.concatenate(packed), halos, means, inv_r_nodes


def free_places():
    used = 6 * RADIAL
    free = BLOCK - used
    moves = np.zeros((3, BLOCK, BLOCK))
    for number in range(3):
        moves[number, used:, number * free : (number + 1) * free] = np.eye(free)
    return moves


def split(values):
    high = values.astype(BF16)
    return high, (values - high.astype(F32)).astype(BF16)


def dot(left, right):
    return jnp.dot(left, right, preferred_element_type=F32)


def dot3(left, right):
    width = right[0].shape[1]
    if width > BLOCK:
        return dot(left[0], right[0]) + (dot(left[0], right[1]) + dot(left[1], right[0]))
    both = dot(left[0], jnp.concatenate(right, axis=1))
    return both[:, :width] + (both[:, width:] + dot(left[1], right[0]))


def whole_spec():
    return pl.BlockSpec(memory_space=pltpu.VMEM)


def kernel_call(
    body, outs, count, scalars=1, scratch=(), vmem=40, name=None
):
    return pl.pallas_call(
        body,
        out_shape=outs,
        in_specs=[pl.BlockSpec(memory_space=pltpu.SMEM)] * scalars + [whole_spec()] * count,
        out_specs=jax.tree.map(lambda _: whole_spec(), outs),
        scratch_shapes=list(scratch),
        compiler_params=pltpu.CompilerParams(vmem_limit_bytes=vmem * MIB),
        name=name,
    )


def lanes_of(at):
    return slice(at * BLOCK, (at + 1) * BLOCK)


def put(high, low, rows, lanes, value):
    value_h, value_l = split(value)
    high[rows, lanes] = value_h
    low[rows, lanes] = value_l


NEAR = 4


def swap(block, bits):
    devices = lax.axis_size("mode")
    return lax.ppermute(block, "mode", [(i, i ^ bits) for i in range(devices)])


def after(block, token):
    return lax.optimization_barrier((block, token))[0]


def near_swaps(groups):
    return [groups[0]] + [swap(groups[t], t) for t in (1, 2, 3)]


def far_swaps(groups, beside=None):
    first = groups[1] if beside is None else after(groups[1], beside[1])
    return [groups[0], swap(first, NEAR)] + [swap(groups[s], NEAR * s) for s in (2, 3)]


def regroup(groups):
    return [jnp.stack([group[at] for group in groups]) for at in range(NEAR)]


def turn(groups):
    every = [(s, t) for s in range(NEAR) for t in range(NEAR)]

    def body(*refs):
        in_refs, out_refs, sems = refs[:NEAR], refs[NEAR : 2 * NEAR], refs[-1]
        copies = []
        for number, (s, t) in enumerate(every):
            copy = pltpu.make_async_copy(in_refs[t].at[s], out_refs[s].at[t], sems.at[number])
            copy.start()
            copies.append(copy)
        for copy in copies:
            copy.wait()

    return pl.pallas_call(
        body,
        in_specs=[pl.BlockSpec(memory_space=pl.ANY)] * NEAR,
        out_specs=[pl.BlockSpec(memory_space=pl.ANY)] * NEAR,
        out_shape=[jax.ShapeDtypeStruct(group.shape, F32) for group in groups],
        scratch_shapes=[pltpu.SemaphoreType.DMA((len(every),))],
        compiler_params=pltpu.CompilerParams(vmem_limit_bytes=4 * MIB),
        name="turn",
    )(*groups)


class Route:
    def __init__(self, devices, local_modes, far_first, staged=True):
        self.staged = staged and devices == NEAR * NEAR and local_modes % 16 == 0
        self.aligned = self.staged or local_modes % 16 == 0
        self.devices, self.local_modes, self.far_first = devices, local_modes, far_first
        self.modes = local_modes if self.aligned else local_modes * devices
        if not self.staged:
            self.pack = self.land = [(0, at, at) for at in range(devices)]
            self.leave = self.arrive = self.pack if self.aligned else [(0, 0, 0)]
            return
        far = [(s, t, NEAR * s + t) for s in range(NEAR) for t in range(NEAR)]
        near = [(t, s, NEAR * s + t) for s in range(NEAR) for t in range(NEAR)]
        self.pack = self.leave = far if far_first else near
        self.land = self.arrive = near if far_first else far

    def outs(self, blocks, *block):
        arrays, places = (1 + max(entry[at] for entry in blocks) for at in range(2))
        return [jax.ShapeDtypeStruct((places,) + block, F32)] * arrays

    def index(self, me_ref, rel):
        return (me_ref[0] ^ rel) if self.staged else rel

    def rows(self, me_ref, rel):
        start = self.index(me_ref, rel) * self.modes
        return pl.ds(pl.multiple_of(start, self.modes), self.modes)

    def load(self, me_ref, refs, high, low):
        for array, place, rel in self.arrive:
            rows = self.rows(me_ref, rel)
            for field in range(refs[array].shape[1]):
                put(high, low, rows, lanes_of(field), refs[array][place, field])

    def store(self, me_ref, refs, field, coeffs):
        for array, place, rel in self.leave:
            refs[array][place, field] = coeffs[self.rows(me_ref, rel), :]

    def packed(self, arrays):
        if self.aligned:
            return arrays
        _, fields, planes, nodes = arrays[0].shape
        blocks = arrays[0].reshape(fields, planes // self.local_modes, self.local_modes, nodes)
        return [blocks.transpose(1, 0, 2, 3)]

    def unpacked(self, arrays):
        if self.aligned:
            return arrays
        devices, fields, modes, nodes = arrays[0].shape
        return [arrays[0].transpose(1, 0, 2, 3).reshape(1, fields, devices * modes, nodes)]


def in_one(arrays):
    return [lax.all_to_all(arrays[0], "mode", split_axis=0, concat_axis=0, tiled=True)]


def pack(me, values, routes):
    outs, copies = [], []
    for at, (array, route) in enumerate(zip(values, routes)):
        fields, local_modes, _ = array.shape
        copies += [(at, len(outs) + out, place, rel) for out, place, rel in route.pack]
        outs += route.outs(route.pack, fields, local_modes, BLOCK)
    count = len(values)

    def body(me_ref, *refs):
        in_refs, out_refs, sems = refs[:count], refs[count:-1], refs[-1]
        started = []
        for number, (at, out, place, rel) in enumerate(copies):
            layer = routes[at].index(me_ref, rel)
            lanes = pl.ds(pl.multiple_of(layer * BLOCK, BLOCK), BLOCK)
            copy = pltpu.make_async_copy(
                in_refs[at].at[:, :, lanes], out_refs[out].at[place], sems.at[number]
            )
            copy.start()
            started.append(copy)
        for copy in started:
            copy.wait()

    packed = pl.pallas_call(
        body,
        in_specs=[pl.BlockSpec(memory_space=pltpu.SMEM)]
        + [pl.BlockSpec(memory_space=pl.ANY)] * count,
        out_specs=[whole_spec()] * len(outs),
        out_shape=outs,
        scratch_shapes=[pltpu.SemaphoreType.DMA((len(copies),))],
        name="pack",
    )(me, *values)
    first = len(routes[0].outs(routes[0].pack, 1))
    return packed[:first], packed[first:]


def places(orient_ref, layer, shape):
    lane = lax.broadcasted_iota(jnp.int32, shape, 1)
    cycle = lane >> 6
    orient = jnp.where(
        cycle == 0, orient_ref[CYCLES * layer], orient_ref[CYCLES * layer + 1]
    )
    lead, trail = (lane >> 3) & 7, lane & 7
    lead = jnp.where((orient & 1) == 1, SIDE - 1 - lead, lead)
    trail = jnp.where((orient & 2) == 2, SIDE - 1 - trail, trail)
    swapped = (orient & 4) == 4
    row = jnp.where(swapped, trail, lead)
    col = jnp.where(swapped, lead, trail)
    return row * RADIAL + cycle * SIDE + col


def from_grid(orient_ref, layer):
    shape = (BLOCK, BLOCK)
    grid_ids = lax.broadcasted_iota(jnp.int32, shape, 0)
    return (grid_ids == places(orient_ref, layer, shape)).astype(F32)


def order_body(
    me_ref, orient_ref, both_ref, faces_ref, halos_ref, inv_r_ref,
    both_out, faces_out, halos_out, inv_r_out,
):
    onto = from_grid(orient_ref, me_ref[0])
    inv_r_out[...] = jnp.broadcast_to(
        jnp.sum(onto * inv_r_ref[...], axis=0, keepdims=True), inv_r_out.shape
    )
    back = onto.T.astype(BF16)
    onto = onto.astype(BF16)
    for at in range(both_ref.shape[0]):
        moved = dot(both_ref[at], onto).astype(BF16)
        both_out[at] = dot(back, moved).astype(BF16)
    for at in range(faces_ref.shape[0]):
        faces_out[at] = dot(back, faces_ref[at]).astype(BF16)
    pairs = ((0, 3), (1, 4), (2, 5), (6, 7), (8, 8))
    for at, pair in enumerate(pairs):
        for half in range(2):
            for side in range(2):
                placed = dot(halos_ref[2 * pair[side] + half], onto).astype(BF16)
                halos_out[2 * at + half, :, side * BLOCK : (side + 1) * BLOCK] = placed


def weights_body(layers, orient_ref, means_ref, out_ref):
    def one(index, carry):
        onto = from_grid(orient_ref, index).astype(BF16)
        below = lax.rem(index + (layers - 1), layers)
        above = lax.rem(index + 1, layers)
        for number, layer in enumerate((below, index, above)):
            back = from_grid(orient_ref, layer).T.astype(BF16)
            moved = dot(means_ref[number], onto).astype(BF16)
            out_ref[index, number * BLOCK : (number + 1) * BLOCK, :] = dot(back, moved).astype(BF16)
        return carry

    lax.fori_loop(0, layers, one, 0)


def face_body(route, count, me_ref, *refs):
    vel_refs, (faces_ref, up_ref, down_ref, high, low) = refs[:count], refs[count:]
    route.load(me_ref, vel_refs, high, low)
    quarter = high.shape[0] // 4

    def faces(rows, variant):
        total = None
        for field in range(3):
            lanes, at = lanes_of(field), 6 * variant + 2 * field
            part = dot3((high[rows, lanes], low[rows, lanes]), (faces_ref[at], faces_ref[at + 1]))
            total = part if total is None else total + part
        return total

    for number in range(3):
        rows = slice(number * quarter, (number + 1) * quarter)
        total = faces(rows, 0) + faces(slice(3 * quarter, 4 * quarter), 1 + number)
        up_ref[rows, :] = total[:, :BLOCK]
        down_ref[rows, :] = total[:, BLOCK:]


FIRST = 3


def members_of(first_ref, second_ref, rows):
    return [ref[at, rows, :] for ref in (first_ref, second_ref) for at in range(ref.shape[0])]


def transform(high_ref, low_ref, rows, coef_h, coef_l, out_ref):
    table = (high_ref[rows, :], low_ref[rows, :])
    fields = out_ref.shape[0]
    for start in range(0, fields, 2):
        stop = min(start + 2, fields)
        lanes = slice(start * BLOCK, stop * BLOCK)
        values = dot3(table, (coef_h[:, lanes], coef_l[:, lanes]))
        for at in range(start, stop):
            out_ref[at] = values[:, lanes_of(at - start)]


def flow_parts(g_r, g_t, g_z, u):
    return (
        0.5 * (g_t[0] - g_r[1]),
        0.5 * (g_z[0] - g_r[2]),
        0.5 * (g_z[1] - g_t[2]),
        2.0 * g_r[0],
        g_t[0] + g_r[1],
        g_z[0] + g_r[2],
        2.0 * g_t[1],
        g_z[1] + g_t[2],
        2.0 * g_z[2],
        -(g_r[0] * u[0] + g_t[0] * u[1] + g_z[0] * u[2]),
        -(g_r[1] * u[0] + g_t[1] * u[1] + g_z[1] * u[2]),
        -(g_r[2] * u[0] + g_t[2] * u[1] + g_z[2] * u[2]),
    )


def matrix_of(ref, at):
    return ref[2 * at], ref[2 * at + 1]


def velocity_body(route, count, me_ref, *refs):
    psi_refs, refs = refs[:count], refs[count:]
    vel_h, vel_l, high_ref, low_ref, both_ref, inv_r_ref, vel_ref, flow_ref = refs[:8]
    coef_h, coef_l, psi_out, values = refs[8:]
    planes = high_ref.shape[1]
    route.load(me_ref, psi_refs, coef_h, coef_l)
    transform(high_ref, low_ref, slice(0, planes), coef_h, coef_l, psi_out)
    table = (high_ref[...], low_ref[...])
    values[:, 0:256] = dot3(table, (vel_h[:, 0:256], vel_l[:, 0:256]))
    values[:, 256:384] = dot3(table, (vel_h[:, 256:384], vel_l[:, 256:384]))
    rows_step = 128

    def chunk(start):
        rows = pl.ds(start, rows_step)
        turned = pl.ds(pl.multiple_of(planes + start, rows_step), rows_step)
        u = [values[rows, lanes_of(f)] for f in range(3)]
        u_s = [split(v) for v in u]
        dth_s = [split(values[turned, lanes_of(f)]) for f in range(3)]
        g_r = [dot3(u_s[f], matrix_of(both_ref, 2)) for f in range(3)]
        g_z = [dot3(u_s[f], matrix_of(both_ref, 3)) for f in range(3)]
        g_t = [dot3(dth_s[f], matrix_of(both_ref, 4)) for f in range(3)]
        g_t[0] = g_t[0] - dot3(u_s[1], matrix_of(both_ref, 4))
        g_t[1] = g_t[1] + dot3(u_s[0], matrix_of(both_ref, 4))
        hoop_rate = u[1] * inv_r_ref[0:1, :]
        parts = flow_parts(g_r, g_t, g_z, u)
        rest = (1.0 - 2.0 * MOBILITY) / RELAX_TIME
        for f in range(3):
            vel_ref[f, rows, :] = u[f]
        for at, part in enumerate((u[0], hoop_rate, u[2]) + parts):
            if at == 3:
                part = part + hoop_rate
            if at - 6 in DIAGONAL:
                part = part - rest
            flow_ref[at, rows, :] = part

    row_chunks(planes, rows_step, chunk)


def halo_body(
    below_ref, above_ref, vel_ref, high_ref, low_ref, halos_ref, places_ref, part_ref, values
):
    planes = high_ref.shape[1]
    quarter = planes // 4
    edges = []
    for ref in (below_ref, above_ref):
        last = None
        for number in range(3):
            part = split(ref[number * quarter : (number + 1) * quarter, :])
            part = dot(part[0], places_ref[number]) + dot(part[1], places_ref[number])
            last = part if last is None else last + part
        edges.append(jnp.concatenate([ref[...], last], axis=0))
    values[...] = dot3((high_ref[...], low_ref[...]), split(jnp.concatenate(edges, axis=1)))
    rows_step = planes // 2

    def chunk(start):
        rows = pl.ds(start, rows_step)
        turned = pl.ds(pl.multiple_of(planes + start, rows_step), rows_step)
        edge, edge_dth = split(values[rows, :]), split(values[turned, :])
        g_r, g_z = zip(*(halved(dot3(edge, matrix_of(halos_ref, f))) for f in range(3)))
        g_t = [
            *halved(dot3(edge_dth, matrix_of(halos_ref, 3))),
            dot3(edge_dth, (halos_ref[8, :, :BLOCK], halos_ref[9, :, :BLOCK])),
        ]
        mean_r, mean_t = halved(dot3(edge, matrix_of(halos_ref, 3)))
        g_t[0] = g_t[0] - mean_t
        g_t[1] = g_t[1] + mean_r
        u = [vel_ref[f, rows, :] for f in range(3)]
        for at, part in enumerate(flow_parts(g_r, g_t, g_z, u)):
            part_ref[at, rows, :] = part

    row_chunks(planes, rows_step, chunk)


def halved(pair):
    return pair[:, :BLOCK], pair[:, BLOCK:]


def square(m):
    a, b, c, d, e, f = m
    bb, cc, ee = b * b, c * c, e * e
    return (
        a * a + (bb + cc),
        b * (a + d) + c * e,
        c * (a + f) + b * e,
        d * d + (bb + ee),
        e * (d + f) + b * c,
        f * f + (cc + ee),
    )


def commuting_product(m, n):
    a, b, c, d, e, f = m
    p, q, r, s, t, u = n
    return (
        a * p + b * q + c * r,
        a * q + b * s + c * t,
        a * r + b * t + c * u,
        b * q + d * s + e * t,
        b * r + d * t + e * u,
        c * r + e * t + f * u,
    )


DIAGONAL = (0, 3, 5)


def plus_identity(m):
    return tuple(v + 1.0 if at in DIAGONAL else v for at, v in enumerate(m))


def exponential(psi, sign):
    square_2 = square(psi)
    square_4 = square(square_2)
    even = plus_identity(
        tuple(v * (0.5 / 64.0) + w * (1.0 / 24.0 / 4096.0) for v, w in zip(square_2, square_4))
    )
    factor = tuple(v * (sign / 6.0 / 512.0) for v in square_2)
    factor = tuple(v + sign * 0.125 if at in DIAGONAL else v for at, v in enumerate(factor))
    odd = commuting_product(psi, factor)
    total = tuple(v + w for v, w in zip(even, odd))
    for _ in range(3):
        total = square(total)
    return total


def row_chunks(planes, rows_step, body):
    def chunk(step, carry):
        body(pl.multiple_of(step * rows_step, rows_step))
        return carry

    lax.fori_loop(0, planes // rows_step, chunk, 0)


def momentum_body(route, count, out_route, out_count, me_ref, *refs):
    psi_refs, refs = refs[:count], refs[count:]
    first_ref, flow_ref, halo_ref, high_ref, low_ref = refs[:5]
    back_high_ref, back_low_ref, both_ref, inv_r_ref = refs[5:9]
    out_refs, refs = refs[9 : 9 + out_count], refs[9 + out_count :]
    coef_h, coef_l, psi_out, conform_out, stress_h, stress_l, vel_h, vel_l, mom_s, coeffs = refs
    planes = high_ref.shape[1]
    route.load(me_ref, psi_refs, coef_h, coef_l)
    transform(high_ref, low_ref, slice(0, planes), coef_h, coef_l, psi_out)
    rows_step = 16

    def chunk(start):
        rows = pl.ds(start, rows_step)
        inv_r = inv_r_ref[0:1, :]
        psi = members_of(first_ref, psi_out, rows)
        conform = exponential(psi, 1.0)
        for member in range(6):
            conform_out[member, rows, :] = conform[member]
        stress = tuple(v - 1.0 if at in DIAGONAL else v for at, v in enumerate(conform))
        for member, at in ((0, (0,)), (2, (1, 4)), (1, (2,)), (4, (3,)), (5, (5,))):
            high, low = split(stress[member])
            for lane in at:
                stress_h[rows, lanes_of(lane)] = high
                stress_l[rows, lanes_of(lane)] = low
        hoop = tuple(stress[at] * inv_r for at in (1, 3, 4))
        turned = pl.ds(pl.multiple_of(planes + start, rows_step), rows_step)
        for at in range(3):
            put(vel_h, vel_l, turned, lanes_of(at), hoop[at])
        carried = [flow_ref[12 + at, rows, :] + halo_ref[9 + at, rows, :] for at in range(3)]
        mom_s[0, rows, :] = carried[0] + (stress[0] * inv_r - hoop[1])
        mom_s[1, rows, :] = carried[1] + 2.0 * hoop[0]
        mom_s[2, rows, :] = carried[2] + stress[2] * inv_r

    row_chunks(planes, rows_step, chunk)
    divergence = tuple(
        jnp.concatenate([both_ref[at], both_ref[2 + at]], axis=0) for at in range(2)
    )
    for at in range(3):
        lanes = slice(2 * at * BLOCK, (2 * at + 2) * BLOCK)
        force = dot3((stress_h[:, lanes], stress_l[:, lanes]), divergence)
        put(vel_h, vel_l, slice(0, planes), lanes_of(at), mom_s[at] + force)
    back = (back_high_ref[...], back_low_ref[...])
    for start, stop in ((0, 2), (2, 3)):
        lanes = slice(start * BLOCK, stop * BLOCK)
        coeffs[:, lanes] = dot3(back, (vel_h[:, lanes], vel_l[:, lanes]))
    for field in range(3):
        out_route.store(me_ref, out_refs, field, coeffs.at[:, lanes_of(field)])


def elastic_body(route, me_ref, *refs):
    (
        first_h, first_l, second_h, second_l, first_ref, second_ref, conform_ref, flow_ref,
        halo_ref, high_ref, low_ref, back_high_ref, back_low_ref, both_ref,
    ) = refs[:14]
    out_ref, dth_s, grad_s, rate_h, rate_l, coeffs = refs[14:]
    planes = high_ref.shape[1]
    turned = slice(planes, 2 * planes)
    transform(high_ref, low_ref, turned, first_h, first_l, dth_s.at[pl.ds(0, FIRST)])
    transform(high_ref, low_ref, turned, second_h, second_l, dth_s.at[pl.ds(FIRST, 6 - FIRST)])
    gradient = tuple(
        jnp.concatenate([both_ref[at], both_ref[2 + at]], axis=1) for at in range(2)
    )
    for member in range(6):
        psi_ref = first_ref if member < FIRST else second_ref
        grad_s[member] = dot3(split(psi_ref[member % FIRST]), gradient)
    rows_step = 16
    inv_relax = 1.0 / RELAX_TIME

    def chunk(start):
        rows = pl.ds(start, rows_step)
        psi = members_of(first_ref, second_ref, rows)
        inverse = exponential(psi, -1.0)
        u_r, hoop_rate, u_z = (flow_ref[at, rows, :] for at in range(3))
        p, q, s, *strain = (
            flow_ref[3 + at, rows, :] + halo_ref[at, rows, :] for at in range(9)
        )
        a, b, c, d, e, f = psi
        pb, qc, se = p * b, q * c, s * e
        turning = (
            2.0 * (pb + qc),
            p * (d - a) + (q * e + s * c),
            q * (f - a) + (p * e - s * b),
            2.0 * (se - pb),
            s * (f - d) - (p * c + q * b),
            -2.0 * (qc + se),
        )
        for member in range(6):
            advect = (
                u_r * grad_s[member, rows, 0:BLOCK]
                + hoop_rate * dth_s[member, rows, :]
                + u_z * grad_s[member, rows, BLOCK : 2 * BLOCK]
            )
            relaxing = ((1.0 - MOBILITY) * inv_relax) * inverse[member] - (
                MOBILITY * inv_relax
            ) * conform_ref[member, rows, :]
            rate = (turning[member] - advect) + (strain[member] + relaxing)
            put(rate_h, rate_l, rows, lanes_of(member), rate)

    row_chunks(planes, rows_step, chunk)
    back = (back_high_ref[:, :planes], back_low_ref[:, :planes])
    for pair in range(3):
        lanes = slice(2 * pair * BLOCK, (2 * pair + 2) * BLOCK)
        coeffs[:, lanes] = dot3(back, (rate_h[:, lanes], rate_l[:, lanes]))
    for field in range(6):
        route.store(me_ref, [out_ref], field, coeffs.at[:, lanes_of(field)])


def advance_body(layers, step, route, count, *refs):
    me_ref, orient_ref, wall_ref = refs[:3]
    rate_refs, (mean_ref, old_ref, out_ref, rates) = refs[3 : 3 + count], refs[3 + count :]
    fields, local_modes = old_ref.shape[0], old_ref.shape[1]
    aligned = rates.dtype == BF16
    rows = fields * local_modes

    @pl.when(pl.program_id(0) == 0)
    def _():
        for array, place, rel in route.land:
            layer = route.index(me_ref, rel)
            if aligned:
                high, low = split(rate_refs[array][place].reshape(rows, BLOCK))
                rates[layer + 1, :rows, :] = high
                rates[layer + 1, rows:, :] = low
            else:
                rates[layer + 1] = rate_refs[array][place]
        rates[0] = rates[layers]
        rates[layers + 1] = rates[1]

    first = pl.program_id(0) * step

    def averaged(index, at, field):
        total = None
        for number in range(3):
            high, low = split(rates[index + number, field])
            weights = mean_ref[at, number * BLOCK : (number + 1) * BLOCK, :]
            part = dot(high, weights) + dot(low, weights)
            total = part if total is None else total + part
        return total

    for at in range(step):
        index = first + at
        lanes = lanes_of(at)
        if aligned:
            near = jnp.concatenate([rates[index + number] for number in range(3)], axis=1)
            every = dot(near, mean_ref[at])
            every = every[:rows] + every[rows:]
            change = [every[f * local_modes : (f + 1) * local_modes] for f in range(fields)]
        else:
            change = [averaged(index, at, f) for f in range(fields)]
        shape = (local_modes, BLOCK)
        column = places(orient_ref, index, shape) & (RADIAL - 1)
        inner = column == 0
        on_wall = jnp.logical_or(inner, column == RADIAL - 1)
        mean_row = jnp.logical_and(lax.broadcasted_iota(jnp.int32, shape, 0) == 0, inner)
        driven = jnp.where(mean_row, wall_ref[0], 0.0)
        for field in range(fields):
            stepped = old_ref[field, :, lanes] + STEP_DT * change[field]
            if fields == 3:
                stepped = jnp.where(on_wall, driven if field == 1 else 0.0, stepped)
            out_ref[field, :, lanes] = stepped


def advance(rates, route, weights, old, me, orientation, wall):
    fields, local_modes, nodes = old.shape
    layers = nodes // BLOCK
    step = 16
    block = pl.BlockSpec((fields, local_modes, step * BLOCK), lambda i: (0, 0, i))
    scalar = pl.BlockSpec(memory_space=pltpu.SMEM)
    return pl.pallas_call(
        functools.partial(advance_body, layers, step, route, len(rates)),
        grid=(layers // step,),
        in_specs=[scalar] * 3
        + [pl.BlockSpec(part.shape, lambda i: (0, 0, 0, 0)) for part in rates]
        + [pl.BlockSpec((step, 3 * BLOCK, BLOCK), lambda i: (i, 0, 0)), block],
        out_specs=block,
        out_shape=jax.ShapeDtypeStruct(old.shape, F32),
        scratch_shapes=[
            pltpu.VMEM((layers + 2, 2 * fields * local_modes, BLOCK), BF16)
            if local_modes % 16 == 0
            else pltpu.VMEM((layers + 2, fields, local_modes, BLOCK), F32)
        ],
        compiler_params=pltpu.CompilerParams(vmem_limit_bytes=24 * MIB),
        name="advance",
    )(me, orientation, wall, *rates, weights, old)


def body(velocity, log_conf, orientation, wall_speed):
    devices = lax.axis_size("mode")
    device = lax.axis_index("mode").astype(jnp.int32)
    me = device.reshape(1)
    local_modes = velocity.shape[1]
    layers = velocity.shape[2] // BLOCK
    planes = local_modes * devices
    far_first = Route(devices, local_modes, True)
    near_first = Route(devices, local_modes, False)
    whole = Route(devices, local_modes, False, False)
    barrier = lax.optimization_barrier
    staged = far_first.staged
    both, faces, halos, means, inv_r_nodes = node_tables()

    def parts(tables):
        return jnp.asarray(np.stack([half for table in tables for half in split_table(table)]))

    fourier = fourier_tables(planes)
    high, low = (jnp.asarray(half) for half in split_table(fourier))
    signed = np.concatenate([fourier[:planes].T, -fourier[planes:].T], axis=1)
    back_high, back_low = (jnp.asarray(half) for half in split_table(signed))
    inv_r_table = jnp.asarray(np.tile(inv_r_nodes[:, None], (1, BLOCK)), F32)

    both_s, faces_s, halos_s, inv_r = kernel_call(
        order_body,
        (
            jax.ShapeDtypeStruct((10, BLOCK, BLOCK), BF16),
            jax.ShapeDtypeStruct((24, BLOCK, 2 * BLOCK), BF16),
            jax.ShapeDtypeStruct((10, 2 * BLOCK, 2 * BLOCK), BF16),
            jax.ShapeDtypeStruct((8, BLOCK), F32),
        ),
        4,
        scalars=2,
        vmem=16,
        name="order",
    )(me, orientation, parts(both), parts(faces), parts(halos), inv_r_table)
    weights = kernel_call(
        functools.partial(weights_body, layers),
        jax.ShapeDtypeStruct((layers, 3 * BLOCK, BLOCK), BF16),
        1,
        vmem=8 + layers // 8,
        name="weights",
    )(orientation, jnp.asarray(means, BF16))

    vel_nodes, psi_nodes = pack(me, (velocity, log_conf), (far_first, near_first))
    fixed = (both_s, faces_s, halos_s, inv_r, weights)
    if staged:
        psi_nodes = near_swaps(psi_nodes)
        vel_nodes = far_swaps(vel_nodes, psi_nodes)
        vel_nodes, psi_nodes, fixed = barrier((vel_nodes, psi_nodes, fixed))
        vel_nodes = near_swaps(regroup(vel_nodes))
        first_nodes = far_swaps(regroup([group[:, :FIRST] for group in psi_nodes]))
        second_nodes = regroup([group[:, FIRST:] for group in psi_nodes])
    else:
        vel_nodes = far_first.unpacked(in_one(vel_nodes))
        psi_nodes = near_first.unpacked(in_one(psi_nodes))
        first_nodes = [group[:, :FIRST] for group in psi_nodes]
        second_nodes = [group[:, FIRST:] for group in psi_nodes]

    both_s, faces_s, halos_s, inv_r, weights = fixed
    edge = jax.ShapeDtypeStruct((planes // 4 * 3, BLOCK), F32)
    vel_half = jax.ShapeDtypeStruct((planes, 3 * BLOCK), BF16)
    to_up, to_down, vel_h, vel_l = kernel_call(
        functools.partial(face_body, far_first, len(vel_nodes)),
        (edge, edge, vel_half, vel_half),
        len(vel_nodes) + 1,
        vmem=16,
        name="faces",
    )(me, *vel_nodes, faces_s)
    up = [(i, (i + 1) % devices) for i in range(devices)]
    below = lax.ppermute(to_up, "mode", up)
    above = lax.ppermute(to_down, "mode", [(j, i) for i, j in up])

    def halves(fields):
        return (
            jax.ShapeDtypeStruct((planes, fields * BLOCK), BF16),
            jax.ShapeDtypeStruct((planes, fields * BLOCK), BF16),
            jax.ShapeDtypeStruct((fields, planes, BLOCK), F32),
        )

    vel, own_flow, first_h, first_l, first = kernel_call(
        functools.partial(velocity_body, near_first, len(first_nodes)),
        (
            jax.ShapeDtypeStruct((3, planes, BLOCK), F32),
            jax.ShapeDtypeStruct((15, planes, BLOCK), F32),
            *halves(FIRST),
        ),
        len(first_nodes) + 6,
        scratch=[pltpu.VMEM((2 * planes, 3 * BLOCK), F32)],
        vmem=20,
        name="velocity",
    )(me, *first_nodes, vel_h, vel_l, high, low, both_s, inv_r)
    if staged:
        early = second_nodes
        second_nodes, below, above, vel = barrier((second_nodes, below, above, vel))
        second_nodes = far_swaps([early[0], second_nodes[1], early[2], early[3]])
    halo_flow = kernel_call(
        halo_body,
        jax.ShapeDtypeStruct((12, planes, BLOCK), F32),
        7,
        scalars=0,
        scratch=[pltpu.VMEM((2 * planes, 2 * BLOCK), F32)],
        vmem=24,
        name="halo",
    )(below, above, vel, high, low, halos_s, jnp.asarray(free_places(), BF16))

    far_outs = far_first.outs(far_first.leave, 3, far_first.modes, BLOCK)
    psi_outs = whole.outs(whole.leave, 6, whole.modes, BLOCK)
    field6 = jax.ShapeDtypeStruct((6, planes, BLOCK), F32)
    *vel_rates, second_h, second_l, second, conform = kernel_call(
        functools.partial(
            momentum_body, near_first, len(second_nodes), far_first, len(far_outs)
        ),
        (*far_outs, *halves(6 - FIRST), field6),
        len(second_nodes) + 9,
        scratch=[
            pltpu.VMEM((planes, 6 * BLOCK), BF16),
            pltpu.VMEM((planes, 6 * BLOCK), BF16),
            pltpu.VMEM((2 * planes, 3 * BLOCK), BF16),
            pltpu.VMEM((2 * planes, 3 * BLOCK), BF16),
            pltpu.VMEM((3, planes, BLOCK), F32),
            pltpu.VMEM((planes, 3 * BLOCK), F32),
        ],
        vmem=24,
        name="momentum",
    )(me, *second_nodes, first, own_flow, halo_flow, high, low, back_high, back_low, both_s, inv_r)
    vel_rates = far_first.packed(vel_rates)
    psi_rates = kernel_call(
        functools.partial(elastic_body, whole),
        (*psi_outs,),
        14,
        scratch=[
            pltpu.VMEM((6, planes, BLOCK), F32),
            pltpu.VMEM((6, planes, 2 * BLOCK), F32),
            pltpu.VMEM((planes, 6 * BLOCK), BF16),
            pltpu.VMEM((planes, 6 * BLOCK), BF16),
            pltpu.VMEM((planes, 6 * BLOCK), F32),
        ],
        vmem=24,
        name="elastic",
    )(
        me, first_h, first_l, second_h, second_l, first, second, conform, own_flow, halo_flow, high, low,
        back_high, back_low, both_s,
    )

    psi_rates = whole.packed(psi_rates)
    if staged:
        vel_rates, psi_rates = barrier((far_swaps(vel_rates), psi_rates))
        vel_rates = near_swaps(turn(vel_rates))
    else:
        vel_rates = in_one(vel_rates)
    psi_rates = in_one(psi_rates)
    wall = jnp.where(device == 0, wall_speed, 0.0)
    at_walls = (me, orientation, wall)
    vel_next = advance(vel_rates, far_first, weights, velocity, *at_walls)
    logc_next = advance(psi_rates, whole, weights, log_conf, *at_walls)
    return vel_next, logc_next


def solution(mesh):
    in_specs = (P("ens", "mode", None), P("ens", "mode", None), P(), P("ens"))
    out_specs = (P("ens", "mode", None), P("ens", "mode", None))
    return jax.shard_map(body, mesh=mesh, in_specs=in_specs, out_specs=out_specs, check_vma=False)
```

```python
import functools

import jax
import jax.numpy as jnp
import ml_dtypes
import numpy as np
from jax import lax
from jax.experimental import pallas as pl
from jax.experimental.pallas import tpu as pltpu
from jax.sharding import PartitionSpec as P

SIDE = 8
CYCLES = 2
RADIAL = SIDE * CYCLES
BLOCK = SIDE * RADIAL
STEP_DT = 0.002
RELAX_TIME = 0.02
MOBILITY = 0.3
LAYER_HEIGHT = 0.25
R_INNER = 1.0
MIB = 1 << 20
F32 = jnp.float32
BF16 = jnp.bfloat16


def split_table(table):
    high = np.asarray(table, np.float32).astype(ml_dtypes.bfloat16)
    low = (np.asarray(table, np.float64) - high.astype(np.float64)).astype(ml_dtypes.bfloat16)
    return high, low


def cheb_table(points):
    nodes_xi = -np.cos(np.pi * np.arange(points) / (points - 1))
    weights = np.ones(points)
    weights[0] = 2.0
    weights[-1] = 2.0
    weights = weights * (-1.0) ** np.arange(points)
    identity = np.eye(points)
    spacing = nodes_xi[:, None] - nodes_xi[None, :] + identity
    matrix = weights[:, None] / weights[None, :] / spacing
    matrix = matrix * (1.0 - identity)
    matrix = matrix - identity * matrix.sum(axis=1)[:, None]
    return nodes_xi, matrix


def fourier_tables(planes):
    phase = np.arange(planes)[:, None] * np.arange(planes // 2)[None, :] % planes
    angles = phase * (2.0 * np.pi / planes)
    cosine = np.cos(angles) * np.sqrt(2.0 / planes)
    sine = np.sin(angles) * np.sqrt(2.0 / planes)
    cosine[:, 0] = planes**-0.5
    sine[:, 0] = (-1.0) ** np.arange(planes) * planes**-0.5
    wavenums = np.arange(planes // 2)
    basis = np.stack([cosine, sine], axis=2).reshape(planes, planes)
    turned = np.stack([-wavenums * sine, wavenums * cosine], axis=2).reshape(planes, planes)
    return np.concatenate([basis, turned], axis=0)


def node_tables():
    nodes_xi, matrix = cheb_table(SIDE)
    radius = R_INNER + (np.arange(CYCLES)[:, None] + (nodes_xi[None, :] + 1.0) / 2.0) / CYCLES
    inv_r = 1.0 / radius.reshape(-1)
    radial_row = np.kron(np.eye(CYCLES), matrix.T * (2.0 * CYCLES))
    radial_mean = np.eye(RADIAL)
    for cycle in range(1, CYCLES):
        low, high = cycle * SIDE - 1, cycle * SIDE
        radial_mean[low : high + 1, low : high + 1] = 0.5
    d_radial = np.kron(np.eye(SIDE), radial_row)
    d_axial = np.kron(matrix.T * (2.0 / LAYER_HEIGHT), np.eye(RADIAL))
    own_weight = np.ones(SIDE)
    own_weight[[0, -1]] = 0.5
    average = np.kron(np.diag(own_weight), radial_mean)
    inv_r_nodes = np.tile(inv_r, SIDE)
    both = np.stack(
        [d_radial, d_axial, d_radial @ average, d_axial @ average, average * inv_r_nodes[None, :]]
    )
    below = np.zeros((SIDE, SIDE))
    below[SIDE - 1, 0] = 0.5
    means = np.stack([np.kron(below, radial_mean), average, np.kron(below.T, radial_mean)])
    faces = np.zeros((3, BLOCK, 2 * BLOCK))
    halos = np.zeros((9, 2 * BLOCK, BLOCK))
    for field in range(3):
        for side, row in ((0, SIDE - 1), (1, 0)):
            at_u = side * BLOCK + field * RADIAL
            at_dz = at_u + 3 * RADIAL
            face_nodes = slice(row * RADIAL, (row + 1) * RADIAL)
            faces[field, face_nodes, at_u : at_u + RADIAL] = np.eye(RADIAL)
            faces[field, :, at_dz : at_dz + RADIAL] = d_axial[:, face_nodes]
            here = SIDE - 1 - row
            out = slice(here * RADIAL, (here + 1) * RADIAL)
            halos[field, at_u : at_u + RADIAL, out] = 0.5 * radial_row @ radial_mean
            halos[3 + field, at_dz : at_dz + RADIAL, out] = 0.5 * radial_mean
            halos[6 + field, at_u : at_u + RADIAL, out] = 0.5 * radial_mean * inv_r[None, :]
    used = 6 * RADIAL
    packed = [faces]
    for number in range(3):
        variant = np.zeros_like(faces)
        for side in (0, BLOCK):
            group = slice(side + number * (BLOCK - used), side + (number + 1) * (BLOCK - used))
            variant[:, :, side + used : side + BLOCK] = faces[:, :, group]
        packed.append(variant)
    return both, np.concatenate(packed), halos, means, inv_r_nodes


def free_places():
    used = 6 * RADIAL
    free = BLOCK - used
    moves = np.zeros((3, BLOCK, BLOCK))
    for number in range(3):
        moves[number, used:, number * free : (number + 1) * free] = np.eye(free)
    return moves


def split(values):
    high = values.astype(BF16)
    return high, (values - high.astype(F32)).astype(BF16)


def dot(left, right):
    return jnp.dot(left, right, preferred_element_type=F32)


def dot3(left, right):
    width = right[0].shape[1]
    if width > BLOCK:
        return dot(left[0], right[0]) + (dot(left[0], right[1]) + dot(left[1], right[0]))
    both = dot(left[0], jnp.concatenate(right, axis=1))
    return both[:, :width] + (both[:, width:] + dot(left[1], right[0]))


def whole_spec():
    return pl.BlockSpec(memory_space=pltpu.VMEM)


def kernel_call(
    body, outs, count, scalars=1, scratch=(), vmem=40, name=None
):
    return pl.pallas_call(
        body,
        out_shape=outs,
        in_specs=[pl.BlockSpec(memory_space=pltpu.SMEM)] * scalars + [whole_spec()] * count,
        out_specs=jax.tree.map(lambda _: whole_spec(), outs),
        scratch_shapes=list(scratch),
        compiler_params=pltpu.CompilerParams(vmem_limit_bytes=vmem * MIB),
        name=name,
    )


def lanes_of(at):
    return slice(at * BLOCK, (at + 1) * BLOCK)


def put(high, low, rows, lanes, value):
    value_h, value_l = split(value)
    high[rows, lanes] = value_h
    low[rows, lanes] = value_l


NEAR = 4


def swap(block, bits):
    devices = lax.axis_size("mode")
    return lax.ppermute(block, "mode", [(i, i ^ bits) for i in range(devices)])


def after(block, token):
    return lax.optimization_barrier((block, token))[0]


def near_swaps(groups):
    return [groups[0]] + [swap(groups[t], t) for t in (1, 2, 3)]


def far_swaps(groups, beside=None):
    first = groups[1] if beside is None else after(groups[1], beside[1])
    return [groups[0], swap(first, NEAR)] + [swap(groups[s], NEAR * s) for s in (2, 3)]


def regroup(groups):
    return [jnp.stack([group[at] for group in groups]) for at in range(NEAR)]


class Route:
    def __init__(self, devices, local_modes, far_first, staged=True):
        self.staged = staged and devices == NEAR * NEAR and local_modes % 16 == 0
        self.aligned = self.staged or local_modes % 16 == 0
        self.devices, self.local_modes, self.far_first = devices, local_modes, far_first
        self.modes = local_modes if self.aligned else local_modes * devices
        if not self.staged:
            self.pack = self.land = [(0, at, at) for at in range(devices)]
            self.leave = self.arrive = self.pack if self.aligned else [(0, 0, 0)]
            return
        far = [(s, t, NEAR * s + t) for s in range(NEAR) for t in range(NEAR)]
        near = [(t, s, NEAR * s + t) for s in range(NEAR) for t in range(NEAR)]
        self.pack = self.leave = far if far_first else near
        self.land = self.arrive = near if far_first else far

    def outs(self, blocks, *block):
        arrays, places = (1 + max(entry[at] for entry in blocks) for at in range(2))
        return [jax.ShapeDtypeStruct((places,) + block, F32)] * arrays

    def index(self, me_ref, rel):
        return (me_ref[0] ^ rel) if self.staged else rel

    def rows(self, me_ref, rel):
        start = self.index(me_ref, rel) * self.modes
        return pl.ds(pl.multiple_of(start, self.modes), self.modes)

    def load(self, me_ref, refs, high, low):
        for array, place, rel in self.arrive:
            rows = self.rows(me_ref, rel)
            for field in range(refs[array].shape[1]):
                put(high, low, rows, lanes_of(field), refs[array][place, field])

    def store(self, me_ref, refs, field, coeffs):
        for array, place, rel in self.leave:
            refs[array][place, field] = coeffs[self.rows(me_ref, rel), :]

    def packed(self, arrays):
        if self.aligned:
            return arrays
        _, fields, planes, nodes = arrays[0].shape
        blocks = arrays[0].reshape(fields, planes // self.local_modes, self.local_modes, nodes)
        return [blocks.transpose(1, 0, 2, 3)]

    def unpacked(self, arrays):
        if self.aligned:
            return arrays
        devices, fields, modes, nodes = arrays[0].shape
        return [arrays[0].transpose(1, 0, 2, 3).reshape(1, fields, devices * modes, nodes)]


def in_one(arrays):
    return [lax.all_to_all(arrays[0], "mode", split_axis=0, concat_axis=0, tiled=True)]


def pack(me, values, routes):
    outs, copies = [], []
    for at, (array, route) in enumerate(zip(values, routes)):
        fields, local_modes, _ = array.shape
        copies += [(at, len(outs) + out, place, rel) for out, place, rel in route.pack]
        outs += route.outs(route.pack, fields, local_modes, BLOCK)
    count = len(values)

    def body(me_ref, *refs):
        in_refs, out_refs, sems = refs[:count], refs[count:-1], refs[-1]
        started = []
        for number, (at, out, place, rel) in enumerate(copies):
            layer = routes[at].index(me_ref, rel)
            lanes = pl.ds(pl.multiple_of(layer * BLOCK, BLOCK), BLOCK)
            copy = pltpu.make_async_copy(
                in_refs[at].at[:, :, lanes], out_refs[out].at[place], sems.at[number]
            )
            copy.start()
            started.append(copy)
        for copy in started:
            copy.wait()

    packed = pl.pallas_call(
        body,
        in_specs=[pl.BlockSpec(memory_space=pltpu.SMEM)]
        + [pl.BlockSpec(memory_space=pl.ANY)] * count,
        out_specs=[whole_spec()] * len(outs),
        out_shape=outs,
        scratch_shapes=[pltpu.SemaphoreType.DMA((len(copies),))],
        name="pack",
    )(me, *values)
    first = len(routes[0].outs(routes[0].pack, 1))
    return packed[:first], packed[first:]


def places(orient_ref, layer, shape):
    lane = lax.broadcasted_iota(jnp.int32, shape, 1)
    cycle = lane >> 6
    orient = jnp.where(
        cycle == 0, orient_ref[CYCLES * layer], orient_ref[CYCLES * layer + 1]
    )
    lead, trail = (lane >> 3) & 7, lane & 7
    lead = jnp.where((orient & 1) == 1, SIDE - 1 - lead, lead)
    trail = jnp.where((orient & 2) == 2, SIDE - 1 - trail, trail)
    swapped = (orient & 4) == 4
    row = jnp.where(swapped, trail, lead)
    col = jnp.where(swapped, lead, trail)
    return row * RADIAL + cycle * SIDE + col


def from_grid(orient_ref, layer):
    shape = (BLOCK, BLOCK)
    grid_ids = lax.broadcasted_iota(jnp.int32, shape, 0)
    return (grid_ids == places(orient_ref, layer, shape)).astype(F32)


def order_body(
    me_ref, orient_ref, both_ref, faces_ref, halos_ref, inv_r_ref,
    both_out, faces_out, halos_out, inv_r_out,
):
    onto = from_grid(orient_ref, me_ref[0])
    inv_r_out[...] = jnp.broadcast_to(
        jnp.sum(onto * inv_r_ref[...], axis=0, keepdims=True), inv_r_out.shape
    )
    back = onto.T.astype(BF16)
    onto = onto.astype(BF16)
    for at in range(both_ref.shape[0]):
        moved = dot(both_ref[at], onto).astype(BF16)
        both_out[at] = dot(back, moved).astype(BF16)
    for at in range(faces_ref.shape[0]):
        faces_out[at] = dot(back, faces_ref[at]).astype(BF16)
    pairs = ((0, 3), (1, 4), (2, 5), (6, 7), (8, 8))
    for at, pair in enumerate(pairs):
        for half in range(2):
            for side in range(2):
                placed = dot(halos_ref[2 * pair[side] + half], onto).astype(BF16)
                halos_out[2 * at + half, :, side * BLOCK : (side + 1) * BLOCK] = placed


def weights_body(layers, orient_ref, means_ref, out_ref):
    def one(index, carry):
        onto = from_grid(orient_ref, index).astype(BF16)
        below = lax.rem(index + (layers - 1), layers)
        above = lax.rem(index + 1, layers)
        for number, layer in enumerate((below, index, above)):
            back = from_grid(orient_ref, layer).T.astype(BF16)
            moved = dot(means_ref[number], onto).astype(BF16)
            out_ref[index, number * BLOCK : (number + 1) * BLOCK, :] = dot(back, moved).astype(BF16)
        return carry

    lax.fori_loop(0, layers, one, 0)


def face_body(route, count, me_ref, *refs):
    vel_refs, (faces_ref, up_ref, down_ref, high, low) = refs[:count], refs[count:]
    route.load(me_ref, vel_refs, high, low)
    quarter = high.shape[0] // 4

    def faces(rows, variant):
        total = None
        for field in range(3):
            lanes, at = lanes_of(field), 6 * variant + 2 * field
            part = dot3((high[rows, lanes], low[rows, lanes]), (faces_ref[at], faces_ref[at + 1]))
            total = part if total is None else total + part
        return total

    for number in range(3):
        rows = slice(number * quarter, (number + 1) * quarter)
        total = faces(rows, 0) + faces(slice(3 * quarter, 4 * quarter), 1 + number)
        up_ref[rows, :] = total[:, :BLOCK]
        down_ref[rows, :] = total[:, BLOCK:]


FIRST = 3


def members_of(first_ref, second_ref, rows):
    return [ref[at, rows, :] for ref in (first_ref, second_ref) for at in range(ref.shape[0])]


def transform(high_ref, low_ref, rows, coef_h, coef_l, out_ref):
    table = (high_ref[rows, :], low_ref[rows, :])
    fields = out_ref.shape[0]
    for start in range(0, fields, 2):
        stop = min(start + 2, fields)
        lanes = slice(start * BLOCK, stop * BLOCK)
        values = dot3(table, (coef_h[:, lanes], coef_l[:, lanes]))
        for at in range(start, stop):
            out_ref[at] = values[:, lanes_of(at - start)]


def flow_parts(g_r, g_t, g_z, u):
    return (
        0.5 * (g_t[0] - g_r[1]),
        0.5 * (g_z[0] - g_r[2]),
        0.5 * (g_z[1] - g_t[2]),
        2.0 * g_r[0],
        g_t[0] + g_r[1],
        g_z[0] + g_r[2],
        2.0 * g_t[1],
        g_z[1] + g_t[2],
        2.0 * g_z[2],
        -(g_r[0] * u[0] + g_t[0] * u[1] + g_z[0] * u[2]),
        -(g_r[1] * u[0] + g_t[1] * u[1] + g_z[1] * u[2]),
        -(g_r[2] * u[0] + g_t[2] * u[1] + g_z[2] * u[2]),
    )


def matrix_of(ref, at):
    return ref[2 * at], ref[2 * at + 1]


def velocity_body(route, count, me_ref, *refs):
    psi_refs, refs = refs[:count], refs[count:]
    vel_h, vel_l, high_ref, low_ref, both_ref, inv_r_ref, vel_ref, flow_ref = refs[:8]
    coef_h, coef_l, psi_out, values = refs[8:]
    planes = high_ref.shape[1]
    route.load(me_ref, psi_refs, coef_h, coef_l)
    transform(high_ref, low_ref, slice(0, planes), coef_h, coef_l, psi_out)
    table = (high_ref[...], low_ref[...])
    values[:, 0:256] = dot3(table, (vel_h[:, 0:256], vel_l[:, 0:256]))
    values[:, 256:384] = dot3(table, (vel_h[:, 256:384], vel_l[:, 256:384]))
    rows_step = 256

    def chunk(start):
        rows = pl.ds(start, rows_step)
        turned = pl.ds(pl.multiple_of(planes + start, rows_step), rows_step)
        u = [values[rows, lanes_of(f)] for f in range(3)]
        u_s = [split(v) for v in u]
        dth_s = [split(values[turned, lanes_of(f)]) for f in range(3)]
        g_r = [dot3(u_s[f], matrix_of(both_ref, 2)) for f in range(3)]
        g_z = [dot3(u_s[f], matrix_of(both_ref, 3)) for f in range(3)]
        g_t = [dot3(dth_s[f], matrix_of(both_ref, 4)) for f in range(3)]
        g_t[0] = g_t[0] - dot3(u_s[1], matrix_of(both_ref, 4))
        g_t[1] = g_t[1] + dot3(u_s[0], matrix_of(both_ref, 4))
        hoop_rate = u[1] * inv_r_ref[0:1, :]
        parts = flow_parts(g_r, g_t, g_z, u)
        rest = (1.0 - 2.0 * MOBILITY) / RELAX_TIME
        for f in range(3):
            vel_ref[f, rows, :] = u[f]
        for at, part in enumerate((u[0], hoop_rate, u[2]) + parts):
            if at == 3:
                part = part + hoop_rate
            if at - 6 in DIAGONAL:
                part = part - rest
            flow_ref[at, rows, :] = part

    row_chunks(planes, rows_step, chunk)


def halo_body(
    below_ref, above_ref, vel_ref, high_ref, low_ref, halos_ref, places_ref, part_ref, values
):
    planes = high_ref.shape[1]
    quarter = planes // 4
    edges = []
    for ref in (below_ref, above_ref):
        last = None
        for number in range(3):
            part = split(ref[number * quarter : (number + 1) * quarter, :])
            part = dot(part[0], places_ref[number]) + dot(part[1], places_ref[number])
            last = part if last is None else last + part
        edges.append(jnp.concatenate([ref[...], last], axis=0))
    values[...] = dot3((high_ref[...], low_ref[...]), split(jnp.concatenate(edges, axis=1)))
    rows_step = planes // 2

    def chunk(start):
        rows = pl.ds(start, rows_step)
        turned = pl.ds(pl.multiple_of(planes + start, rows_step), rows_step)
        edge, edge_dth = split(values[rows, :]), split(values[turned, :])
        g_r, g_z = zip(*(halved(dot3(edge, matrix_of(halos_ref, f))) for f in range(3)))
        g_t = [
            *halved(dot3(edge_dth, matrix_of(halos_ref, 3))),
            dot3(edge_dth, (halos_ref[8, :, :BLOCK], halos_ref[9, :, :BLOCK])),
        ]
        mean_r, mean_t = halved(dot3(edge, matrix_of(halos_ref, 3)))
        g_t[0] = g_t[0] - mean_t
        g_t[1] = g_t[1] + mean_r
        u = [vel_ref[f, rows, :] for f in range(3)]
        for at, part in enumerate(flow_parts(g_r, g_t, g_z, u)):
            part_ref[at, rows, :] = part

    row_chunks(planes, rows_step, chunk)


def halved(pair):
    return pair[:, :BLOCK], pair[:, BLOCK:]


def square(m):
    a, b, c, d, e, f = m
    bb, cc, ee = b * b, c * c, e * e
    return (
        a * a + (bb + cc),
        b * (a + d) + c * e,
        c * (a + f) + b * e,
        d * d + (bb + ee),
        e * (d + f) + b * c,
        f * f + (cc + ee),
    )


def commuting_product(m, n):
    a, b, c, d, e, f = m
    p, q, r, s, t, u = n
    return (
        a * p + b * q + c * r,
        a * q + b * s + c * t,
        a * r + b * t + c * u,
        b * q + d * s + e * t,
        b * r + d * t + e * u,
        c * r + e * t + f * u,
    )


DIAGONAL = (0, 3, 5)


def plus_identity(m):
    return tuple(v + 1.0 if at in DIAGONAL else v for at, v in enumerate(m))


def exponential(psi, sign):
    square_2 = square(psi)
    square_4 = square(square_2)
    even = plus_identity(
        tuple(v * (0.5 / 64.0) + w * (1.0 / 24.0 / 4096.0) for v, w in zip(square_2, square_4))
    )
    factor = tuple(v * (sign / 6.0 / 512.0) for v in square_2)
    factor = tuple(v + sign * 0.125 if at in DIAGONAL else v for at, v in enumerate(factor))
    odd = commuting_product(psi, factor)
    total = tuple(v + w for v, w in zip(even, odd))
    for _ in range(3):
        total = square(total)
    return total


def row_chunks(planes, rows_step, body):
    def chunk(step, carry):
        body(pl.multiple_of(step * rows_step, rows_step))
        return carry

    lax.fori_loop(0, planes // rows_step, chunk, 0)


def momentum_body(route, count, out_route, out_count, me_ref, *refs):
    psi_refs, refs = refs[:count], refs[count:]
    first_ref, flow_ref, halo_ref, high_ref, low_ref = refs[:5]
    back_high_ref, back_low_ref, both_ref, inv_r_ref = refs[5:9]
    out_refs, refs = refs[9 : 9 + out_count], refs[9 + out_count :]
    coef_h, coef_l, psi_out, conform_out, stress_h, stress_l, vel_h, vel_l, mom_s, coeffs = refs
    planes = high_ref.shape[1]
    route.load(me_ref, psi_refs, coef_h, coef_l)
    transform(high_ref, low_ref, slice(0, planes), coef_h, coef_l, psi_out)
    rows_step = 16

    def chunk(start):
        rows = pl.ds(start, rows_step)
        inv_r = inv_r_ref[0:1, :]
        psi = members_of(first_ref, psi_out, rows)
        conform = exponential(psi, 1.0)
        for member in range(6):
            conform_out[member, rows, :] = conform[member]
        stress = tuple(v - 1.0 if at in DIAGONAL else v for at, v in enumerate(conform))
        for member, at in ((0, (0,)), (2, (1, 4)), (1, (2,)), (4, (3,)), (5, (5,))):
            high, low = split(stress[member])
            for lane in at:
                stress_h[rows, lanes_of(lane)] = high
                stress_l[rows, lanes_of(lane)] = low
        hoop = tuple(stress[at] * inv_r for at in (1, 3, 4))
        turned = pl.ds(pl.multiple_of(planes + start, rows_step), rows_step)
        for at in range(3):
            put(vel_h, vel_l, turned, lanes_of(at), hoop[at])
        carried = [flow_ref[12 + at, rows, :] + halo_ref[9 + at, rows, :] for at in range(3)]
        mom_s[0, rows, :] = carried[0] + (stress[0] * inv_r - hoop[1])
        mom_s[1, rows, :] = carried[1] + 2.0 * hoop[0]
        mom_s[2, rows, :] = carried[2] + stress[2] * inv_r

    row_chunks(planes, rows_step, chunk)
    divergence = tuple(
        jnp.concatenate([both_ref[at], both_ref[2 + at]], axis=0) for at in range(2)
    )
    for at in range(3):
        lanes = slice(2 * at * BLOCK, (2 * at + 2) * BLOCK)
        force = dot3((stress_h[:, lanes], stress_l[:, lanes]), divergence)
        put(vel_h, vel_l, slice(0, planes), lanes_of(at), mom_s[at] + force)
    back = (back_high_ref[...], back_low_ref[...])
    for start, stop in ((0, 2), (2, 3)):
        lanes = slice(start * BLOCK, stop * BLOCK)
        coeffs[:, lanes] = dot3(back, (vel_h[:, lanes], vel_l[:, lanes]))
    for field in range(3):
        out_route.store(me_ref, out_refs, field, coeffs.at[:, lanes_of(field)])


def elastic_body(route, me_ref, *refs):
    (
        first_h, first_l, second_h, second_l, first_ref, second_ref, conform_ref, flow_ref,
        halo_ref, high_ref, low_ref, back_high_ref, back_low_ref, both_ref,
    ) = refs[:14]
    out_ref, dth_s, grad_s, rate_h, rate_l, coeffs = refs[14:]
    planes = high_ref.shape[1]
    turned = slice(planes, 2 * planes)
    transform(high_ref, low_ref, turned, first_h, first_l, dth_s.at[pl.ds(0, FIRST)])
    transform(high_ref, low_ref, turned, second_h, second_l, dth_s.at[pl.ds(FIRST, 6 - FIRST)])
    gradient = tuple(
        jnp.concatenate([both_ref[at], both_ref[2 + at]], axis=1) for at in range(2)
    )
    for member in range(6):
        psi_ref = first_ref if member < FIRST else second_ref
        grad_s[member] = dot3(split(psi_ref[member % FIRST]), gradient)
    rows_step = 16
    inv_relax = 1.0 / RELAX_TIME

    def chunk(start):
        rows = pl.ds(start, rows_step)
        psi = members_of(first_ref, second_ref, rows)
        inverse = exponential(psi, -1.0)
        u_r, hoop_rate, u_z = (flow_ref[at, rows, :] for at in range(3))
        p, q, s, *strain = (
            flow_ref[3 + at, rows, :] + halo_ref[at, rows, :] for at in range(9)
        )
        a, b, c, d, e, f = psi
        pb, qc, se = p * b, q * c, s * e
        turning = (
            2.0 * (pb + qc),
            p * (d - a) + (q * e + s * c),
            q * (f - a) + (p * e - s * b),
            2.0 * (se - pb),
            s * (f - d) - (p * c + q * b),
            -2.0 * (qc + se),
        )
        for member in range(6):
            advect = (
                u_r * grad_s[member, rows, 0:BLOCK]
                + hoop_rate * dth_s[member, rows, :]
                + u_z * grad_s[member, rows, BLOCK : 2 * BLOCK]
            )
            relaxing = ((1.0 - MOBILITY) * inv_relax) * inverse[member] - (
                MOBILITY * inv_relax
            ) * conform_ref[member, rows, :]
            rate = (turning[member] - advect) + (strain[member] + relaxing)
            put(rate_h, rate_l, rows, lanes_of(member), rate)

    row_chunks(planes, rows_step, chunk)
    back = (back_high_ref[:, :planes], back_low_ref[:, :planes])
    for pair in range(3):
        lanes = slice(2 * pair * BLOCK, (2 * pair + 2) * BLOCK)
        coeffs[:, lanes] = dot3(back, (rate_h[:, lanes], rate_l[:, lanes]))
    for field in range(6):
        route.store(me_ref, [out_ref], field, coeffs.at[:, lanes_of(field)])


def advance_body(layers, step, route, count, *refs):
    me_ref, orient_ref, wall_ref = refs[:3]
    rate_refs, (mean_ref, old_ref, out_ref, rates) = refs[3 : 3 + count], refs[3 + count :]
    fields, local_modes = old_ref.shape[0], old_ref.shape[1]
    aligned = rates.dtype == BF16
    rows = fields * local_modes

    @pl.when(pl.program_id(0) == 0)
    def _():
        for array, place, rel in route.land:
            layer = route.index(me_ref, rel)
            if aligned:
                high, low = split(rate_refs[array][place].reshape(rows, BLOCK))
                rates[layer + 1, :rows, :] = high
                rates[layer + 1, rows:, :] = low
            else:
                rates[layer + 1] = rate_refs[array][place]
        rates[0] = rates[layers]
        rates[layers + 1] = rates[1]

    first = pl.program_id(0) * step

    def averaged(index, at, field):
        total = None
        for number in range(3):
            high, low = split(rates[index + number, field])
            weights = mean_ref[at, number * BLOCK : (number + 1) * BLOCK, :]
            part = dot(high, weights) + dot(low, weights)
            total = part if total is None else total + part
        return total

    for at in range(step):
        index = first + at
        lanes = lanes_of(at)
        if aligned:
            near = jnp.concatenate([rates[index + number] for number in range(3)], axis=1)
            every = dot(near, mean_ref[at])
            every = every[:rows] + every[rows:]
            change = [every[f * local_modes : (f + 1) * local_modes] for f in range(fields)]
        else:
            change = [averaged(index, at, f) for f in range(fields)]
        shape = (local_modes, BLOCK)
        column = places(orient_ref, index, shape) & (RADIAL - 1)
        inner = column == 0
        on_wall = jnp.logical_or(inner, column == RADIAL - 1)
        mean_row = jnp.logical_and(lax.broadcasted_iota(jnp.int32, shape, 0) == 0, inner)
        driven = jnp.where(mean_row, wall_ref[0], 0.0)
        for field in range(fields):
            stepped = old_ref[field, :, lanes] + STEP_DT * change[field]
            if fields == 3:
                stepped = jnp.where(on_wall, driven if field == 1 else 0.0, stepped)
            out_ref[field, :, lanes] = stepped


def advance(rates, route, weights, old, me, orientation, wall):
    fields, local_modes, nodes = old.shape
    layers = nodes // BLOCK
    step = 16
    block = pl.BlockSpec((fields, local_modes, step * BLOCK), lambda i: (0, 0, i))
    scalar = pl.BlockSpec(memory_space=pltpu.SMEM)
    return pl.pallas_call(
        functools.partial(advance_body, layers, step, route, len(rates)),
        grid=(layers // step,),
        in_specs=[scalar] * 3
        + [pl.BlockSpec(part.shape, lambda i: (0, 0, 0, 0)) for part in rates]
        + [pl.BlockSpec((step, 3 * BLOCK, BLOCK), lambda i: (i, 0, 0)), block],
        out_specs=block,
        out_shape=jax.ShapeDtypeStruct(old.shape, F32),
        scratch_shapes=[
            pltpu.VMEM((layers + 2, 2 * fields * local_modes, BLOCK), BF16)
            if local_modes % 16 == 0
            else pltpu.VMEM((layers + 2, fields, local_modes, BLOCK), F32)
        ],
        compiler_params=pltpu.CompilerParams(vmem_limit_bytes=24 * MIB),
        name="advance",
    )(me, orientation, wall, *rates, weights, old)


def body(velocity, log_conf, orientation, wall_speed):
    devices = lax.axis_size("mode")
    device = lax.axis_index("mode").astype(jnp.int32)
    me = device.reshape(1)
    local_modes = velocity.shape[1]
    layers = velocity.shape[2] // BLOCK
    planes = local_modes * devices
    far_first = Route(devices, local_modes, True)
    near_first = Route(devices, local_modes, False)
    whole = Route(devices, local_modes, False, False)
    barrier = lax.optimization_barrier
    staged = far_first.staged
    both, faces, halos, means, inv_r_nodes = node_tables()

    def parts(tables):
        return jnp.asarray(np.stack([half for table in tables for half in split_table(table)]))

    fourier = fourier_tables(planes)
    high, low = (jnp.asarray(half) for half in split_table(fourier))
    signed = np.concatenate([fourier[:planes].T, -fourier[planes:].T], axis=1)
    back_high, back_low = (jnp.asarray(half) for half in split_table(signed))
    inv_r_table = jnp.asarray(np.tile(inv_r_nodes[:, None], (1, BLOCK)), F32)

    both_s, faces_s, halos_s, inv_r = kernel_call(
        order_body,
        (
            jax.ShapeDtypeStruct((10, BLOCK, BLOCK), BF16),
            jax.ShapeDtypeStruct((24, BLOCK, 2 * BLOCK), BF16),
            jax.ShapeDtypeStruct((10, 2 * BLOCK, 2 * BLOCK), BF16),
            jax.ShapeDtypeStruct((8, BLOCK), F32),
        ),
        4,
        scalars=2,
        vmem=16,
        name="order",
    )(me, orientation, parts(both), parts(faces), parts(halos), inv_r_table)
    weights = kernel_call(
        functools.partial(weights_body, layers),
        jax.ShapeDtypeStruct((layers, 3 * BLOCK, BLOCK), BF16),
        1,
        vmem=8 + layers // 8,
        name="weights",
    )(orientation, jnp.asarray(means, BF16))

    vel_nodes, psi_nodes = pack(me, (velocity, log_conf), (far_first, near_first))
    fixed = (both_s, faces_s, halos_s, inv_r, weights)
    if staged:
        psi_nodes = near_swaps(psi_nodes)
        vel_nodes = far_swaps(vel_nodes, psi_nodes)
        vel_nodes, psi_nodes, fixed = barrier((vel_nodes, psi_nodes, fixed))
        vel_nodes = near_swaps(regroup(vel_nodes))
        first_nodes = far_swaps(regroup([group[:, :FIRST] for group in psi_nodes]))
        second_nodes = regroup([group[:, FIRST:] for group in psi_nodes])
    else:
        vel_nodes = far_first.unpacked(in_one(vel_nodes))
        psi_nodes = near_first.unpacked(in_one(psi_nodes))
        first_nodes = [group[:, :FIRST] for group in psi_nodes]
        second_nodes = [group[:, FIRST:] for group in psi_nodes]

    both_s, faces_s, halos_s, inv_r, weights = fixed
    edge = jax.ShapeDtypeStruct((planes // 4 * 3, BLOCK), F32)
    vel_half = jax.ShapeDtypeStruct((planes, 3 * BLOCK), BF16)
    to_up, to_down, vel_h, vel_l = kernel_call(
        functools.partial(face_body, far_first, len(vel_nodes)),
        (edge, edge, vel_half, vel_half),
        len(vel_nodes) + 1,
        vmem=16,
        name="faces",
    )(me, *vel_nodes, faces_s)
    up = [(i, (i + 1) % devices) for i in range(devices)]
    below = lax.ppermute(to_up, "mode", up)
    above = lax.ppermute(to_down, "mode", [(j, i) for i, j in up])

    def halves(fields):
        return (
            jax.ShapeDtypeStruct((planes, fields * BLOCK), BF16),
            jax.ShapeDtypeStruct((planes, fields * BLOCK), BF16),
            jax.ShapeDtypeStruct((fields, planes, BLOCK), F32),
        )

    vel, own_flow, first_h, first_l, first = kernel_call(
        functools.partial(velocity_body, near_first, len(first_nodes)),
        (
            jax.ShapeDtypeStruct((3, planes, BLOCK), F32),
            jax.ShapeDtypeStruct((15, planes, BLOCK), F32),
            *halves(FIRST),
        ),
        len(first_nodes) + 6,
        scratch=[pltpu.VMEM((2 * planes, 3 * BLOCK), F32)],
        vmem=20,
        name="velocity",
    )(me, *first_nodes, vel_h, vel_l, high, low, both_s, inv_r)
    if staged:
        early = second_nodes
        second_nodes, below, above, vel = barrier((second_nodes, below, above, vel))
        second_nodes = far_swaps([early[0], second_nodes[1], early[2], early[3]])
    halo_flow = kernel_call(
        halo_body,
        jax.ShapeDtypeStruct((12, planes, BLOCK), F32),
        7,
        scalars=0,
        scratch=[pltpu.VMEM((2 * planes, 2 * BLOCK), F32)],
        vmem=24,
        name="halo",
    )(below, above, vel, high, low, halos_s, jnp.asarray(free_places(), BF16))

    far_outs = far_first.outs(far_first.leave, 3, far_first.modes, BLOCK)
    psi_outs = whole.outs(whole.leave, 6, whole.modes, BLOCK)
    field6 = jax.ShapeDtypeStruct((6, planes, BLOCK), F32)
    *vel_rates, second_h, second_l, second, conform = kernel_call(
        functools.partial(
            momentum_body, near_first, len(second_nodes), far_first, len(far_outs)
        ),
        (*far_outs, *halves(6 - FIRST), field6),
        len(second_nodes) + 9,
        scratch=[
            pltpu.VMEM((planes, 6 * BLOCK), BF16),
            pltpu.VMEM((planes, 6 * BLOCK), BF16),
            pltpu.VMEM((2 * planes, 3 * BLOCK), BF16),
            pltpu.VMEM((2 * planes, 3 * BLOCK), BF16),
            pltpu.VMEM((3, planes, BLOCK), F32),
            pltpu.VMEM((planes, 3 * BLOCK), F32),
        ],
        vmem=24,
        name="momentum",
    )(me, *second_nodes, first, own_flow, halo_flow, high, low, back_high, back_low, both_s, inv_r)
    vel_rates = far_first.packed(vel_rates)
    psi_rates = kernel_call(
        functools.partial(elastic_body, whole),
        (*psi_outs,),
        14,
        scratch=[
            pltpu.VMEM((6, planes, BLOCK), F32),
            pltpu.VMEM((6, planes, 2 * BLOCK), F32),
            pltpu.VMEM((planes, 6 * BLOCK), BF16),
            pltpu.VMEM((planes, 6 * BLOCK), BF16),
            pltpu.VMEM((planes, 6 * BLOCK), F32),
        ],
        vmem=24,
        name="elastic",
    )(
        me, first_h, first_l, second_h, second_l, first, second, conform, own_flow, halo_flow, high, low,
        back_high, back_low, both_s,
    )

    psi_rates = whole.packed(psi_rates)
    if staged:
        vel_rates, psi_rates = barrier((far_swaps(vel_rates), psi_rates))
        vel_rates = near_swaps(regroup(vel_rates))
    else:
        vel_rates = in_one(vel_rates)
    psi_rates = in_one(psi_rates)
    wall = jnp.where(device == 0, wall_speed, 0.0)
    at_walls = (me, orientation, wall)
    vel_next = advance(vel_rates, far_first, weights, velocity, *at_walls)
    logc_next = advance(psi_rates, whole, weights, log_conf, *at_walls)
    return vel_next, logc_next


def solution(mesh):
    in_specs = (P("ens", "mode", None), P("ens", "mode", None), P(), P("ens"))
    out_specs = (P("ens", "mode", None), P("ens", "mode", None))
    return jax.shard_map(body, mesh=mesh, in_specs=in_specs, out_specs=out_specs, check_vma=False)
```

```python
import functools

import jax
import jax.numpy as jnp
import ml_dtypes
import numpy as np
from jax import lax
from jax.experimental import pallas as pl
from jax.experimental.pallas import tpu as pltpu
from jax.sharding import PartitionSpec as P

SIDE = 8
CYCLES = 2
RADIAL = SIDE * CYCLES
BLOCK = SIDE * RADIAL
STEP_DT = 0.002
RELAX_TIME = 0.02
MOBILITY = 0.3
LAYER_HEIGHT = 0.25
R_INNER = 1.0
MIB = 1 << 20
F32 = jnp.float32
BF16 = jnp.bfloat16


def split_table(table):
    high = np.asarray(table, np.float32).astype(ml_dtypes.bfloat16)
    low = (np.asarray(table, np.float64) - high.astype(np.float64)).astype(ml_dtypes.bfloat16)
    return high, low


def cheb_table(points):
    nodes_xi = -np.cos(np.pi * np.arange(points) / (points - 1))
    weights = np.ones(points)
    weights[0] = 2.0
    weights[-1] = 2.0
    weights = weights * (-1.0) ** np.arange(points)
    identity = np.eye(points)
    spacing = nodes_xi[:, None] - nodes_xi[None, :] + identity
    matrix = weights[:, None] / weights[None, :] / spacing
    matrix = matrix * (1.0 - identity)
    matrix = matrix - identity * matrix.sum(axis=1)[:, None]
    return nodes_xi, matrix


def fourier_tables(planes):
    phase = np.arange(planes)[:, None] * np.arange(planes // 2)[None, :] % planes
    angles = phase * (2.0 * np.pi / planes)
    cosine = np.cos(angles) * np.sqrt(2.0 / planes)
    sine = np.sin(angles) * np.sqrt(2.0 / planes)
    cosine[:, 0] = planes**-0.5
    sine[:, 0] = (-1.0) ** np.arange(planes) * planes**-0.5
    wavenums = np.arange(planes // 2)
    basis = np.stack([cosine, sine], axis=2).reshape(planes, planes)
    turned = np.stack([-wavenums * sine, wavenums * cosine], axis=2).reshape(planes, planes)
    return np.concatenate([basis, turned], axis=0)


def node_tables():
    nodes_xi, matrix = cheb_table(SIDE)
    radius = R_INNER + (np.arange(CYCLES)[:, None] + (nodes_xi[None, :] + 1.0) / 2.0) / CYCLES
    inv_r = 1.0 / radius.reshape(-1)
    radial_row = np.kron(np.eye(CYCLES), matrix.T * (2.0 * CYCLES))
    radial_mean = np.eye(RADIAL)
    for cycle in range(1, CYCLES):
        low, high = cycle * SIDE - 1, cycle * SIDE
        radial_mean[low : high + 1, low : high + 1] = 0.5
    d_radial = np.kron(np.eye(SIDE), radial_row)
    d_axial = np.kron(matrix.T * (2.0 / LAYER_HEIGHT), np.eye(RADIAL))
    own_weight = np.ones(SIDE)
    own_weight[[0, -1]] = 0.5
    average = np.kron(np.diag(own_weight), radial_mean)
    inv_r_nodes = np.tile(inv_r, SIDE)
    both = np.stack(
        [d_radial, d_axial, d_radial @ average, d_axial @ average, average * inv_r_nodes[None, :]]
    )
    below = np.zeros((SIDE, SIDE))
    below[SIDE - 1, 0] = 0.5
    means = np.stack([np.kron(below, radial_mean), average, np.kron(below.T, radial_mean)])
    faces = np.zeros((3, BLOCK, 2 * BLOCK))
    halos = np.zeros((9, 2 * BLOCK, BLOCK))
    for field in range(3):
        for side, row in ((0, SIDE - 1), (1, 0)):
            at_u = side * BLOCK + field * RADIAL
            at_dz = at_u + 3 * RADIAL
            face_nodes = slice(row * RADIAL, (row + 1) * RADIAL)
            faces[field, face_nodes, at_u : at_u + RADIAL] = np.eye(RADIAL)
            faces[field, :, at_dz : at_dz + RADIAL] = d_axial[:, face_nodes]
            here = SIDE - 1 - row
            out = slice(here * RADIAL, (here + 1) * RADIAL)
            halos[field, at_u : at_u + RADIAL, out] = 0.5 * radial_row @ radial_mean
            halos[3 + field, at_dz : at_dz + RADIAL, out] = 0.5 * radial_mean
            halos[6 + field, at_u : at_u + RADIAL, out] = 0.5 * radial_mean * inv_r[None, :]
    used = 6 * RADIAL
    packed = [faces]
    for number in range(3):
        variant = np.zeros_like(faces)
        for side in (0, BLOCK):
            group = slice(side + number * (BLOCK - used), side + (number + 1) * (BLOCK - used))
            variant[:, :, side + used : side + BLOCK] = faces[:, :, group]
        packed.append(variant)
    return both, np.concatenate(packed), halos, means, inv_r_nodes


def free_places():
    used = 6 * RADIAL
    free = BLOCK - used
    moves = np.zeros((3, BLOCK, BLOCK))
    for number in range(3):
        moves[number, used:, number * free : (number + 1) * free] = np.eye(free)
    return moves


def split(values):
    high = values.astype(BF16)
    return high, (values - high.astype(F32)).astype(BF16)


def dot(left, right):
    return jnp.dot(left, right, preferred_element_type=F32)


def dot3(left, right):
    width = right[0].shape[1]
    if width > BLOCK:
        return dot(left[0], right[0]) + (dot(left[0], right[1]) + dot(left[1], right[0]))
    both = dot(left[0], jnp.concatenate(right, axis=1))
    return both[:, :width] + (both[:, width:] + dot(left[1], right[0]))


def whole_spec():
    return pl.BlockSpec(memory_space=pltpu.VMEM)


def kernel_call(
    body, outs, count, scalars=1, scratch=(), vmem=40, name=None
):
    return pl.pallas_call(
        body,
        out_shape=outs,
        in_specs=[pl.BlockSpec(memory_space=pltpu.SMEM)] * scalars + [whole_spec()] * count,
        out_specs=jax.tree.map(lambda _: whole_spec(), outs),
        scratch_shapes=list(scratch),
        compiler_params=pltpu.CompilerParams(vmem_limit_bytes=vmem * MIB),
        name=name,
    )


def lanes_of(at):
    return slice(at * BLOCK, (at + 1) * BLOCK)


def put(high, low, rows, lanes, value):
    value_h, value_l = split(value)
    high[rows, lanes] = value_h
    low[rows, lanes] = value_l


NEAR = 4


def swap(block, bits):
    devices = lax.axis_size("mode")
    return lax.ppermute(block, "mode", [(i, i ^ bits) for i in range(devices)])


def after(block, token):
    return lax.optimization_barrier((block, token))[0]


def near_swaps(groups):
    return [groups[0]] + [swap(groups[t], t) for t in (1, 2, 3)]


def far_swaps(groups, beside=None):
    first = groups[1] if beside is None else after(groups[1], beside[1])
    return [groups[0], swap(first, NEAR)] + [swap(groups[s], NEAR * s) for s in (2, 3)]


def regroup(groups):
    return [jnp.stack([group[at] for group in groups]) for at in range(NEAR)]


class Route:
    def __init__(self, devices, local_modes, far_first, staged=True):
        self.staged = staged and devices == NEAR * NEAR and local_modes % 16 == 0
        self.aligned = self.staged or local_modes % 16 == 0
        self.devices, self.local_modes, self.far_first = devices, local_modes, far_first
        self.modes = local_modes if self.aligned else local_modes * devices
        if not self.staged:
            self.pack = self.land = [(0, at, at) for at in range(devices)]
            self.leave = self.arrive = self.pack if self.aligned else [(0, 0, 0)]
            return
        far = [(s, t, NEAR * s + t) for s in range(NEAR) for t in range(NEAR)]
        near = [(t, s, NEAR * s + t) for s in range(NEAR) for t in range(NEAR)]
        self.pack = self.leave = far if far_first else near
        self.land = self.arrive = near if far_first else far

    def outs(self, blocks, *block):
        arrays, places = (1 + max(entry[at] for entry in blocks) for at in range(2))
        return [jax.ShapeDtypeStruct((places,) + block, F32)] * arrays

    def index(self, me_ref, rel):
        return (me_ref[0] ^ rel) if self.staged else rel

    def rows(self, me_ref, rel):
        start = self.index(me_ref, rel) * self.modes
        return pl.ds(pl.multiple_of(start, self.modes), self.modes)

    def load(self, me_ref, refs, high, low):
        for array, place, rel in self.arrive:
            rows = self.rows(me_ref, rel)
            for field in range(refs[array].shape[1]):
                put(high, low, rows, lanes_of(field), refs[array][place, field])

    def store(self, me_ref, refs, field, coeffs):
        for array, place, rel in self.leave:
            refs[array][place, field] = coeffs[self.rows(me_ref, rel), :]

    def packed(self, arrays):
        if self.aligned:
            return arrays
        _, fields, planes, nodes = arrays[0].shape
        blocks = arrays[0].reshape(fields, planes // self.local_modes, self.local_modes, nodes)
        return [blocks.transpose(1, 0, 2, 3)]

    def unpacked(self, arrays):
        if self.aligned:
            return arrays
        devices, fields, modes, nodes = arrays[0].shape
        return [arrays[0].transpose(1, 0, 2, 3).reshape(1, fields, devices * modes, nodes)]


def in_one(arrays):
    return [lax.all_to_all(arrays[0], "mode", split_axis=0, concat_axis=0, tiled=True)]


def pack(me, values, routes):
    outs, copies = [], []
    for at, (array, route) in enumerate(zip(values, routes)):
        fields, local_modes, _ = array.shape
        copies += [(at, len(outs) + out, place, rel) for out, place, rel in route.pack]
        outs += route.outs(route.pack, fields, local_modes, BLOCK)
    count = len(values)

    def body(me_ref, *refs):
        in_refs, out_refs, sems = refs[:count], refs[count:-1], refs[-1]
        started = []
        for number, (at, out, place, rel) in enumerate(copies):
            layer = routes[at].index(me_ref, rel)
            lanes = pl.ds(pl.multiple_of(layer * BLOCK, BLOCK), BLOCK)
            copy = pltpu.make_async_copy(
                in_refs[at].at[:, :, lanes], out_refs[out].at[place], sems.at[number]
            )
            copy.start()
            started.append(copy)
        for copy in started:
            copy.wait()

    packed = pl.pallas_call(
        body,
        in_specs=[pl.BlockSpec(memory_space=pltpu.SMEM)]
        + [pl.BlockSpec(memory_space=pl.ANY)] * count,
        out_specs=[whole_spec()] * len(outs),
        out_shape=outs,
        scratch_shapes=[pltpu.SemaphoreType.DMA((len(copies),))],
        name="pack",
    )(me, *values)
    first = len(routes[0].outs(routes[0].pack, 1))
    return packed[:first], packed[first:]


def places(orient_ref, layer, shape):
    lane = lax.broadcasted_iota(jnp.int32, shape, 1)
    cycle = lane >> 6
    orient = jnp.where(
        cycle == 0, orient_ref[CYCLES * layer], orient_ref[CYCLES * layer + 1]
    )
    lead, trail = (lane >> 3) & 7, lane & 7
    lead = jnp.where((orient & 1) == 1, SIDE - 1 - lead, lead)
    trail = jnp.where((orient & 2) == 2, SIDE - 1 - trail, trail)
    swapped = (orient & 4) == 4
    row = jnp.where(swapped, trail, lead)
    col = jnp.where(swapped, lead, trail)
    return row * RADIAL + cycle * SIDE + col


def from_grid(orient_ref, layer):
    shape = (BLOCK, BLOCK)
    grid_ids = lax.broadcasted_iota(jnp.int32, shape, 0)
    return (grid_ids == places(orient_ref, layer, shape)).astype(F32)


def order_body(
    me_ref, orient_ref, both_ref, faces_ref, halos_ref, inv_r_ref,
    both_out, faces_out, halos_out, inv_r_out,
):
    onto = from_grid(orient_ref, me_ref[0])
    inv_r_out[...] = jnp.broadcast_to(
        jnp.sum(onto * inv_r_ref[...], axis=0, keepdims=True), inv_r_out.shape
    )
    back = onto.T.astype(BF16)
    onto = onto.astype(BF16)
    for at in range(both_ref.shape[0]):
        moved = dot(both_ref[at], onto).astype(BF16)
        both_out[at] = dot(back, moved).astype(BF16)
    for at in range(faces_ref.shape[0]):
        faces_out[at] = dot(back, faces_ref[at]).astype(BF16)
    pairs = ((0, 3), (1, 4), (2, 5), (6, 7), (8, 8))
    for at, pair in enumerate(pairs):
        for half in range(2):
            for side in range(2):
                placed = dot(halos_ref[2 * pair[side] + half], onto).astype(BF16)
                halos_out[2 * at + half, :, side * BLOCK : (side + 1) * BLOCK] = placed


def weights_body(layers, orient_ref, means_ref, out_ref):
    def one(index, carry):
        onto = from_grid(orient_ref, index).astype(BF16)
        below = lax.rem(index + (layers - 1), layers)
        above = lax.rem(index + 1, layers)
        for number, layer in enumerate((below, index, above)):
            back = from_grid(orient_ref, layer).T.astype(BF16)
            moved = dot(means_ref[number], onto).astype(BF16)
            out_ref[index, number * BLOCK : (number + 1) * BLOCK, :] = dot(back, moved).astype(BF16)
        return carry

    lax.fori_loop(0, layers, one, 0)


def face_body(route, count, me_ref, *refs):
    vel_refs, (faces_ref, up_ref, down_ref, high, low) = refs[:count], refs[count:]
    route.load(me_ref, vel_refs, high, low)
    quarter = high.shape[0] // 4

    def faces(rows, variant):
        total = None
        for field in range(3):
            lanes, at = lanes_of(field), 6 * variant + 2 * field
            part = dot3((high[rows, lanes], low[rows, lanes]), (faces_ref[at], faces_ref[at + 1]))
            total = part if total is None else total + part
        return total

    for number in range(3):
        rows = slice(number * quarter, (number + 1) * quarter)
        total = faces(rows, 0) + faces(slice(3 * quarter, 4 * quarter), 1 + number)
        up_ref[rows, :] = total[:, :BLOCK]
        down_ref[rows, :] = total[:, BLOCK:]


FIRST = 3


def members_of(first_ref, second_ref, rows):
    return [ref[at, rows, :] for ref in (first_ref, second_ref) for at in range(ref.shape[0])]


def transform(high_ref, low_ref, rows, coef_h, coef_l, out_ref):
    table = (high_ref[rows, :], low_ref[rows, :])
    fields = out_ref.shape[0]
    for start in range(0, fields, 2):
        stop = min(start + 2, fields)
        lanes = slice(start * BLOCK, stop * BLOCK)
        values = dot3(table, (coef_h[:, lanes], coef_l[:, lanes]))
        for at in range(start, stop):
            out_ref[at] = values[:, lanes_of(at - start)]


def flow_parts(g_r, g_t, g_z, u):
    return (
        0.5 * (g_t[0] - g_r[1]),
        0.5 * (g_z[0] - g_r[2]),
        0.5 * (g_z[1] - g_t[2]),
        2.0 * g_r[0],
        g_t[0] + g_r[1],
        g_z[0] + g_r[2],
        2.0 * g_t[1],
        g_z[1] + g_t[2],
        2.0 * g_z[2],
        -(g_r[0] * u[0] + g_t[0] * u[1] + g_z[0] * u[2]),
        -(g_r[1] * u[0] + g_t[1] * u[1] + g_z[1] * u[2]),
        -(g_r[2] * u[0] + g_t[2] * u[1] + g_z[2] * u[2]),
    )


def matrix_of(ref, at):
    return ref[2 * at], ref[2 * at + 1]


def velocity_body(route, count, me_ref, *refs):
    psi_refs, refs = refs[:count], refs[count:]
    vel_h, vel_l, high_ref, low_ref, both_ref, inv_r_ref, vel_ref, flow_ref = refs[:8]
    coef_h, coef_l, psi_out, values = refs[8:]
    planes = high_ref.shape[1]
    route.load(me_ref, psi_refs, coef_h, coef_l)
    transform(high_ref, low_ref, slice(0, planes), coef_h, coef_l, psi_out)
    table = (high_ref[...], low_ref[...])
    values[:, 0:256] = dot3(table, (vel_h[:, 0:256], vel_l[:, 0:256]))
    values[:, 256:384] = dot3(table, (vel_h[:, 256:384], vel_l[:, 256:384]))
    rows_step = 256

    def chunk(start):
        rows = pl.ds(start, rows_step)
        turned = pl.ds(pl.multiple_of(planes + start, rows_step), rows_step)
        u = [values[rows, lanes_of(f)] for f in range(3)]
        u_s = [split(v) for v in u]
        dth_s = [split(values[turned, lanes_of(f)]) for f in range(3)]
        g_r = [dot3(u_s[f], matrix_of(both_ref, 2)) for f in range(3)]
        g_z = [dot3(u_s[f], matrix_of(both_ref, 3)) for f in range(3)]
        g_t = [dot3(dth_s[f], matrix_of(both_ref, 4)) for f in range(3)]
        g_t[0] = g_t[0] - dot3(u_s[1], matrix_of(both_ref, 4))
        g_t[1] = g_t[1] + dot3(u_s[0], matrix_of(both_ref, 4))
        hoop_rate = u[1] * inv_r_ref[0:1, :]
        parts = flow_parts(g_r, g_t, g_z, u)
        rest = (1.0 - 2.0 * MOBILITY) / RELAX_TIME
        for f in range(3):
            vel_ref[f, rows, :] = u[f]
        for at, part in enumerate((u[0], hoop_rate, u[2]) + parts):
            if at == 3:
                part = part + hoop_rate
            if at - 6 in DIAGONAL:
                part = part - rest
            flow_ref[at, rows, :] = part

    row_chunks(planes, rows_step, chunk)


def halo_body(
    below_ref, above_ref, vel_ref, high_ref, low_ref, halos_ref, places_ref, part_ref, values
):
    planes = high_ref.shape[1]
    quarter = planes // 4
    edges = []
    for ref in (below_ref, above_ref):
        last = None
        for number in range(3):
            part = split(ref[number * quarter : (number + 1) * quarter, :])
            part = dot(part[0], places_ref[number]) + dot(part[1], places_ref[number])
            last = part if last is None else last + part
        edges.append(jnp.concatenate([ref[...], last], axis=0))
    values[...] = dot3((high_ref[...], low_ref[...]), split(jnp.concatenate(edges, axis=1)))
    rows_step = planes // 2

    def chunk(start):
        rows = pl.ds(start, rows_step)
        turned = pl.ds(pl.multiple_of(planes + start, rows_step), rows_step)
        edge, edge_dth = split(values[rows, :]), split(values[turned, :])
        g_r, g_z = zip(*(halved(dot3(edge, matrix_of(halos_ref, f))) for f in range(3)))
        g_t = [
            *halved(dot3(edge_dth, matrix_of(halos_ref, 3))),
            dot3(edge_dth, (halos_ref[8, :, :BLOCK], halos_ref[9, :, :BLOCK])),
        ]
        mean_r, mean_t = halved(dot3(edge, matrix_of(halos_ref, 3)))
        g_t[0] = g_t[0] - mean_t
        g_t[1] = g_t[1] + mean_r
        u = [vel_ref[f, rows, :] for f in range(3)]
        for at, part in enumerate(flow_parts(g_r, g_t, g_z, u)):
            part_ref[at, rows, :] = part

    row_chunks(planes, rows_step, chunk)


def halved(pair):
    return pair[:, :BLOCK], pair[:, BLOCK:]


def square(m):
    a, b, c, d, e, f = m
    bb, cc, ee = b * b, c * c, e * e
    return (
        a * a + (bb + cc),
        b * (a + d) + c * e,
        c * (a + f) + b * e,
        d * d + (bb + ee),
        e * (d + f) + b * c,
        f * f + (cc + ee),
    )


def commuting_product(m, n):
    a, b, c, d, e, f = m
    p, q, r, s, t, u = n
    return (
        a * p + b * q + c * r,
        a * q + b * s + c * t,
        a * r + b * t + c * u,
        b * q + d * s + e * t,
        b * r + d * t + e * u,
        c * r + e * t + f * u,
    )


DIAGONAL = (0, 3, 5)


def plus_identity(m):
    return tuple(v + 1.0 if at in DIAGONAL else v for at, v in enumerate(m))


def exponential(psi, sign):
    square_2 = square(psi)
    square_4 = square(square_2)
    even = plus_identity(
        tuple(v * (0.5 / 64.0) + w * (1.0 / 24.0 / 4096.0) for v, w in zip(square_2, square_4))
    )
    factor = tuple(v * (sign / 6.0 / 512.0) for v in square_2)
    factor = tuple(v + sign * 0.125 if at in DIAGONAL else v for at, v in enumerate(factor))
    odd = commuting_product(psi, factor)
    total = tuple(v + w for v, w in zip(even, odd))
    for _ in range(3):
        total = square(total)
    return total


def row_chunks(planes, rows_step, body):
    def chunk(step, carry):
        body(pl.multiple_of(step * rows_step, rows_step))
        return carry

    lax.fori_loop(0, planes // rows_step, chunk, 0)


def momentum_body(route, count, out_route, out_count, me_ref, *refs):
    psi_refs, refs = refs[:count], refs[count:]
    first_ref, flow_ref, halo_ref, high_ref, low_ref = refs[:5]
    back_high_ref, back_low_ref, both_ref, inv_r_ref = refs[5:9]
    out_refs, refs = refs[9 : 9 + out_count], refs[9 + out_count :]
    coef_h, coef_l, psi_out, conform_out, stress_h, stress_l, vel_h, vel_l, mom_s, coeffs = refs
    planes = high_ref.shape[1]
    route.load(me_ref, psi_refs, coef_h, coef_l)
    transform(high_ref, low_ref, slice(0, planes), coef_h, coef_l, psi_out)
    rows_step = 32

    def chunk(start):
        rows = pl.ds(start, rows_step)
        inv_r = inv_r_ref[0:1, :]
        psi = members_of(first_ref, psi_out, rows)
        conform = exponential(psi, 1.0)
        for member in range(6):
            conform_out[member, rows, :] = conform[member]
        stress = tuple(v - 1.0 if at in DIAGONAL else v for at, v in enumerate(conform))
        for member, at in ((0, (0,)), (2, (1, 4)), (1, (2,)), (4, (3,)), (5, (5,))):
            high, low = split(stress[member])
            for lane in at:
                stress_h[rows, lanes_of(lane)] = high
                stress_l[rows, lanes_of(lane)] = low
        hoop = tuple(stress[at] * inv_r for at in (1, 3, 4))
        turned = pl.ds(pl.multiple_of(planes + start, rows_step), rows_step)
        for at in range(3):
            put(vel_h, vel_l, turned, lanes_of(at), hoop[at])
        carried = [flow_ref[12 + at, rows, :] + halo_ref[9 + at, rows, :] for at in range(3)]
        mom_s[0, rows, :] = carried[0] + (stress[0] * inv_r - hoop[1])
        mom_s[1, rows, :] = carried[1] + 2.0 * hoop[0]
        mom_s[2, rows, :] = carried[2] + stress[2] * inv_r

    row_chunks(planes, rows_step, chunk)
    divergence = tuple(
        jnp.concatenate([both_ref[at], both_ref[2 + at]], axis=0) for at in range(2)
    )
    for at in range(3):
        lanes = slice(2 * at * BLOCK, (2 * at + 2) * BLOCK)
        force = dot3((stress_h[:, lanes], stress_l[:, lanes]), divergence)
        put(vel_h, vel_l, slice(0, planes), lanes_of(at), mom_s[at] + force)
    back = (back_high_ref[...], back_low_ref[...])
    for start, stop in ((0, 2), (2, 3)):
        lanes = slice(start * BLOCK, stop * BLOCK)
        coeffs[:, lanes] = dot3(back, (vel_h[:, lanes], vel_l[:, lanes]))
    for field in range(3):
        out_route.store(me_ref, out_refs, field, coeffs.at[:, lanes_of(field)])


def elastic_body(route, me_ref, *refs):
    (
        first_h, first_l, second_h, second_l, first_ref, second_ref, conform_ref, flow_ref,
        halo_ref, high_ref, low_ref, back_high_ref, back_low_ref, both_ref,
    ) = refs[:14]
    out_ref, dth_s, grad_s, rate_h, rate_l, coeffs = refs[14:]
    planes = high_ref.shape[1]
    turned = slice(planes, 2 * planes)
    transform(high_ref, low_ref, turned, first_h, first_l, dth_s.at[pl.ds(0, FIRST)])
    transform(high_ref, low_ref, turned, second_h, second_l, dth_s.at[pl.ds(FIRST, 6 - FIRST)])
    gradient = tuple(
        jnp.concatenate([both_ref[at], both_ref[2 + at]], axis=1) for at in range(2)
    )
    for member in range(6):
        psi_ref = first_ref if member < FIRST else second_ref
        grad_s[member] = dot3(split(psi_ref[member % FIRST]), gradient)
    rows_step = 32
    inv_relax = 1.0 / RELAX_TIME

    def chunk(start):
        rows = pl.ds(start, rows_step)
        psi = members_of(first_ref, second_ref, rows)
        inverse = exponential(psi, -1.0)
        u_r, hoop_rate, u_z = (flow_ref[at, rows, :] for at in range(3))
        p, q, s, *strain = (
            flow_ref[3 + at, rows, :] + halo_ref[at, rows, :] for at in range(9)
        )
        a, b, c, d, e, f = psi
        pb, qc, se = p * b, q * c, s * e
        turning = (
            2.0 * (pb + qc),
            p * (d - a) + (q * e + s * c),
            q * (f - a) + (p * e - s * b),
            2.0 * (se - pb),
            s * (f - d) - (p * c + q * b),
            -2.0 * (qc + se),
        )
        for member in range(6):
            advect = (
                u_r * grad_s[member, rows, 0:BLOCK]
                + hoop_rate * dth_s[member, rows, :]
                + u_z * grad_s[member, rows, BLOCK : 2 * BLOCK]
            )
            relaxing = ((1.0 - MOBILITY) * inv_relax) * inverse[member] - (
                MOBILITY * inv_relax
            ) * conform_ref[member, rows, :]
            rate = (turning[member] - advect) + (strain[member] + relaxing)
            put(rate_h, rate_l, rows, lanes_of(member), rate)

    row_chunks(planes, rows_step, chunk)
    back = (back_high_ref[:, :planes], back_low_ref[:, :planes])
    for pair in range(3):
        lanes = slice(2 * pair * BLOCK, (2 * pair + 2) * BLOCK)
        coeffs[:, lanes] = dot3(back, (rate_h[:, lanes], rate_l[:, lanes]))
    for field in range(6):
        route.store(me_ref, [out_ref], field, coeffs.at[:, lanes_of(field)])


def advance_body(layers, step, route, count, *refs):
    me_ref, orient_ref, wall_ref = refs[:3]
    rate_refs, (mean_ref, old_ref, out_ref, rates) = refs[3 : 3 + count], refs[3 + count :]
    fields, local_modes = old_ref.shape[0], old_ref.shape[1]
    aligned = rates.dtype == BF16
    rows = fields * local_modes

    @pl.when(pl.program_id(0) == 0)
    def _():
        for array, place, rel in route.land:
            layer = route.index(me_ref, rel)
            if aligned:
                high, low = split(rate_refs[array][place].reshape(rows, BLOCK))
                rates[layer + 1, :rows, :] = high
                rates[layer + 1, rows:, :] = low
            else:
                rates[layer + 1] = rate_refs[array][place]
        rates[0] = rates[layers]
        rates[layers + 1] = rates[1]

    first = pl.program_id(0) * step

    def averaged(index, at, field):
        total = None
        for number in range(3):
            high, low = split(rates[index + number, field])
            weights = mean_ref[at, number * BLOCK : (number + 1) * BLOCK, :]
            part = dot(high, weights) + dot(low, weights)
            total = part if total is None else total + part
        return total

    for at in range(step):
        index = first + at
        lanes = lanes_of(at)
        if aligned:
            near = jnp.concatenate([rates[index + number] for number in range(3)], axis=1)
            every = dot(near, mean_ref[at])
            every = every[:rows] + every[rows:]
            change = [every[f * local_modes : (f + 1) * local_modes] for f in range(fields)]
        else:
            change = [averaged(index, at, f) for f in range(fields)]
        shape = (local_modes, BLOCK)
        column = places(orient_ref, index, shape) & (RADIAL - 1)
        inner = column == 0
        on_wall = jnp.logical_or(inner, column == RADIAL - 1)
        mean_row = jnp.logical_and(lax.broadcasted_iota(jnp.int32, shape, 0) == 0, inner)
        driven = jnp.where(mean_row, wall_ref[0], 0.0)
        for field in range(fields):
            stepped = old_ref[field, :, lanes] + STEP_DT * change[field]
            if fields == 3:
                stepped = jnp.where(on_wall, driven if field == 1 else 0.0, stepped)
            out_ref[field, :, lanes] = stepped


def advance(rates, route, weights, old, me, orientation, wall):
    fields, local_modes, nodes = old.shape
    layers = nodes // BLOCK
    step = 16
    block = pl.BlockSpec((fields, local_modes, step * BLOCK), lambda i: (0, 0, i))
    scalar = pl.BlockSpec(memory_space=pltpu.SMEM)
    return pl.pallas_call(
        functools.partial(advance_body, layers, step, route, len(rates)),
        grid=(layers // step,),
        in_specs=[scalar] * 3
        + [pl.BlockSpec(part.shape, lambda i: (0, 0, 0, 0)) for part in rates]
        + [pl.BlockSpec((step, 3 * BLOCK, BLOCK), lambda i: (i, 0, 0)), block],
        out_specs=block,
        out_shape=jax.ShapeDtypeStruct(old.shape, F32),
        scratch_shapes=[
            pltpu.VMEM((layers + 2, 2 * fields * local_modes, BLOCK), BF16)
            if local_modes % 16 == 0
            else pltpu.VMEM((layers + 2, fields, local_modes, BLOCK), F32)
        ],
        compiler_params=pltpu.CompilerParams(vmem_limit_bytes=24 * MIB),
        name="advance",
    )(me, orientation, wall, *rates, weights, old)


def body(velocity, log_conf, orientation, wall_speed):
    devices = lax.axis_size("mode")
    device = lax.axis_index("mode").astype(jnp.int32)
    me = device.reshape(1)
    local_modes = velocity.shape[1]
    layers = velocity.shape[2] // BLOCK
    planes = local_modes * devices
    far_first = Route(devices, local_modes, True)
    near_first = Route(devices, local_modes, False)
    whole = Route(devices, local_modes, False, False)
    barrier = lax.optimization_barrier
    staged = far_first.staged
    both, faces, halos, means, inv_r_nodes = node_tables()

    def parts(tables):
        return jnp.asarray(np.stack([half for table in tables for half in split_table(table)]))

    fourier = fourier_tables(planes)
    high, low = (jnp.asarray(half) for half in split_table(fourier))
    signed = np.concatenate([fourier[:planes].T, -fourier[planes:].T], axis=1)
    back_high, back_low = (jnp.asarray(half) for half in split_table(signed))
    inv_r_table = jnp.asarray(np.tile(inv_r_nodes[:, None], (1, BLOCK)), F32)

    both_s, faces_s, halos_s, inv_r = kernel_call(
        order_body,
        (
            jax.ShapeDtypeStruct((10, BLOCK, BLOCK), BF16),
            jax.ShapeDtypeStruct((24, BLOCK, 2 * BLOCK), BF16),
            jax.ShapeDtypeStruct((10, 2 * BLOCK, 2 * BLOCK), BF16),
            jax.ShapeDtypeStruct((8, BLOCK), F32),
        ),
        4,
        scalars=2,
        vmem=16,
        name="order",
    )(me, orientation, parts(both), parts(faces), parts(halos), inv_r_table)
    weights = kernel_call(
        functools.partial(weights_body, layers),
        jax.ShapeDtypeStruct((layers, 3 * BLOCK, BLOCK), BF16),
        1,
        vmem=8 + layers // 8,
        name="weights",
    )(orientation, jnp.asarray(means, BF16))

    vel_nodes, psi_nodes = pack(me, (velocity, log_conf), (far_first, near_first))
    fixed = (both_s, faces_s, halos_s, inv_r, weights)
    if staged:
        psi_nodes = near_swaps(psi_nodes)
        vel_nodes = far_swaps(vel_nodes, psi_nodes)
        vel_nodes, psi_nodes, fixed = barrier((vel_nodes, psi_nodes, fixed))
        vel_nodes = near_swaps(regroup(vel_nodes))
        first_nodes = far_swaps(regroup([group[:, :FIRST] for group in psi_nodes]))
        second_nodes = regroup([group[:, FIRST:] for group in psi_nodes])
    else:
        vel_nodes = far_first.unpacked(in_one(vel_nodes))
        psi_nodes = near_first.unpacked(in_one(psi_nodes))
        first_nodes = [group[:, :FIRST] for group in psi_nodes]
        second_nodes = [group[:, FIRST:] for group in psi_nodes]

    both_s, faces_s, halos_s, inv_r, weights = fixed
    edge = jax.ShapeDtypeStruct((planes // 4 * 3, BLOCK), F32)
    vel_half = jax.ShapeDtypeStruct((planes, 3 * BLOCK), BF16)
    to_up, to_down, vel_h, vel_l = kernel_call(
        functools.partial(face_body, far_first, len(vel_nodes)),
        (edge, edge, vel_half, vel_half),
        len(vel_nodes) + 1,
        vmem=16,
        name="faces",
    )(me, *vel_nodes, faces_s)
    up = [(i, (i + 1) % devices) for i in range(devices)]
    below = lax.ppermute(to_up, "mode", up)
    above = lax.ppermute(to_down, "mode", [(j, i) for i, j in up])

    def halves(fields):
        return (
            jax.ShapeDtypeStruct((planes, fields * BLOCK), BF16),
            jax.ShapeDtypeStruct((planes, fields * BLOCK), BF16),
            jax.ShapeDtypeStruct((fields, planes, BLOCK), F32),
        )

    vel, own_flow, first_h, first_l, first = kernel_call(
        functools.partial(velocity_body, near_first, len(first_nodes)),
        (
            jax.ShapeDtypeStruct((3, planes, BLOCK), F32),
            jax.ShapeDtypeStruct((15, planes, BLOCK), F32),
            *halves(FIRST),
        ),
        len(first_nodes) + 6,
        scratch=[pltpu.VMEM((2 * planes, 3 * BLOCK), F32)],
        vmem=20,
        name="velocity",
    )(me, *first_nodes, vel_h, vel_l, high, low, both_s, inv_r)
    if staged:
        early = second_nodes
        second_nodes, below, above, vel = barrier((second_nodes, below, above, vel))
        second_nodes = far_swaps([early[0], second_nodes[1], early[2], early[3]])
    halo_flow = kernel_call(
        halo_body,
        jax.ShapeDtypeStruct((12, planes, BLOCK), F32),
        7,
        scalars=0,
        scratch=[pltpu.VMEM((2 * planes, 2 * BLOCK), F32)],
        vmem=24,
        name="halo",
    )(below, above, vel, high, low, halos_s, jnp.asarray(free_places(), BF16))

    far_outs = far_first.outs(far_first.leave, 3, far_first.modes, BLOCK)
    psi_outs = whole.outs(whole.leave, 6, whole.modes, BLOCK)
    field6 = jax.ShapeDtypeStruct((6, planes, BLOCK), F32)
    *vel_rates, second_h, second_l, second, conform = kernel_call(
        functools.partial(
            momentum_body, near_first, len(second_nodes), far_first, len(far_outs)
        ),
        (*far_outs, *halves(6 - FIRST), field6),
        len(second_nodes) + 9,
        scratch=[
            pltpu.VMEM((planes, 6 * BLOCK), BF16),
            pltpu.VMEM((planes, 6 * BLOCK), BF16),
            pltpu.VMEM((2 * planes, 3 * BLOCK), BF16),
            pltpu.VMEM((2 * planes, 3 * BLOCK), BF16),
            pltpu.VMEM((3, planes, BLOCK), F32),
            pltpu.VMEM((planes, 3 * BLOCK), F32),
        ],
        vmem=24,
        name="momentum",
    )(me, *second_nodes, first, own_flow, halo_flow, high, low, back_high, back_low, both_s, inv_r)
    vel_rates = far_first.packed(vel_rates)
    psi_rates = kernel_call(
        functools.partial(elastic_body, whole),
        (*psi_outs,),
        14,
        scratch=[
            pltpu.VMEM((6, planes, BLOCK), F32),
            pltpu.VMEM((6, planes, 2 * BLOCK), F32),
            pltpu.VMEM((planes, 6 * BLOCK), BF16),
            pltpu.VMEM((planes, 6 * BLOCK), BF16),
            pltpu.VMEM((planes, 6 * BLOCK), F32),
        ],
        vmem=24,
        name="elastic",
    )(
        me, first_h, first_l, second_h, second_l, first, second, conform, own_flow, halo_flow, high, low,
        back_high, back_low, both_s,
    )

    psi_rates = whole.packed(psi_rates)
    if staged:
        vel_rates, psi_rates = barrier((far_swaps(vel_rates), psi_rates))
        vel_rates = near_swaps(regroup(vel_rates))
    else:
        vel_rates = in_one(vel_rates)
    psi_rates = in_one(psi_rates)
    wall = jnp.where(device == 0, wall_speed, 0.0)
    at_walls = (me, orientation, wall)
    vel_next = advance(vel_rates, far_first, weights, velocity, *at_walls)
    logc_next = advance(psi_rates, whole, weights, log_conf, *at_walls)
    return vel_next, logc_next


def solution(mesh):
    in_specs = (P("ens", "mode", None), P("ens", "mode", None), P(), P("ens"))
    out_specs = (P("ens", "mode", None), P("ens", "mode", None))
    return jax.shard_map(body, mesh=mesh, in_specs=in_specs, out_specs=out_specs, check_vma=False)
```
